128 devices in a mesh: tm: 16 (over y, z_lo, core), space: 8 (over z_hi, x).
Axes of the slice: x: 4, y: 4, z: 4 (z_hi: 2, z_lo: 2; z = z_hi * 2 + z_lo), core: 2. Of those that a mesh axis runs over, the one named last changes fastest.
Arguments:
- tokens: bfloat16 [128, 256, 768], P('tm', 'space'), may hold values from -6 to 6
- x_weight: bfloat16 [768, 1536], replicated, may hold values from -0.21875 to 0.21875
- z_weight: bfloat16 [768, 1536], replicated, may hold values from -0.21875 to 0.21875
- bc_weight: bfloat16 [768, 256], replicated, may hold values from -0.21875 to 0.21875
- dt_weight: bfloat16 [768, 24], replicated, may hold values from -0.21875 to 0.21875
- conv_weight: float32 [2, 4, 1792], replicated, may hold values from -3 to 3
- conv_bias: float32 [2, 1792], replicated, may hold values from -1.8 to 1.8
- dt_bias: float32 [2, 24], replicated, may hold values from -4 to -1
- decay_rate: float32 [2, 24], replicated, may hold values from 1e-06 to 1
- skip_gain: float32 [2, 24], replicated, may hold values from 0.5 to 1.5
- norm_gain: float32 [1536], replicated, may hold values from 0.1 to 1.9
- out_weight: bfloat16 [1536, 768], replicated, may hold values from -0.15625 to 0.15625
Outputs:
- mixed: bfloat16 [128, 256, 768], P('tm', 'space')
The draws below stay inside these ranges and needn't reach their ends.
All inputs are finite; a program needn't handle non-finite values.
Results may differ from the reference program's by a relative error of at most 0.0044.
The reference program's roundings to bfloat16 on the way (of `xbc`, `forward_in`, `backward_in`, `weights`, `scaled` and `normed`) count: a program that leaves them out, or rounds other values in their place, can miss the bound.
Values may be sent and summed in bfloat16 or wider, within the bound.
A program may use at most 448 MiB of HBM per device.

```python
import math
import jax
import jax.numpy as jnp
from jax import lax

D = 768
HEADS = 24
HEADDIM = 64
STATE = 128
KERNEL = 4
PATCH = 256
INNER = 1536
FRAMES = 128


def levels(stream_key, extent, split, least, high):
    gain, own = 1.0, jax.random.fold_in(stream_key, 6)
    for axis_at, shards_of in split:
        heights = jnp.exp(jax.random.uniform(jax.random.fold_in(own, axis_at), (shards_of,), jnp.float32, least / len(split), high / len(split)))
        gain = gain * jnp.repeat(heights, extent[axis_at] // shards_of).reshape([-1 if axis == axis_at else 1 for axis in range(len(extent))])
    return gain


def normal_values(stream_key, dims, scale, limit, pieces=(), dtype=jnp.bfloat16):
    gain = levels(stream_key, dims, pieces, -0.22, 0.18) if pieces else 1.0
    entries = jax.random.normal(stream_key, dims, jnp.float32) * scale * gain
    return jnp.minimum(jnp.maximum(entries, -limit), limit).astype(dtype)


def setup_inputs(seed: int = 0) -> dict:
    key_of = jax.random.split(jax.random.key(seed), 13)
    return {
        "tokens": normal_values(key_of[0], (FRAMES, PATCH, D), 1.0, 6.0, ((0, 16), (1, 8))),
        "x_weight": normal_values(key_of[1], (D, INNER), D ** -0.5, 0.21875),
        "z_weight": normal_values(key_of[2], (D, INNER), D ** -0.5, 0.21875),
        "bc_weight": normal_values(key_of[3], (D, 2 * STATE), D ** -0.5, 0.21875),
        "dt_weight": normal_values(key_of[4], (D, HEADS), D ** -0.5, 0.21875),
        "conv_weight": normal_values(key_of[5], (2, KERNEL, INNER + 2 * STATE), 0.5, 3.0, (), jnp.float32),
        "conv_bias": normal_values(key_of[6], (2, INNER + 2 * STATE), 0.3, 1.8, (), jnp.float32),
        "dt_bias": jnp.clip(jax.random.uniform(key_of[7], (2, HEADS), jnp.float32, -4.0, -1.0), -4.0, -1.0),
        "decay_rate": jnp.clip(jnp.exp(jax.random.uniform(key_of[8], (2, HEADS), jnp.float32, math.log(9.999999974752427e-07), math.log(1.0))), 9.999999974752427e-07, 1.0),
        "skip_gain": jnp.clip(jax.random.uniform(key_of[9], (2, HEADS), jnp.float32, 0.5, 1.5), 0.5, 1.5),
        "norm_gain": jnp.clip(1.0 + 0.18 * jax.random.normal(key_of[10], (INNER,), jnp.float32), 0.1, 1.9),
        "out_weight": normal_values(key_of[11], (INNER, D), INNER ** -0.5, 0.15625),
    }


def causal_mix(padded, kernel_taps, kernel_bias):
    length = padded.shape[0] - KERNEL + 1
    running = kernel_bias[None, :]
    for offset in range(KERNEL):
        running = running + kernel_taps[offset][None, :] * padded[offset:offset + length].astype(jnp.float32)
    return jax.nn.silu(running).astype(jnp.bfloat16)

def span_intra(x_blocks, b_blocks, c_blocks, step_sizes, prefix):
    scores = jnp.einsum('qin,qjn->qij', c_blocks.astype(jnp.float32), b_blocks.astype(jnp.float32))
    prefix_heads = jnp.swapaxes(prefix, 1, 2)
    gaps = prefix_heads[:, :, :, None] - prefix_heads[:, :, None, :]
    block_len = prefix.shape[1]
    lower = lax.broadcasted_iota(jnp.int32, (block_len, block_len), 0) >= lax.broadcasted_iota(jnp.int32, (block_len, block_len), 1)
    decay = jnp.exp(jnp.where(lower, gaps, -jnp.inf))
    weights = (scores[:, None] * decay * jnp.swapaxes(step_sizes, 1, 2)[:, :, None, :]).astype(jnp.bfloat16)
    return jnp.einsum('qhij,qjhp->qihp', weights.astype(jnp.float32), x_blocks.astype(jnp.float32))

def span_states(x_blocks, b_blocks, step_sizes, prefix):
    to_end = jnp.exp(prefix[:, -1:, :] - prefix)
    scaled = (x_blocks.astype(jnp.float32) * (step_sizes * to_end)[..., None]).astype(jnp.bfloat16)
    return jnp.einsum('qlhp,qln->qhpn', scaled.astype(jnp.float32), b_blocks.astype(jnp.float32))

def span_inter(c_blocks, entering, prefix):
    rounded = entering.astype(jnp.bfloat16)
    produced = jnp.einsum('qln,qhpn->qlhp', c_blocks.astype(jnp.float32), rounded.astype(jnp.float32))
    return jnp.exp(prefix)[..., None] * produced

def one_direction(conv_out, dt_rows, bias_row, rate_row, skip_row):
    row_count = conv_out.shape[0]
    blocks = row_count // PATCH
    x_blocks = conv_out[:, :HEADS * HEADDIM].reshape(blocks, 1, PATCH, HEADS, HEADDIM)
    b_blocks = conv_out[:, HEADS * HEADDIM:HEADS * HEADDIM + STATE].reshape(blocks, 1, PATCH, STATE)
    c_blocks = conv_out[:, HEADS * HEADDIM + STATE:].reshape(blocks, 1, PATCH, STATE)
    step_sizes = jax.nn.softplus(dt_rows + bias_row[None, :]).reshape(blocks, 1, PATCH, HEADS)

    def advance(carried, inputs):
        x_block, b_block, c_block, step_block = inputs
        prefix = jnp.cumsum(-rate_row[None, None, :] * step_block, axis=1)
        intra = span_intra(x_block, b_block, c_block, step_block, prefix)
        inter = span_inter(c_block, carried[None], prefix)
        fresh = span_states(x_block, b_block, step_block, prefix)[0]
        updated = jnp.exp(prefix[0, -1, :])[:, None, None] * carried + fresh
        return (updated, intra + inter)
    initial = jnp.zeros((HEADS, HEADDIM, STATE), jnp.float32)
    _, produced = lax.scan(advance, initial, (x_blocks, b_blocks, c_blocks, step_sizes))
    produced = produced.reshape(row_count, HEADS, HEADDIM)
    x_rows = conv_out[:, :HEADS * HEADDIM].reshape(row_count, HEADS, HEADDIM).astype(jnp.float32)
    produced = produced + skip_row[None, :, None] * x_rows
    return produced.reshape(row_count, HEADS * HEADDIM)

def reference(tokens, x_weight, z_weight, bc_weight, dt_weight, conv_weight, conv_bias, dt_bias, decay_rate, skip_gain, norm_gain, out_weight):
    sequence = tokens.reshape(-1, D)
    in_weight = jnp.concatenate([x_weight, bc_weight], axis=1)
    xbc = jnp.dot(sequence, in_weight, preferred_element_type=jnp.float32).astype(jnp.bfloat16)
    gate_z = jnp.dot(sequence, z_weight, preferred_element_type=jnp.float32)
    dt_raw = jnp.dot(sequence, dt_weight, preferred_element_type=jnp.float32)
    zero_rows = jnp.zeros((KERNEL - 1, xbc.shape[1]), jnp.bfloat16)
    forward_in = causal_mix(jnp.concatenate([zero_rows, xbc], axis=0), conv_weight[0], conv_bias[0])
    backward_in = causal_mix(jnp.concatenate([zero_rows, xbc[::-1]], axis=0), conv_weight[1], conv_bias[1])
    y_forward = one_direction(forward_in, dt_raw, dt_bias[0], decay_rate[0], skip_gain[0])
    y_backward = one_direction(backward_in, dt_raw[::-1], dt_bias[1], decay_rate[1], skip_gain[1])[::-1]
    gated = (y_forward + y_backward) * jax.nn.silu(gate_z)
    scale = lax.rsqrt(lax.optimization_barrier(jnp.mean(gated * gated, axis=-1, keepdims=True)) + 1e-05)
    normed = (gated * scale * norm_gain[None, :]).astype(jnp.bfloat16)
    mixed = jnp.dot(normed, out_weight, preferred_element_type=jnp.float32).astype(jnp.bfloat16)
    return mixed.reshape(FRAMES, PATCH, D)
```

```python
import jax
import jax.numpy as jnp
from jax import lax
from jax.experimental import pallas as pl
from jax.experimental.pallas import tpu as pltpu
from jax.sharding import PartitionSpec as P

HEADS = 24
STATE = 128
PATCH = 256
D = 768
INNER = 1536
WIDE = INNER + 2 * STATE
HALF = INNER // 2
GROUP = 8
EDGE = 16
CHUNK = 256
LOG2E = 1.4426950408889634
F32, BF16 = jnp.float32, jnp.bfloat16
MESH = pl.DeviceIdType.MESH


def iota(shape, dim):
    return lax.broadcasted_iota(jnp.int32, shape, dim)


def split(a, parts):
    pieces = []
    for _ in range(parts):
        piece = a.astype(BF16)
        pieces.append(piece)
        a = a - piece.astype(F32)
    return jnp.concatenate(pieces, axis=1)


def dot(a, b):
    return jnp.dot(a, b, preferred_element_type=F32)


def silu(a):
    half = 0.5 * a
    return half + half * jnp.tanh(half)


def spread(parts, width, target):
    rows = iota((parts * 128, width), 0) & 127
    return (rows == target(iota((parts * 128, width), 1))).astype(F32).astype(BF16)


def pad_lanes(first, second):
    rows = first.shape[0]
    return jnp.concatenate([first, second, jnp.zeros((rows, 128 - 2 * HEADS), F32)], axis=1)


def kernel(
    tokens,
    x_weight,
    z_weight,
    bc_weight,
    dt_weight,
    conv_weight,
    conv_bias,
    dt_bias,
    decay_rate,
    skip_gain,
    norm_gain,
    out_weight,
    out,
    w_in,
    w_z,
    w_out,
    tok,
    xbc,
    conv_f,
    conv_b,
    b_turned,
    gate,
    y,
    scores,
    columns,
    q_rows,
    fac,
    ep,
    skip_rows,
    st,
    part_out,
    part_in,
    local,
    coef,
    coef_t,
    slab_out,
    slab_in,
    ent_out,
    ent_in,
    ent,
    log_mine,
    log_in,
    log_slab,
    log_slabs,
    mix,
    w_sem,
    tok_sem,
    tok_send,
    edge_send,
    log_send,
    log_recv,
    logt_send,
    logt_recv,
    pair_send,
    pair_recv,
    part_send,
    part_recv,
    slab_send,
    slab_recv,
    ent_send,
    ent_recv,
    epair_send,
    epair_recv,
    out_send,
    out_sem,
):
    tm = lax.axis_index("tm")
    s = lax.axis_index("space")
    slab = tm // 2
    c = tm % 2
    u = 2 * s + c
    corner_hi = jnp.logical_and(s == GROUP - 1, c == 1)
    corner_lo = jnp.logical_and(s == 0, c == 0)

    loads = [
        pltpu.make_async_copy(bc_weight, w_in.at[:, pl.ds(INNER, 2 * STATE)], w_sem.at[0]),
        pltpu.make_async_copy(x_weight, w_in.at[:, pl.ds(0, INNER)], w_sem.at[1]),
        pltpu.make_async_copy(z_weight, w_z, w_sem.at[2]),
        pltpu.make_async_copy(out_weight, w_out, w_sem.at[3]),
    ]
    for load in loads:
        load.start()

    barrier = pltpu.get_barrier_semaphore()

    def greet(d, _):
        v = lax.rem(u + d, 16)
        pl.semaphore_signal(barrier, inc=1, device_id=(2 * slab + v % 2, v // 2), device_id_type=MESH)
        return 0

    lax.fori_loop(1, 16, greet, 0)

    def greet_slab(d, _):
        t = lax.rem(slab + d, GROUP)
        pl.semaphore_signal(barrier, inc=1, device_id=(2 * t + c, s), device_id_type=MESH)
        return 0

    lax.fori_loop(1, GROUP, greet_slab, 0)
    above = lax.rem(slab + 1, GROUP)
    below = lax.rem(slab + GROUP - 1, GROUP)

    @pl.when(corner_hi)
    def _():
        pl.semaphore_signal(barrier, inc=1, device_id=(2 * above, 0), device_id_type=MESH)

    @pl.when(corner_lo)
    def _():
        pl.semaphore_signal(
            barrier, inc=1, device_id=(2 * below + 1, GROUP - 1), device_id_type=MESH
        )

    pl.semaphore_wait(barrier, 22 + jnp.logical_or(corner_hi, corner_lo).astype(jnp.int32))

    def send_tokens(j, action):
        ds, dc = 4 * c + j // 2, j % 2
        mine = jnp.logical_and(ds == s, dc == c)
        src, dst = tokens.at[j], tok.at[pl.ds(pl.multiple_of(EDGE + 32 * s, 16), 32)]

        @pl.when(jnp.logical_not(mine))
        def _():
            action(
                pltpu.make_async_remote_copy(
                    src, dst, tok_send.at[j], tok_sem, (2 * slab + dc, ds), MESH
                )
            )

        if action is started:

            @pl.when(mine)
            def _():
                pltpu.make_async_copy(src, dst, tok_sem).start()

    def send_edge(j, action, side):
        g = 8 * c + j + (1 if side == 0 else -1)
        ds, dc = lax.rem(g + 16, 16) // 2, lax.rem(g + 16, 16) % 2
        dt = lax.rem(slab + lax.div(g + 16, 16) - 1 + GROUP, GROUP)
        mine = jnp.logical_and(jnp.logical_and(ds == s, dc == c), dt == slab)
        src = tokens.at[j, pl.ds(16 if side == 0 else 0, EDGE)]
        dst = tok.at[pl.ds(0 if side == 0 else EDGE + PATCH, EDGE)]

        @pl.when(jnp.logical_not(mine))
        def _():
            action(
                pltpu.make_async_remote_copy(
                    src, dst, edge_send.at[side, j], tok_sem, (2 * dt + dc, ds), MESH
                )
            )

        if action is started:

            @pl.when(mine)
            def _():
                pltpu.make_async_copy(src, dst, tok_sem).start()

    def started(copy):
        copy.start()

    def left(copy):
        copy.wait_send()

    def all_tokens(action):
        def one(j, _):
            send_tokens(j, action)
            return 0

        lax.fori_loop(0, 8, one, 0)

        @pl.when(s == GROUP - 1)
        def _():
            def one(j, _):
                send_edge(j, action, 0)
                return 0

            lax.fori_loop(0, 8, one, 0)

        @pl.when(s == 0)
        def _():
            def one(j, _):
                send_edge(j, action, 1)
                return 0

            lax.fori_loop(0, 8, one, 0)

    all_tokens(started)

    skips = pad_lanes(skip_gain[0:1, :], skip_gain[1:2, :])
    for e in range(2):
        skip_rows[e : e + 1, :] = dot(
            split(jnp.broadcast_to(skips, (8, 128)), 3),
            spread(3, INNER, lambda l: HEADS * e + (l >> 6)),
        )[0:1, :]

    pltpu.make_async_copy(tok, tok, tok_sem).wait()

    @pl.when(jnp.logical_and(corner_lo, slab == 0))
    def _():
        tok[0:EDGE, :] = jnp.zeros((EDGE, D), BF16)

    @pl.when(jnp.logical_and(corner_hi, slab == GROUP - 1))
    def _():
        tok[EDGE + PATCH :, :] = jnp.zeros((EDGE, D), BF16)

    dt_raw = dot(tok[EDGE : EDGE + PATCH, :], dt_weight[...])
    step = jax.nn.softplus(
        pad_lanes(dt_raw, dt_raw) + pad_lanes(dt_bias[0:1, :], dt_bias[1:2, :])
    )
    rates = pad_lanes(decay_rate[0:1, :], decay_rate[1:2, :])
    rate_step = split(step * (rates * -LOG2E), 3)
    row, col = iota((PATCH, PATCH), 0), iota((PATCH, PATCH), 1)
    down = dot((row >= col).astype(F32).astype(BF16), rate_step)
    up = dot((row <= col).astype(F32).astype(BF16), rate_step)
    down = down[:, 0:128] + (down[:, 128:256] + down[:, 256:384])
    up = up[:, 0:128] + (up[:, 128:256] + up[:, 256:384])
    lane = iota((PATCH, 128), 1)
    prefix = jnp.where(lane < HEADS, down, up)
    total = jnp.where(lane[0:1] < HEADS, down[PATCH - 1 :, :], up[0:1, :])
    log_mine[...] = jnp.broadcast_to(total, (8, 128))
    log_in[u] = log_mine[...]

    def send_logs(d, _):
        v = lax.rem(u + d, 16)
        pltpu.make_async_remote_copy(
            log_mine,
            log_in.at[u],
            log_send.at[v],
            log_recv.at[u],
            (2 * slab + v % 2, v // 2),
            MESH,
        ).start()
        return 0

    lax.fori_loop(1, 16, send_logs, 0)

    columns[...] = split(prefix, 3)
    fac[...] = split(jnp.exp2(total - prefix) * step, 2)
    ep[...] = split(jnp.exp2(prefix), 2)
    q_rows[...] = (prefix - LOG2E * jnp.log(step)).T

    def convolved(offset):
        span = pl.ds(offset, CHUNK)
        xbc[...] = dot(tok[...], w_in[:, span]).astype(BF16).astype(F32)
        forward = conv_bias[0:1, span]
        backward = conv_bias[1:2, span]
        for k in range(4):
            forward = forward + conv_weight[0, k : k + 1, span] * xbc[pl.ds(EDGE - 3 + k, PATCH), :]
            backward = (
                backward + conv_weight[1, k : k + 1, span] * xbc[pl.ds(EDGE + 3 - k, PATCH), :]
            )
        forward, backward = silu(forward).astype(BF16), silu(backward).astype(BF16)
        conv_f[:, span] = forward
        conv_b[:, span] = backward
        return forward, backward

    loads[0].wait()
    both = convolved(INNER)
    for e in range(2):
        b_turned[e] = both[e][:, 0:STATE].astype(F32).T.astype(BF16)
    loads[1].wait()

    def pair_copy():
        return pltpu.make_async_remote_copy(
            st.at[2], st.at[c], pair_send, pair_recv, (2 * slab + 1 - c, s), MESH
        )

    def head_target(t):
        return lambda l: (l >> 6) + jnp.where(l < CHUNK, 4 * t, HEADS - 4 + 4 * t)

    def project(i, _):
        t = lax.rem((1 - c) * 3 + i, 6)
        x_f, x_b = convolved(pl.multiple_of(t * CHUNK, CHUNK))
        factor = dot(fac[...], spread(2, 2 * CHUNK, head_target(t)))
        slot = jnp.where(t // 3 == c, c, 2)
        place = pl.ds(pl.multiple_of((t % 3) * CHUNK, CHUNK), CHUNK)
        for e, x in ((0, x_f), (1, x_b)):
            scaled = (x.astype(F32) * factor[:, e * CHUNK : (e + 1) * CHUNK]).astype(BF16)
            st[slot, e, :, place] = dot(b_turned[e], scaled)

        @pl.when(i == 2)
        def _():
            pair_copy().start()

        return 0

    lax.fori_loop(0, 6, project, 0)

    def wait_logs(d, _):
        v = lax.rem(u + d, 16)
        pltpu.make_async_remote_copy(
            log_mine, log_in.at[v], log_send.at[v], log_recv.at[v], (tm, s), MESH
        ).wait_recv()
        return 0

    lax.fori_loop(1, 16, wait_logs, 0)
    chips = [log_in[2 * k][0:1, :] + log_in[2 * k + 1][0:1, :] for k in range(GROUP)]
    zero = jnp.zeros((1, 128), F32)
    before, after = [zero], [zero]
    for k in range(GROUP):
        before.append(before[-1] + chips[k])
        after.append(after[-1] + chips[GROUP - 1 - k])
    narrow = iota((1, 128), 1) < HEADS
    outside = [jnp.where(narrow, before[k], after[GROUP - 1 - k]) for k in range(GROUP)]
    log_slab[...] = jnp.broadcast_to(before[GROUP], (8, 128))
    log_slabs[slab] = log_slab[...]

    def slab_log_copy(t, source):
        return pltpu.make_async_remote_copy(
            log_slab, log_slabs.at[source], logt_send.at[t], logt_recv.at[source], (2 * t + c, s), MESH
        )

    def send_slab_logs(d, _):
        slab_log_copy(lax.rem(slab + d, GROUP), slab).start()
        return 0

    lax.fori_loop(1, GROUP, send_slab_logs, 0)

    half_target = lambda l: (l >> 6) + jnp.where(l < HALF, 12 * c, HEADS - 12 + 12 * c)
    table = jnp.concatenate(
        chips
        + outside
        + [log_in[2 * s][0:1, :], log_in[2 * s + 1][0:1, :]]
        + [jnp.zeros((6, 128), F32)],
        axis=0,
    )
    expand = spread(3, INNER, half_target)
    coef[...] = dot(split(jnp.exp2(table), 3), expand)

    pair_copy().wait_recv()
    d0, d1 = coef[16:17, :], coef[17:18, :]

    def part_copy(k, source):
        return pltpu.make_async_remote_copy(
            part_out.at[k],
            part_in.at[source],
            part_send.at[k],
            part_recv.at[source],
            (tm, k),
            MESH,
        )

    def combined(k):
        rows = pl.ds(pl.multiple_of(k * 16, 16), 16)
        return jnp.concatenate(
            [
                d1[:, :HALF] * st[0, 0, rows, :] + st[1, 0, rows, :],
                d0[:, HALF:] * st[1, 1, rows, :] + st[0, 1, rows, :],
            ],
            axis=1,
        ).astype(BF16)

    def send_part(d, _):
        k = lax.rem(s + d, GROUP)
        part_out[k] = combined(k)
        part_copy(k, s).start()
        return 0

    lax.fori_loop(1, GROUP, send_part, 0)
    part_in[s] = combined(s)

    for e, conv in ((0, conv_f), (1, conv_b)):
        scores[e] = lax.dot_general(
            conv[:, INNER + STATE :],
            conv[:, INNER : INNER + STATE],
            (((1,), (1,)), ((), ())),
            preferred_element_type=F32,
        )
    lower = iota((128, 128), 0) >= iota((128, 128), 1)
    upper = iota((128, 128), 0) <= iota((128, 128), 1)
    near = [
        (iota((1, 128), 1) < 64).astype(F32).astype(BF16),
        (iota((1, 128), 1) >= 64).astype(F32).astype(BF16),
    ]

    def weigh(e, i, j, column, line, mask):
        gap = column[128 * i : 128 * i + 128, :] - line[:, 128 * j : 128 * j + 128]
        if mask is not None:
            gap = jnp.where(mask, gap, -jnp.inf)
        return (
            scores[e, 128 * i : 128 * i + 128, 128 * j : 128 * j + 128] * jnp.exp2(gap)
        ).astype(BF16)

    def within(t, _):
        span = pl.ds(pl.multiple_of(t * 128, 128), 128)
        x_f, x_b = conv_f[:, span], conv_b[:, span]
        wide = dot(
            columns[...],
            spread(3, 512, lambda l: 2 * t + ((l >> 7) & 1) + jnp.where(l < 256, 0, HEADS)),
        )
        tops, bottoms, top_x, bottom_x = [], [], [], []
        for h in range(2):
            pf, pb = wide[:, 128 * h : 128 * h + 128], wide[:, 256 + 128 * h : 384 + 128 * h]
            qf, qb = q_rows[pl.ds(2 * t + h, 1), :], q_rows[pl.ds(HEADS + 2 * t + h, 1), :]
            tops += [
                weigh(0, 0, 0, pf, qf, lower),
                weigh(1, 0, 0, pb, qb, upper),
                weigh(1, 0, 1, pb, qb, None),
            ]
            bottoms += [
                weigh(0, 1, 0, pf, qf, None),
                weigh(0, 1, 1, pf, qf, lower),
                weigh(1, 1, 1, pb, qb, upper),
            ]
            xf, xb = x_f * near[h], x_b * near[h]
            top_x += [xf[0:128], xb]
            bottom_x += [xf, xb[128:256]]
        y[0:128, span] = dot(jnp.concatenate(tops, axis=1), jnp.concatenate(top_x, axis=0))
        y[128:256, span] = dot(jnp.concatenate(bottoms, axis=1), jnp.concatenate(bottom_x, axis=0))
        return 0

    def gate_columns(t, _):
        span = pl.ds(pl.multiple_of(t * CHUNK, CHUNK), CHUNK)
        gate[:, span] = silu(dot(tok[EDGE : EDGE + PATCH, :], w_z[:, span]))
        return 0

    loads[2].wait()
    lax.fori_loop(0, 6, gate_columns, 0)
    lax.fori_loop(0, 3, within, 0)

    def wait_part(d, _):
        k = lax.rem(s + d, GROUP)
        part_copy(k, k).wait_recv()
        return 0

    lax.fori_loop(1, GROUP, wait_part, 0)
    forward = jnp.zeros((16, HALF), F32)
    backward = jnp.zeros((16, HALF), F32)
    for k in range(GROUP):
        r = GROUP - 1 - k
        local[k, :, :HALF] = forward
        local[r, :, HALF:] = backward
        forward = coef[k : k + 1, :HALF] * forward + part_in[k, :, :HALF].astype(F32)
        backward = coef[r : r + 1, HALF:] * backward + part_in[r, :, HALF:].astype(F32)
    slab_out[...] = jnp.concatenate([forward, backward], axis=1).astype(BF16)

    def slab_copy(t, source):
        return pltpu.make_async_remote_copy(
            slab_out, slab_in.at[source], slab_send.at[t], slab_recv.at[source], (2 * t + c, s), MESH
        )

    def send_slab(d, _):
        slab_copy(lax.rem(slab + d, GROUP), slab).start()
        return 0

    lax.fori_loop(1, GROUP, send_slab, 0)
    slab_in[slab] = slab_out[...]

    lax.fori_loop(3, 8, within, 0)

    def wait_slab(d, _):
        t = lax.rem(slab + d, GROUP)
        slab_log_copy(t, t).wait_recv()
        slab_copy(t, t).wait_recv()
        return 0

    lax.fori_loop(1, GROUP, wait_slab, 0)
    table = jnp.concatenate([log_slabs[t][0:1, :] for t in range(GROUP)], axis=0)
    coef_t[...] = dot(split(jnp.exp2(table), 3), spread(3, INNER, half_target))
    forward = jnp.zeros((16, HALF), F32)
    backward = jnp.zeros((16, HALF), F32)
    for k in range(GROUP):
        r = GROUP - 1 - k
        forward = jnp.where(
            k < slab, coef_t[k : k + 1, :HALF] * forward + slab_in[k, :, :HALF].astype(F32), forward
        )
        backward = jnp.where(
            r > slab, coef_t[r : r + 1, HALF:] * backward + slab_in[r, :, HALF:].astype(F32), backward
        )
    come = jnp.concatenate([forward, backward], axis=1)

    def ent_copy(k, source):
        return pltpu.make_async_remote_copy(
            ent_out.at[k], ent_in.at[source], ent_send.at[k], ent_recv.at[source], (tm, k), MESH
        )

    def entering(k):
        return (local[k] + coef[pl.ds(GROUP + k, 1), :] * come).astype(BF16)

    def send_ent(d, _):
        k = lax.rem(s + d, GROUP)
        ent_out[k] = entering(k)
        ent_copy(k, s).start()
        return 0

    lax.fori_loop(1, GROUP, send_ent, 0)
    ent_in[s] = entering(s)

    lax.fori_loop(8, 12, within, 0)

    def wait_ent(d, _):
        k = lax.rem(s + d, GROUP)
        ent_copy(k, k).wait_recv()
        return 0

    lax.fori_loop(1, GROUP, wait_ent, 0)
    for k in range(GROUP):
        rows = slice(16 * k, 16 * k + 16)
        first, last = ent_in[k, :, :HALF], ent_in[k, :, HALF:]
        ent[0, 0, rows, :] = first
        ent[1, 1, rows, :] = last
        ent[1, 0, rows, :] = (d0[:, :HALF] * first.astype(F32) + st[0, 0, rows, :]).astype(BF16)
        ent[0, 1, rows, :] = (d1[:, HALF:] * last.astype(F32) + st[1, 1, rows, :]).astype(BF16)
    ent_pair = pltpu.make_async_remote_copy(
        ent.at[1 - c], ent.at[2], epair_send, epair_recv, (2 * slab + 1 - c, s), MESH
    )
    ent_pair.start()

    def finish(i, squares):
        t = lax.rem(c * 3 + i, 6)

        @pl.when(i == 3)
        def _():
            ent_pair.wait_recv()

        span = pl.ds(pl.multiple_of(t * CHUNK, CHUNK), CHUNK)
        slot = jnp.where(t // 3 == c, c, 2)
        place = pl.ds(pl.multiple_of((t % 3) * CHUNK, CHUNK), CHUNK)
        grow = dot(ep[...], spread(2, 2 * CHUNK, head_target(t)))
        total = y[:, span]
        for e, conv in ((0, conv_f), (1, conv_b)):
            total = total + grow[:, e * CHUNK : (e + 1) * CHUNK] * dot(
                conv[:, INNER + STATE :], ent[slot, e, :, place]
            )
            total = total + skip_rows[e : e + 1, span] * conv[:, span].astype(F32)
        gated = total * gate[:, span]
        y[:, span] = gated
        return squares + jnp.sum(gated * gated, axis=1, keepdims=True)

    squares = lax.fori_loop(0, 6, finish, jnp.zeros((PATCH, 1), F32))
    scale = lax.rsqrt(squares * (1.0 / INNER) + 1e-05)
    gains = norm_gain[...].reshape(1, INNER)
    loads[3].wait()

    core_home = s // 4
    slot_home = u - 8 * core_home

    def send_out(b, action):
        mine = jnp.logical_and(b == s, core_home == c)
        src, dst = mix.at[pl.ds(pl.multiple_of(32 * b, 32), 32)], out.at[slot_home]

        @pl.when(jnp.logical_not(mine))
        def _():
            action(
                pltpu.make_async_remote_copy(
                    src, dst, out_send.at[b], out_sem, (2 * slab + core_home, b), MESH
                )
            )

        if action is started:

            @pl.when(mine)
            def _():
                pltpu.make_async_copy(src, dst, out_sem).start()

    for half in range(2):
        rows = slice(128 * half, 128 * half + 128)
        normed = (y[rows, :] * scale[rows, :] * gains).astype(BF16)
        mix[rows, :] = dot(normed, w_out[...]).astype(BF16)
        for b in range(4 * half, 4 * half + 4):
            send_out(b, started)

    all_tokens(left)
    pair_copy().wait_send()
    ent_pair.wait_send()

    def wait_sent(d, _):
        v = lax.rem(u + d, 16)
        pltpu.make_async_remote_copy(
            log_mine, log_in.at[u], log_send.at[v], log_recv.at[u], (tm, s), MESH
        ).wait_send()
        return 0

    lax.fori_loop(1, 16, wait_sent, 0)

    def wait_sent_group(d, _):
        k = lax.rem(s + d, GROUP)
        part_copy(k, s).wait_send()
        ent_copy(k, s).wait_send()
        t = lax.rem(slab + d, GROUP)
        slab_log_copy(t, slab).wait_send()
        slab_copy(t, slab).wait_send()
        return 0

    lax.fori_loop(1, GROUP, wait_sent_group, 0)
    for b in range(8):
        send_out(b, left)
    pltpu.make_async_copy(out, out, out_sem).wait()


def body(*args):
    hbm = pl.BlockSpec(memory_space=pl.ANY)
    vmem = pl.BlockSpec(memory_space=pltpu.VMEM)
    dma = pltpu.SemaphoreType.DMA
    scratch = [
        pltpu.VMEM((D, WIDE), BF16),
        pltpu.VMEM((D, INNER), BF16),
        pltpu.VMEM((INNER, D), BF16),
        pltpu.VMEM((PATCH + 2 * EDGE, D), BF16),
        pltpu.VMEM((PATCH + 2 * EDGE, CHUNK), F32),
        pltpu.VMEM((PATCH, WIDE), BF16),
        pltpu.VMEM((PATCH, WIDE), BF16),
        pltpu.VMEM((2, STATE, PATCH), BF16),
        pltpu.VMEM((PATCH, INNER), F32),
        pltpu.VMEM((PATCH, INNER), F32),
        pltpu.VMEM((2, PATCH, PATCH), F32),
        pltpu.VMEM((PATCH, 384), BF16),
        pltpu.VMEM((128, PATCH), F32),
        pltpu.VMEM((PATCH, 256), BF16),
        pltpu.VMEM((PATCH, 256), BF16),
        pltpu.VMEM((8, INNER), F32),
        pltpu.VMEM((3, 2, STATE, HALF), F32),
        pltpu.VMEM((GROUP, 16, INNER), BF16),
        pltpu.VMEM((GROUP, 16, INNER), BF16),
        pltpu.VMEM((GROUP, 16, INNER), F32),
        pltpu.VMEM((24, INNER), F32),
        pltpu.VMEM((GROUP, INNER), F32),
        pltpu.VMEM((16, INNER), BF16),
        pltpu.VMEM((GROUP, 16, INNER), BF16),
        pltpu.VMEM((GROUP, 16, INNER), BF16),
        pltpu.VMEM((GROUP, 16, INNER), BF16),
        pltpu.VMEM((3, 2, STATE, HALF), BF16),
        pltpu.VMEM((8, 128), F32),
        pltpu.VMEM((16, 8, 128), F32),
        pltpu.VMEM((8, 128), F32),
        pltpu.VMEM((GROUP, 8, 128), F32),
        pltpu.VMEM((PATCH, D), BF16),
        dma((4,)),
        dma,
        dma((8,)),
        dma((2, 8)),
        dma((16,)),
        dma((16,)),
        dma((GROUP,)),
        dma((GROUP,)),
        dma,
        dma,
        dma((GROUP,)),
        dma((GROUP,)),
        dma((GROUP,)),
        dma((GROUP,)),
        dma((GROUP,)),
        dma((GROUP,)),
        dma,
        dma,
        dma((8,)),
        dma,
    ]
    return pl.pallas_call(
        kernel,
        out_shape=jax.ShapeDtypeStruct((8, 32, D), BF16),
        in_specs=[hbm] * 4 + [vmem] * 7 + [hbm],
        out_specs=hbm,
        scratch_shapes=scratch,
        compiler_params=pltpu.CompilerParams(
            collective_id=0, has_side_effects=True, vmem_limit_bytes=48 * 1024 * 1024
        ),
    )(*args)


def solution(mesh):
    return jax.shard_map(
        body,
        mesh=mesh,
        in_specs=(P("tm", "space", None),) + (P(),) * 11,
        out_specs=P("tm", "space", None),
        check_vma=False,
    )
```

```python
import jax
import jax.numpy as jnp
from jax import lax
from jax.experimental import pallas as pl
from jax.experimental.pallas import tpu as pltpu
from jax.sharding import PartitionSpec as P

HEADS = 24
STATE = 128
PATCH = 256
D = 768
INNER = 1536
WIDE = INNER + 2 * STATE
HALF = INNER // 2
GROUP = 8
EDGE = 16
CHUNK = 256
LOG2E = 1.4426950408889634
F32, BF16 = jnp.float32, jnp.bfloat16
MESH = pl.DeviceIdType.MESH


def iota(shape, dim):
    return lax.broadcasted_iota(jnp.int32, shape, dim)


def split(a, parts):
    pieces = []
    for _ in range(parts):
        piece = a.astype(BF16)
        pieces.append(piece)
        a = a - piece.astype(F32)
    return jnp.concatenate(pieces, axis=1)


def dot(a, b):
    return jnp.dot(a, b, preferred_element_type=F32)


def silu(a):
    half = 0.5 * a
    return half + half * jnp.tanh(half)


def spread(parts, width, target):
    rows = iota((parts * 128, width), 0) & 127
    return (rows == target(iota((parts * 128, width), 1))).astype(F32).astype(BF16)


def pad_lanes(first, second):
    rows = first.shape[0]
    return jnp.concatenate([first, second, jnp.zeros((rows, 128 - 2 * HEADS), F32)], axis=1)


def kernel(
    tokens,
    x_weight,
    z_weight,
    bc_weight,
    dt_weight_hbm,
    conv_weight_hbm,
    conv_bias_hbm,
    dt_bias_hbm,
    decay_rate_hbm,
    skip_gain_hbm,
    norm_gain_hbm,
    out_weight,
    out,
    dt_weight,
    conv_weight,
    conv_bias,
    dt_bias,
    decay_rate,
    skip_gain,
    norm_gain,
    w_in,
    w_z,
    w_out,
    tok,
    xbc,
    conv_f,
    conv_b,
    b_turned,
    gate,
    y,
    scores,
    columns,
    q_rows,
    fac,
    ep,
    skip_rows,
    st,
    part_out,
    part_in,
    local,
    coef,
    coef_t,
    slab_out,
    slab_in,
    ent_out,
    ent_in,
    ent,
    log_mine,
    log_in,
    log_slab,
    log_slabs,
    mix,
    w_sem,
    tok_sem,
    tok_send,
    edge_send,
    log_send,
    log_recv,
    logt_send,
    logt_recv,
    pair_send,
    pair_recv,
    part_send,
    part_recv,
    slab_send,
    slab_recv,
    ent_send,
    ent_recv,
    epair_send,
    epair_recv,
    out_send,
    out_sem,
):
    tm = lax.axis_index("tm")
    s = lax.axis_index("space")
    slab = tm // 2
    c = tm % 2
    u = 2 * s + c
    corner_hi = jnp.logical_and(s == GROUP - 1, c == 1)
    corner_lo = jnp.logical_and(s == 0, c == 0)

    loads = [
        pltpu.make_async_copy(bc_weight, w_in.at[:, pl.ds(INNER, 2 * STATE)], w_sem.at[0]),
        pltpu.make_async_copy(x_weight, w_in.at[:, pl.ds(0, INNER)], w_sem.at[1]),
        pltpu.make_async_copy(z_weight, w_z, w_sem.at[2]),
        pltpu.make_async_copy(out_weight, w_out, w_sem.at[3]),
    ]
    small = [
        pltpu.make_async_copy(source, target, w_sem.at[4 + at])
        for at, (source, target) in enumerate(
            (
                (skip_gain_hbm, skip_gain),
                (dt_weight_hbm, dt_weight),
                (dt_bias_hbm, dt_bias),
                (decay_rate_hbm, decay_rate),
                (conv_weight_hbm, conv_weight),
                (conv_bias_hbm, conv_bias),
                (norm_gain_hbm, norm_gain),
            )
        )
    ]
    for load in small + loads:
        load.start()

    barrier = pltpu.get_barrier_semaphore()

    def greet(d, _):
        v = lax.rem(u + d, 16)
        pl.semaphore_signal(barrier, inc=1, device_id=(2 * slab + v % 2, v // 2), device_id_type=MESH)
        return 0

    lax.fori_loop(1, 16, greet, 0)

    def greet_slab(d, _):
        t = lax.rem(slab + d, GROUP)
        pl.semaphore_signal(barrier, inc=1, device_id=(2 * t + c, s), device_id_type=MESH)
        return 0

    lax.fori_loop(1, GROUP, greet_slab, 0)
    above = lax.rem(slab + 1, GROUP)
    below = lax.rem(slab + GROUP - 1, GROUP)

    @pl.when(corner_hi)
    def _():
        pl.semaphore_signal(barrier, inc=1, device_id=(2 * above, 0), device_id_type=MESH)

    @pl.when(corner_lo)
    def _():
        pl.semaphore_signal(
            barrier, inc=1, device_id=(2 * below + 1, GROUP - 1), device_id_type=MESH
        )

    pl.semaphore_wait(barrier, 22 + jnp.logical_or(corner_hi, corner_lo).astype(jnp.int32))

    def send_tokens(j, action):
        ds, dc = 4 * c + j // 2, j % 2
        mine = jnp.logical_and(ds == s, dc == c)
        src, dst = tokens.at[j], tok.at[pl.ds(pl.multiple_of(EDGE + 32 * s, 16), 32)]

        @pl.when(jnp.logical_not(mine))
        def _():
            action(
                pltpu.make_async_remote_copy(
                    src, dst, tok_send.at[j], tok_sem, (2 * slab + dc, ds), MESH
                )
            )

        if action is started:

            @pl.when(mine)
            def _():
                pltpu.make_async_copy(src, dst, tok_sem).start()

    def send_edge(j, action, side):
        g = 8 * c + j + (1 if side == 0 else -1)
        ds, dc = lax.rem(g + 16, 16) // 2, lax.rem(g + 16, 16) % 2
        dt = lax.rem(slab + lax.div(g + 16, 16) - 1 + GROUP, GROUP)
        mine = jnp.logical_and(jnp.logical_and(ds == s, dc == c), dt == slab)
        src = tokens.at[j, pl.ds(16 if side == 0 else 0, EDGE)]
        dst = tok.at[pl.ds(0 if side == 0 else EDGE + PATCH, EDGE)]

        @pl.when(jnp.logical_not(mine))
        def _():
            action(
                pltpu.make_async_remote_copy(
                    src, dst, edge_send.at[side, j], tok_sem, (2 * dt + dc, ds), MESH
                )
            )

        if action is started:

            @pl.when(mine)
            def _():
                pltpu.make_async_copy(src, dst, tok_sem).start()

    def started(copy):
        copy.start()

    def left(copy):
        copy.wait_send()

    def all_tokens(action):
        def one(j, _):
            send_tokens(j, action)
            return 0

        lax.fori_loop(0, 8, one, 0)

        @pl.when(s == GROUP - 1)
        def _():
            def one(j, _):
                send_edge(j, action, 0)
                return 0

            lax.fori_loop(0, 8, one, 0)

        @pl.when(s == 0)
        def _():
            def one(j, _):
                send_edge(j, action, 1)
                return 0

            lax.fori_loop(0, 8, one, 0)

    all_tokens(started)

    for load in small:
        load.wait()
    skips = pad_lanes(skip_gain[0:1, :], skip_gain[1:2, :])
    for e in range(2):
        skip_rows[e : e + 1, :] = dot(
            split(jnp.broadcast_to(skips, (8, 128)), 3),
            spread(3, INNER, lambda l: HEADS * e + (l >> 6)),
        )[0:1, :]

    pltpu.make_async_copy(tok, tok, tok_sem).wait()

    @pl.when(jnp.logical_and(corner_lo, slab == 0))
    def _():
        tok[0:EDGE, :] = jnp.zeros((EDGE, D), BF16)

    @pl.when(jnp.logical_and(corner_hi, slab == GROUP - 1))
    def _():
        tok[EDGE + PATCH :, :] = jnp.zeros((EDGE, D), BF16)

    dt_raw = lax.dot_general(
        tok[EDGE : EDGE + PATCH, :],
        dt_weight[...],
        (((1,), (1,)), ((), ())),
        preferred_element_type=F32,
    )
    step = jax.nn.softplus(
        pad_lanes(dt_raw, dt_raw) + pad_lanes(dt_bias[0:1, :], dt_bias[1:2, :])
    )
    rates = pad_lanes(decay_rate[0:1, :], decay_rate[1:2, :])
    rate_step = split(step * (rates * -LOG2E), 3)
    row, col = iota((PATCH, PATCH), 0), iota((PATCH, PATCH), 1)
    down = dot((row >= col).astype(F32).astype(BF16), rate_step)
    up = dot((row <= col).astype(F32).astype(BF16), rate_step)
    down = down[:, 0:128] + (down[:, 128:256] + down[:, 256:384])
    up = up[:, 0:128] + (up[:, 128:256] + up[:, 256:384])
    lane = iota((PATCH, 128), 1)
    prefix = jnp.where(lane < HEADS, down, up)
    total = jnp.where(lane[0:1] < HEADS, down[PATCH - 1 :, :], up[0:1, :])
    log_mine[...] = jnp.broadcast_to(total, (8, 128))
    log_in[u] = log_mine[...]

    def send_logs(d, _):
        v = lax.rem(u + d, 16)
        pltpu.make_async_remote_copy(
            log_mine,
            log_in.at[u],
            log_send.at[v],
            log_recv.at[u],
            (2 * slab + v % 2, v // 2),
            MESH,
        ).start()
        return 0

    lax.fori_loop(1, 16, send_logs, 0)

    columns[...] = split(prefix, 3)
    fac[...] = split(jnp.exp2(total - prefix) * step, 2)
    ep[...] = split(jnp.exp2(prefix), 2)
    q_rows[...] = (prefix - LOG2E * jnp.log(step)).T

    def convolved(offset):
        span = pl.ds(offset, CHUNK)
        xbc[...] = dot(tok[...], w_in[:, span]).astype(BF16).astype(F32)
        forward = conv_bias[0:1, span]
        backward = conv_bias[1:2, span]
        for k in range(4):
            forward = forward + conv_weight[0, k : k + 1, span] * xbc[pl.ds(EDGE - 3 + k, PATCH), :]
            backward = (
                backward + conv_weight[1, k : k + 1, span] * xbc[pl.ds(EDGE + 3 - k, PATCH), :]
            )
        forward, backward = silu(forward).astype(BF16), silu(backward).astype(BF16)
        conv_f[:, span] = forward
        conv_b[:, span] = backward
        return forward, backward

    loads[0].wait()
    both = convolved(INNER)
    for e in range(2):
        b_turned[e] = both[e][:, 0:STATE].astype(F32).T.astype(BF16)
    loads[1].wait()

    def pair_copy():
        return pltpu.make_async_remote_copy(
            st.at[2], st.at[c], pair_send, pair_recv, (2 * slab + 1 - c, s), MESH
        )

    def head_target(t):
        return lambda l: (l >> 6) + jnp.where(l < CHUNK, 4 * t, HEADS - 4 + 4 * t)

    def project(i, _):
        t = lax.rem((1 - c) * 3 + i, 6)
        x_f, x_b = convolved(pl.multiple_of(t * CHUNK, CHUNK))
        factor = dot(fac[...], spread(2, 2 * CHUNK, head_target(t)))
        slot = jnp.where(t // 3 == c, c, 2)
        place = pl.ds(pl.multiple_of((t % 3) * CHUNK, CHUNK), CHUNK)
        for e, x in ((0, x_f), (1, x_b)):
            scaled = (x.astype(F32) * factor[:, e * CHUNK : (e + 1) * CHUNK]).astype(BF16)
            st[slot, e, :, place] = dot(b_turned[e], scaled)

        @pl.when(i == 2)
        def _():
            pair_copy().start()

        return 0

    lax.fori_loop(0, 6, project, 0)

    def wait_logs(d, _):
        v = lax.rem(u + d, 16)
        pltpu.make_async_remote_copy(
            log_mine, log_in.at[v], log_send.at[v], log_recv.at[v], (tm, s), MESH
        ).wait_recv()
        return 0

    lax.fori_loop(1, 16, wait_logs, 0)
    chips = [log_in[2 * k][0:1, :] + log_in[2 * k + 1][0:1, :] for k in range(GROUP)]
    zero = jnp.zeros((1, 128), F32)
    before, after = [zero], [zero]
    for k in range(GROUP):
        before.append(before[-1] + chips[k])
        after.append(after[-1] + chips[GROUP - 1 - k])
    narrow = iota((1, 128), 1) < HEADS
    outside = [jnp.where(narrow, before[k], after[GROUP - 1 - k]) for k in range(GROUP)]
    log_slab[...] = jnp.broadcast_to(before[GROUP], (8, 128))
    log_slabs[slab] = log_slab[...]

    def slab_log_copy(t, source):
        return pltpu.make_async_remote_copy(
            log_slab, log_slabs.at[source], logt_send.at[t], logt_recv.at[source], (2 * t + c, s), MESH
        )

    def send_slab_logs(d, _):
        slab_log_copy(lax.rem(slab + d, GROUP), slab).start()
        return 0

    lax.fori_loop(1, GROUP, send_slab_logs, 0)

    half_target = lambda l: (l >> 6) + jnp.where(l < HALF, 12 * c, HEADS - 12 + 12 * c)
    table = jnp.concatenate(
        chips
        + outside
        + [log_in[2 * s][0:1, :], log_in[2 * s + 1][0:1, :]]
        + [jnp.zeros((6, 128), F32)],
        axis=0,
    )
    expand = spread(3, INNER, half_target)
    coef[...] = dot(split(jnp.exp2(table), 3), expand)

    pair_copy().wait_recv()
    d0, d1 = coef[16:17, :], coef[17:18, :]

    def part_copy(k, source):
        return pltpu.make_async_remote_copy(
            part_out.at[k],
            part_in.at[source],
            part_send.at[k],
            part_recv.at[source],
            (tm, k),
            MESH,
        )

    def combined(k):
        rows = pl.ds(pl.multiple_of(k * 16, 16), 16)
        return jnp.concatenate(
            [
                d1[:, :HALF] * st[0, 0, rows, :] + st[1, 0, rows, :],
                d0[:, HALF:] * st[1, 1, rows, :] + st[0, 1, rows, :],
            ],
            axis=1,
        ).astype(BF16)

    def send_part(d, _):
        k = lax.rem(s + d, GROUP)
        part_out[k] = combined(k)
        part_copy(k, s).start()
        return 0

    lax.fori_loop(1, GROUP, send_part, 0)
    part_in[s] = combined(s)

    for e, conv in ((0, conv_f), (1, conv_b)):
        scores[e] = lax.dot_general(
            conv[:, INNER + STATE :],
            conv[:, INNER : INNER + STATE],
            (((1,), (1,)), ((), ())),
            preferred_element_type=F32,
        )
    lower = iota((128, 128), 0) >= iota((128, 128), 1)
    upper = iota((128, 128), 0) <= iota((128, 128), 1)
    near = [
        (iota((1, 128), 1) < 64).astype(F32).astype(BF16),
        (iota((1, 128), 1) >= 64).astype(F32).astype(BF16),
    ]

    def weigh(e, i, j, column, line, mask):
        gap = column[128 * i : 128 * i + 128, :] - line[:, 128 * j : 128 * j + 128]
        if mask is not None:
            gap = jnp.where(mask, gap, -jnp.inf)
        return (
            scores[e, 128 * i : 128 * i + 128, 128 * j : 128 * j + 128] * jnp.exp2(gap)
        ).astype(BF16)

    def within(t, _):
        span = pl.ds(pl.multiple_of(t * 128, 128), 128)
        x_f, x_b = conv_f[:, span], conv_b[:, span]
        wide = dot(
            columns[...],
            spread(3, 512, lambda l: 2 * t + ((l >> 7) & 1) + jnp.where(l < 256, 0, HEADS)),
        )
        tops, bottoms, top_x, bottom_x = [], [], [], []
        for h in range(2):
            pf, pb = wide[:, 128 * h : 128 * h + 128], wide[:, 256 + 128 * h : 384 + 128 * h]
            qf, qb = q_rows[pl.ds(2 * t + h, 1), :], q_rows[pl.ds(HEADS + 2 * t + h, 1), :]
            tops += [
                weigh(0, 0, 0, pf, qf, lower),
                weigh(1, 0, 0, pb, qb, upper),
                weigh(1, 0, 1, pb, qb, None),
            ]
            bottoms += [
                weigh(0, 1, 0, pf, qf, None),
                weigh(0, 1, 1, pf, qf, lower),
                weigh(1, 1, 1, pb, qb, upper),
            ]
            xf, xb = x_f * near[h], x_b * near[h]
            top_x += [xf[0:128], xb]
            bottom_x += [xf, xb[128:256]]
        y[0:128, span] = dot(jnp.concatenate(tops, axis=1), jnp.concatenate(top_x, axis=0))
        y[128:256, span] = dot(jnp.concatenate(bottoms, axis=1), jnp.concatenate(bottom_x, axis=0))
        return 0

    def gate_columns(t, _):
        span = pl.ds(pl.multiple_of(t * CHUNK, CHUNK), CHUNK)
        gate[:, span] = silu(dot(tok[EDGE : EDGE + PATCH, :], w_z[:, span]))
        return 0

    loads[2].wait()
    lax.fori_loop(0, 6, gate_columns, 0)
    lax.fori_loop(0, 3, within, 0)

    def wait_part(d, _):
        k = lax.rem(s + d, GROUP)
        part_copy(k, k).wait_recv()
        return 0

    lax.fori_loop(1, GROUP, wait_part, 0)
    forward = jnp.zeros((16, HALF), F32)
    backward = jnp.zeros((16, HALF), F32)
    for k in range(GROUP):
        r = GROUP - 1 - k
        local[k, :, :HALF] = forward
        local[r, :, HALF:] = backward
        forward = coef[k : k + 1, :HALF] * forward + part_in[k, :, :HALF].astype(F32)
        backward = coef[r : r + 1, HALF:] * backward + part_in[r, :, HALF:].astype(F32)
    slab_out[...] = jnp.concatenate([forward, backward], axis=1).astype(BF16)

    def slab_copy(t, source):
        return pltpu.make_async_remote_copy(
            slab_out, slab_in.at[source], slab_send.at[t], slab_recv.at[source], (2 * t + c, s), MESH
        )

    def send_slab(d, _):
        slab_copy(lax.rem(slab + d, GROUP), slab).start()
        return 0

    lax.fori_loop(1, GROUP, send_slab, 0)
    slab_in[slab] = slab_out[...]

    lax.fori_loop(3, 8, within, 0)

    def wait_slab(d, _):
        t = lax.rem(slab + d, GROUP)
        slab_log_copy(t, t).wait_recv()
        slab_copy(t, t).wait_recv()
        return 0

    lax.fori_loop(1, GROUP, wait_slab, 0)
    table = jnp.concatenate([log_slabs[t][0:1, :] for t in range(GROUP)], axis=0)
    coef_t[...] = dot(split(jnp.exp2(table), 3), spread(3, INNER, half_target))
    forward = jnp.zeros((16, HALF), F32)
    backward = jnp.zeros((16, HALF), F32)
    for k in range(GROUP):
        r = GROUP - 1 - k
        forward = jnp.where(
            k < slab, coef_t[k : k + 1, :HALF] * forward + slab_in[k, :, :HALF].astype(F32), forward
        )
        backward = jnp.where(
            r > slab, coef_t[r : r + 1, HALF:] * backward + slab_in[r, :, HALF:].astype(F32), backward
        )
    come = jnp.concatenate([forward, backward], axis=1)

    def ent_copy(k, source):
        return pltpu.make_async_remote_copy(
            ent_out.at[k], ent_in.at[source], ent_send.at[k], ent_recv.at[source], (tm, k), MESH
        )

    def entering(k):
        return (local[k] + coef[pl.ds(GROUP + k, 1), :] * come).astype(BF16)

    def send_ent(d, _):
        k = lax.rem(s + d, GROUP)
        ent_out[k] = entering(k)
        ent_copy(k, s).start()
        return 0

    lax.fori_loop(1, GROUP, send_ent, 0)
    ent_in[s] = entering(s)

    lax.fori_loop(8, 12, within, 0)

    def wait_ent(d, _):
        k = lax.rem(s + d, GROUP)
        ent_copy(k, k).wait_recv()
        return 0

    lax.fori_loop(1, GROUP, wait_ent, 0)
    for k in range(GROUP):
        rows = slice(16 * k, 16 * k + 16)
        first, last = ent_in[k, :, :HALF], ent_in[k, :, HALF:]
        ent[0, 0, rows, :] = first
        ent[1, 1, rows, :] = last
        ent[1, 0, rows, :] = (d0[:, :HALF] * first.astype(F32) + st[0, 0, rows, :]).astype(BF16)
        ent[0, 1, rows, :] = (d1[:, HALF:] * last.astype(F32) + st[1, 1, rows, :]).astype(BF16)
    ent_pair = pltpu.make_async_remote_copy(
        ent.at[1 - c], ent.at[2], epair_send, epair_recv, (2 * slab + 1 - c, s), MESH
    )
    ent_pair.start()

    def finish(i, squares):
        t = lax.rem(c * 3 + i, 6)

        @pl.when(i == 3)
        def _():
            ent_pair.wait_recv()

        span = pl.ds(pl.multiple_of(t * CHUNK, CHUNK), CHUNK)
        slot = jnp.where(t // 3 == c, c, 2)
        place = pl.ds(pl.multiple_of((t % 3) * CHUNK, CHUNK), CHUNK)
        grow = dot(ep[...], spread(2, 2 * CHUNK, head_target(t)))
        total = y[:, span]
        for e, conv in ((0, conv_f), (1, conv_b)):
            total = total + grow[:, e * CHUNK : (e + 1) * CHUNK] * dot(
                conv[:, INNER + STATE :], ent[slot, e, :, place]
            )
            total = total + skip_rows[e : e + 1, span] * conv[:, span].astype(F32)
        gated = total * gate[:, span]
        y[:, span] = gated
        return squares + jnp.sum(gated * gated, axis=1, keepdims=True)

    squares = lax.fori_loop(0, 6, finish, jnp.zeros((PATCH, 1), F32))
    scale = lax.rsqrt(squares * (1.0 / INNER) + 1e-05)
    gains = norm_gain[...].reshape(1, INNER)
    loads[3].wait()

    core_home = s // 4
    slot_home = u - 8 * core_home

    def send_out(b, action):
        mine = jnp.logical_and(b == s, core_home == c)
        src, dst = mix.at[pl.ds(pl.multiple_of(32 * b, 32), 32)], out.at[slot_home]

        @pl.when(jnp.logical_not(mine))
        def _():
            action(
                pltpu.make_async_remote_copy(
                    src, dst, out_send.at[b], out_sem, (2 * slab + core_home, b), MESH
                )
            )

        if action is started:

            @pl.when(mine)
            def _():
                pltpu.make_async_copy(src, dst, out_sem).start()

    for half in range(2):
        rows = slice(128 * half, 128 * half + 128)
        normed = (y[rows, :] * scale[rows, :] * gains).astype(BF16)
        mix[rows, :] = dot(normed, w_out[...]).astype(BF16)
        for b in range(4 * half, 4 * half + 4):
            send_out(b, started)

    all_tokens(left)
    pair_copy().wait_send()
    ent_pair.wait_send()

    def wait_sent(d, _):
        v = lax.rem(u + d, 16)
        pltpu.make_async_remote_copy(
            log_mine, log_in.at[u], log_send.at[v], log_recv.at[u], (tm, s), MESH
        ).wait_send()
        return 0

    lax.fori_loop(1, 16, wait_sent, 0)

    def wait_sent_group(d, _):
        k = lax.rem(s + d, GROUP)
        part_copy(k, s).wait_send()
        ent_copy(k, s).wait_send()
        t = lax.rem(slab + d, GROUP)
        slab_log_copy(t, slab).wait_send()
        slab_copy(t, slab).wait_send()
        return 0

    lax.fori_loop(1, GROUP, wait_sent_group, 0)
    for b in range(8):
        send_out(b, left)
    pltpu.make_async_copy(out, out, out_sem).wait()


def body(*args):
    args = args[:4] + (args[4].T,) + args[5:]
    hbm = pl.BlockSpec(memory_space=pl.ANY)
    dma = pltpu.SemaphoreType.DMA
    scratch = [
        pltpu.VMEM((HEADS, D), BF16),
        pltpu.VMEM((2, 4, WIDE), F32),
        pltpu.VMEM((2, WIDE), F32),
        pltpu.VMEM((2, HEADS), F32),
        pltpu.VMEM((2, HEADS), F32),
        pltpu.VMEM((2, HEADS), F32),
        pltpu.VMEM((INNER,), F32),
        pltpu.VMEM((D, WIDE), BF16),
        pltpu.VMEM((D, INNER), BF16),
        pltpu.VMEM((INNER, D), BF16),
        pltpu.VMEM((PATCH + 2 * EDGE, D), BF16),
        pltpu.VMEM((PATCH + 2 * EDGE, CHUNK), F32),
        pltpu.VMEM((PATCH, WIDE), BF16),
        pltpu.VMEM((PATCH, WIDE), BF16),
        pltpu.VMEM((2, STATE, PATCH), BF16),
        pltpu.VMEM((PATCH, INNER), F32),
        pltpu.VMEM((PATCH, INNER), F32),
        pltpu.VMEM((2, PATCH, PATCH), F32),
        pltpu.VMEM((PATCH, 384), BF16),
        pltpu.VMEM((128, PATCH), F32),
        pltpu.VMEM((PATCH, 256), BF16),
        pltpu.VMEM((PATCH, 256), BF16),
        pltpu.VMEM((8, INNER), F32),
        pltpu.VMEM((3, 2, STATE, HALF), F32),
        pltpu.VMEM((GROUP, 16, INNER), BF16),
        pltpu.VMEM((GROUP, 16, INNER), BF16),
        pltpu.VMEM((GROUP, 16, INNER), F32),
        pltpu.VMEM((24, INNER), F32),
        pltpu.VMEM((GROUP, INNER), F32),
        pltpu.VMEM((16, INNER), BF16),
        pltpu.VMEM((GROUP, 16, INNER), BF16),
        pltpu.VMEM((GROUP, 16, INNER), BF16),
        pltpu.VMEM((GROUP, 16, INNER), BF16),
        pltpu.VMEM((3, 2, STATE, HALF), BF16),
        pltpu.VMEM((8, 128), F32),
        pltpu.VMEM((16, 8, 128), F32),
        pltpu.VMEM((8, 128), F32),
        pltpu.VMEM((GROUP, 8, 128), F32),
        pltpu.VMEM((PATCH, D), BF16),
        dma((11,)),
        dma,
        dma((8,)),
        dma((2, 8)),
        dma((16,)),
        dma((16,)),
        dma((GROUP,)),
        dma((GROUP,)),
        dma,
        dma,
        dma((GROUP,)),
        dma((GROUP,)),
        dma((GROUP,)),
        dma((GROUP,)),
        dma((GROUP,)),
        dma((GROUP,)),
        dma,
        dma,
        dma((8,)),
        dma,
    ]
    return pl.pallas_call(
        kernel,
        out_shape=jax.ShapeDtypeStruct((8, 32, D), BF16),
        in_specs=[hbm] * 12,
        out_specs=hbm,
        scratch_shapes=scratch,
        compiler_params=pltpu.CompilerParams(
            collective_id=0, has_side_effects=True, vmem_limit_bytes=60 * 1024 * 1024
        ),
    )(*args)


def solution(mesh):
    return jax.shard_map(
        body,
        mesh=mesh,
        in_specs=(P("tm", "space", None),) + (P(),) * 11,
        out_specs=P("tm", "space", None),
        check_vma=False,
    )
```

```python
import jax
import jax.numpy as jnp
from jax import lax
from jax.experimental import pallas as pl
from jax.experimental.pallas import tpu as pltpu
from jax.sharding import PartitionSpec as P

HEADS = 24
STATE = 128
PATCH = 256
D = 768
INNER = 1536
WIDE = INNER + 2 * STATE
HALF = INNER // 2
GROUP = 8
EDGE = 16
CHUNK = 256
LOG2E = 1.4426950408889634
F32, BF16 = jnp.float32, jnp.bfloat16
MESH = pl.DeviceIdType.MESH


def iota(shape, dim):
    return lax.broadcasted_iota(jnp.int32, shape, dim)


def split(a, parts):
    pieces = []
    for _ in range(parts):
        piece = a.astype(BF16)
        pieces.append(piece)
        a = a - piece.astype(F32)
    return jnp.concatenate(pieces, axis=1)


def dot(a, b):
    return jnp.dot(a, b, preferred_element_type=F32)


def silu(a):
    half = 0.5 * a
    return half + half * jnp.tanh(half)


def spread(parts, width, target):
    rows = iota((parts * 128, width), 0) & 127
    return (rows == target(iota((parts * 128, width), 1))).astype(F32).astype(BF16)


def pad_lanes(first, second):
    rows = first.shape[0]
    return jnp.concatenate([first, second, jnp.zeros((rows, 128 - 2 * HEADS), F32)], axis=1)


def kernel(
    tokens,
    x_weight,
    z_weight,
    bc_weight,
    dt_weight_hbm,
    conv_weight_hbm,
    conv_bias_hbm,
    dt_bias_hbm,
    decay_rate_hbm,
    skip_gain_hbm,
    norm_gain_hbm,
    out_weight,
    out,
    dt_weight,
    conv_weight,
    conv_bias,
    dt_bias,
    decay_rate,
    skip_gain,
    norm_gain,
    w_in,
    w_z,
    w_out,
    tok,
    xbc,
    conv_f,
    conv_b,
    b_turned,
    gate,
    y,
    scores,
    columns,
    q_rows,
    fac,
    ep,
    skip_rows,
    expand,
    heads,
    grow,
    st,
    part_out,
    part_in,
    local,
    coef,
    coef_t,
    slab_out,
    slab_in,
    ent_out,
    ent_in,
    ent,
    log_mine,
    log_in,
    log_chip,
    log_chips,
    log_slab,
    log_slabs,
    mix,
    w_sem,
    tok_sem,
    tok_send,
    edge_send,
    log_send,
    log_recv,
    logc_send,
    logc_recv,
    logt_send,
    logt_recv,
    pair_send,
    pair_recv,
    part_send,
    part_recv,
    slab_send,
    slab_recv,
    ent_send,
    ent_recv,
    epair_send,
    epair_recv,
    out_send,
    out_sem,
):
    tm = lax.axis_index("tm")
    s = lax.axis_index("space")
    slab = tm // 2
    c = tm % 2
    u = 2 * s + c
    corner_hi = jnp.logical_and(s == GROUP - 1, c == 1)
    corner_lo = jnp.logical_and(s == 0, c == 0)

    loads = [
        pltpu.make_async_copy(bc_weight, w_in.at[:, pl.ds(INNER, 2 * STATE)], w_sem.at[0]),
        pltpu.make_async_copy(x_weight, w_in.at[:, pl.ds(0, INNER)], w_sem.at[1]),
        pltpu.make_async_copy(z_weight, w_z, w_sem.at[2]),
        pltpu.make_async_copy(out_weight, w_out, w_sem.at[3]),
    ]
    small = [
        pltpu.make_async_copy(source, target, w_sem.at[4 + at])
        for at, (source, target) in enumerate(
            (
                (skip_gain_hbm, skip_gain),
                (dt_weight_hbm, dt_weight),
                (dt_bias_hbm, dt_bias),
                (decay_rate_hbm, decay_rate),
                (conv_weight_hbm, conv_weight),
                (conv_bias_hbm, conv_bias),
                (norm_gain_hbm, norm_gain),
            )
        )
    ]
    for load in small + loads:
        load.start()

    barrier = pltpu.get_barrier_semaphore()

    def greet(d, _):
        v = lax.rem(u + d, 16)
        pl.semaphore_signal(barrier, inc=1, device_id=(2 * slab + v % 2, v // 2), device_id_type=MESH)
        return 0

    lax.fori_loop(1, 16, greet, 0)

    def greet_slab(d, _):
        t = lax.rem(slab + d, GROUP)
        pl.semaphore_signal(barrier, inc=1, device_id=(2 * t + c, s), device_id_type=MESH)
        return 0

    lax.fori_loop(1, GROUP, greet_slab, 0)
    above = lax.rem(slab + 1, GROUP)
    below = lax.rem(slab + GROUP - 1, GROUP)

    @pl.when(corner_hi)
    def _():
        pl.semaphore_signal(barrier, inc=1, device_id=(2 * above, 0), device_id_type=MESH)

    @pl.when(corner_lo)
    def _():
        pl.semaphore_signal(
            barrier, inc=1, device_id=(2 * below + 1, GROUP - 1), device_id_type=MESH
        )

    pl.semaphore_wait(barrier, 22 + jnp.logical_or(corner_hi, corner_lo).astype(jnp.int32))

    def send_tokens(j, action):
        ds, dc = 4 * c + j // 2, j % 2
        mine = jnp.logical_and(ds == s, dc == c)
        src, dst = tokens.at[j], tok.at[pl.ds(pl.multiple_of(EDGE + 32 * s, 16), 32)]

        @pl.when(jnp.logical_not(mine))
        def _():
            action(
                pltpu.make_async_remote_copy(
                    src, dst, tok_send.at[j], tok_sem, (2 * slab + dc, ds), MESH
                )
            )

        if action is started:

            @pl.when(mine)
            def _():
                pltpu.make_async_copy(src, dst, tok_sem).start()

    def send_edge(j, action, side):
        g = 8 * c + j + (1 if side == 0 else -1)
        ds, dc = lax.rem(g + 16, 16) // 2, lax.rem(g + 16, 16) % 2
        dt = lax.rem(slab + lax.div(g + 16, 16) - 1 + GROUP, GROUP)
        mine = jnp.logical_and(jnp.logical_and(ds == s, dc == c), dt == slab)
        src = tokens.at[j, pl.ds(16 if side == 0 else 0, EDGE)]
        dst = tok.at[pl.ds(0 if side == 0 else EDGE + PATCH, EDGE)]

        @pl.when(jnp.logical_not(mine))
        def _():
            action(
                pltpu.make_async_remote_copy(
                    src, dst, edge_send.at[side, j], tok_sem, (2 * dt + dc, ds), MESH
                )
            )

        if action is started:

            @pl.when(mine)
            def _():
                pltpu.make_async_copy(src, dst, tok_sem).start()

    def started(copy):
        copy.start()

    def left(copy):
        copy.wait_send()

    def all_tokens(action):
        def one(i, _):
            send_tokens(lax.rem(s + i, 8), action)
            return 0

        lax.fori_loop(0, 8, one, 0)

        @pl.when(s == GROUP - 1)
        def _():
            def one(j, _):
                send_edge(j, action, 0)
                return 0

            lax.fori_loop(0, 8, one, 0)

        @pl.when(s == 0)
        def _():
            def one(j, _):
                send_edge(j, action, 1)
                return 0

            lax.fori_loop(0, 8, one, 0)

    all_tokens(started)

    for load in small:
        load.wait()
    half_target = lambda l: (l >> 6) + jnp.where(l < HALF, 12 * c, HEADS - 12 + 12 * c)
    expand[...] = spread(3, INNER, half_target)
    for e in range(2):
        heads[e] = spread(3, INNER, lambda l: HEADS * e + (l >> 6))
    skips = pad_lanes(skip_gain[0:1, :], skip_gain[1:2, :])
    for e in range(2):
        skip_rows[e : e + 1, :] = dot(split(jnp.broadcast_to(skips, (8, 128)), 3), heads[e])[0:1, :]

    pltpu.make_async_copy(tok, tok, tok_sem).wait()

    @pl.when(jnp.logical_and(corner_lo, slab == 0))
    def _():
        tok[0:EDGE, :] = jnp.zeros((EDGE, D), BF16)

    @pl.when(jnp.logical_and(corner_hi, slab == GROUP - 1))
    def _():
        tok[EDGE + PATCH :, :] = jnp.zeros((EDGE, D), BF16)

    dt_raw = lax.dot_general(
        tok[EDGE : EDGE + PATCH, :],
        dt_weight[...],
        (((1,), (1,)), ((), ())),
        preferred_element_type=F32,
    )
    step = jax.nn.softplus(
        pad_lanes(dt_raw, dt_raw) + pad_lanes(dt_bias[0:1, :], dt_bias[1:2, :])
    )
    rates = pad_lanes(decay_rate[0:1, :], decay_rate[1:2, :])
    rate_step = split(step * (rates * -LOG2E), 3)
    row, col = iota((PATCH, PATCH), 0), iota((PATCH, PATCH), 1)
    down = dot((row >= col).astype(F32).astype(BF16), rate_step)
    up = dot((row <= col).astype(F32).astype(BF16), rate_step)
    down = down[:, 0:128] + (down[:, 128:256] + down[:, 256:384])
    up = up[:, 0:128] + (up[:, 128:256] + up[:, 256:384])
    lane = iota((PATCH, 128), 1)
    prefix = jnp.where(lane < HEADS, down, up)
    total = jnp.where(lane[0:1] < HEADS, down[PATCH - 1 :, :], up[0:1, :])
    log_mine[...] = jnp.broadcast_to(total, (8, 128))
    log_in[c] = log_mine[...]

    def log_copy():
        return pltpu.make_async_remote_copy(
            log_mine, log_in.at[c], log_send, log_recv, (2 * slab + 1 - c, s), MESH
        )

    log_copy().start()

    columns[...] = split(prefix, 3)
    fac[...] = split(jnp.exp2(total - prefix) * step, 2)
    ep[...] = split(jnp.exp2(prefix), 2)
    q_rows[...] = (prefix - LOG2E * jnp.log(step)).T

    def convolved(offset):
        span = pl.ds(offset, CHUNK)
        xbc[...] = dot(tok[...], w_in[:, span]).astype(BF16).astype(F32)
        forward = conv_bias[0:1, span]
        backward = conv_bias[1:2, span]
        for k in range(4):
            forward = forward + conv_weight[0, k : k + 1, span] * xbc[pl.ds(EDGE - 3 + k, PATCH), :]
            backward = (
                backward + conv_weight[1, k : k + 1, span] * xbc[pl.ds(EDGE + 3 - k, PATCH), :]
            )
        forward, backward = silu(forward).astype(BF16), silu(backward).astype(BF16)
        conv_f[:, span] = forward
        conv_b[:, span] = backward
        return forward, backward

    loads[0].wait()
    both = convolved(INNER)
    for e in range(2):
        b_turned[e] = both[e][:, 0:STATE].astype(F32).T.astype(BF16)
    loads[1].wait()

    def pair_copy():
        return pltpu.make_async_remote_copy(
            st.at[2], st.at[c], pair_send, pair_recv, (2 * slab + 1 - c, s), MESH
        )

    def project(i, _):
        t = lax.rem((1 - c) * 3 + i, 6)
        x_f, x_b = convolved(pl.multiple_of(t * CHUNK, CHUNK))
        slot = jnp.where(t // 3 == c, c, 2)
        place = pl.ds(pl.multiple_of((t % 3) * CHUNK, CHUNK), CHUNK)
        for e, x in ((0, x_f), (1, x_b)):
            factor = dot(fac[...], heads[e, 0:256, pl.ds(pl.multiple_of(t * CHUNK, CHUNK), CHUNK)])
            scaled = (x.astype(F32) * factor).astype(BF16)
            st[slot, e, :, place] = dot(b_turned[e], scaled)

        @pl.when(i == 2)
        def _():
            pair_copy().start()

        return 0

    lax.fori_loop(0, 6, project, 0)

    log_copy().wait_recv()
    pair_logs = [log_in[0][0:1, :], log_in[1][0:1, :]]
    chip_log = pair_logs[0] + pair_logs[1]
    log_chip[...] = jnp.broadcast_to(chip_log, (8, 128))
    log_chips[s] = log_chip[...]
    coef[16:24, :] = dot(
        split(jnp.exp2(jnp.concatenate(pair_logs + [jnp.zeros((6, 128), F32)], axis=0)), 3),
        expand[...],
    )

    pair_copy().wait_recv()
    d0, d1 = coef[16:17, :], coef[17:18, :]

    def part_copy(k, source):
        return pltpu.make_async_remote_copy(
            part_out.at[k],
            part_in.at[source],
            part_send.at[k],
            part_recv.at[source],
            (tm, k),
            MESH,
        )

    def combined(k):
        rows = pl.ds(pl.multiple_of(k * 16, 16), 16)
        return jnp.concatenate(
            [
                d1[:, :HALF] * st[0, 0, rows, :] + st[1, 0, rows, :],
                d0[:, HALF:] * st[1, 1, rows, :] + st[0, 1, rows, :],
            ],
            axis=1,
        ).astype(BF16)

    def send_part(d, _):
        k = lax.rem(s + d, GROUP)
        part_out[k] = combined(k)
        part_copy(k, s).start()
        return 0

    lax.fori_loop(1, GROUP, send_part, 0)

    def chip_log_copy(k, source):
        return pltpu.make_async_remote_copy(
            log_chip, log_chips.at[source], logc_send.at[k], logc_recv.at[source], (tm, k), MESH
        )

    def send_chip_logs(d, _):
        chip_log_copy(lax.rem(s + d, GROUP), s).start()
        return 0

    lax.fori_loop(1, GROUP, send_chip_logs, 0)
    part_in[s] = combined(s)

    for e, conv in ((0, conv_f), (1, conv_b)):
        scores[e] = lax.dot_general(
            conv[:, INNER + STATE :],
            conv[:, INNER : INNER + STATE],
            (((1,), (1,)), ((), ())),
            preferred_element_type=F32,
        )
    lower = iota((128, 128), 0) >= iota((128, 128), 1)
    upper = iota((128, 128), 0) <= iota((128, 128), 1)
    near = [
        (iota((1, 128), 1) < 64).astype(F32).astype(BF16),
        (iota((1, 128), 1) >= 64).astype(F32).astype(BF16),
    ]

    def weigh(e, i, j, column, line, mask):
        gap = column[128 * i : 128 * i + 128, :] - line[:, 128 * j : 128 * j + 128]
        if mask is not None:
            gap = jnp.where(mask, gap, -jnp.inf)
        return (
            scores[e, 128 * i : 128 * i + 128, 128 * j : 128 * j + 128] * jnp.exp2(gap)
        ).astype(BF16)

    def within(t, _):
        span = pl.ds(pl.multiple_of(t * 128, 128), 128)
        x_f, x_b = conv_f[:, span], conv_b[:, span]
        wide = dot(
            columns[...],
            spread(3, 512, lambda l: 2 * t + ((l >> 7) & 1) + jnp.where(l < 256, 0, HEADS)),
        )
        tops, bottoms, top_x, bottom_x = [], [], [], []
        for h in range(2):
            pf, pb = wide[:, 128 * h : 128 * h + 128], wide[:, 256 + 128 * h : 384 + 128 * h]
            qf, qb = q_rows[pl.ds(2 * t + h, 1), :], q_rows[pl.ds(HEADS + 2 * t + h, 1), :]
            tops += [
                weigh(0, 0, 0, pf, qf, lower),
                weigh(1, 0, 0, pb, qb, upper),
                weigh(1, 0, 1, pb, qb, None),
            ]
            bottoms += [
                weigh(0, 1, 0, pf, qf, None),
                weigh(0, 1, 1, pf, qf, lower),
                weigh(1, 1, 1, pb, qb, upper),
            ]
            xf, xb = x_f * near[h], x_b * near[h]
            top_x += [xf[0:128], xb]
            bottom_x += [xf, xb[128:256]]
        skip = skip_rows[0:1, span] * x_f.astype(F32) + skip_rows[1:2, span] * x_b.astype(F32)
        y[0:128, span] = skip[0:128] + dot(jnp.concatenate(tops, axis=1), jnp.concatenate(top_x, axis=0))
        y[128:256, span] = skip[128:256] + dot(jnp.concatenate(bottoms, axis=1), jnp.concatenate(bottom_x, axis=0))
        return 0

    def gate_columns(t, _):
        span = pl.ds(pl.multiple_of(t * CHUNK, CHUNK), CHUNK)
        gate[:, span] = silu(dot(tok[EDGE : EDGE + PATCH, :], w_z[:, span]))
        for e in range(2):
            grow[e, :, span] = dot(ep[...], heads[e, 0:256, span])
        return 0

    loads[2].wait()
    lax.fori_loop(0, 6, gate_columns, 0)

    def wait_chip_logs(d, _):
        k = lax.rem(s + d, GROUP)
        chip_log_copy(k, k).wait_recv()
        return 0

    lax.fori_loop(1, GROUP, wait_chip_logs, 0)
    chips = [log_chips[k][0:1, :] for k in range(GROUP)]
    zero = jnp.zeros((1, 128), F32)
    before, after = [zero], [zero]
    for k in range(GROUP):
        before.append(before[-1] + chips[k])
        after.append(after[-1] + chips[GROUP - 1 - k])
    narrow = iota((1, 128), 1) < HEADS
    outside = [jnp.where(narrow, before[k], after[GROUP - 1 - k]) for k in range(GROUP)]
    log_slab[...] = jnp.broadcast_to(before[GROUP], (8, 128))
    log_slabs[slab] = log_slab[...]

    def slab_log_copy(t, source):
        return pltpu.make_async_remote_copy(
            log_slab,
            log_slabs.at[source],
            logt_send.at[t],
            logt_recv.at[source],
            (2 * t + c, s),
            MESH,
        )

    def send_slab_logs(d, _):
        slab_log_copy(lax.rem(slab + d, GROUP), slab).start()
        return 0

    lax.fori_loop(1, GROUP, send_slab_logs, 0)
    coef[0:16, :] = dot(
        split(jnp.exp2(jnp.concatenate(chips + outside, axis=0)), 3), expand[...]
    )

    def wait_part(d, _):
        k = lax.rem(s + d, GROUP)
        part_copy(k, k).wait_recv()
        return 0

    lax.fori_loop(1, GROUP, wait_part, 0)
    forward = jnp.zeros((16, HALF), F32)
    backward = jnp.zeros((16, HALF), F32)
    for k in range(GROUP):
        r = GROUP - 1 - k
        local[k, :, :HALF] = forward
        local[r, :, HALF:] = backward
        forward = coef[k : k + 1, :HALF] * forward + part_in[k, :, :HALF].astype(F32)
        backward = coef[r : r + 1, HALF:] * backward + part_in[r, :, HALF:].astype(F32)
    slab_out[0] = forward.astype(BF16)
    slab_out[1] = backward.astype(BF16)

    def slab_copy(t, source):
        return pltpu.make_async_remote_copy(
            slab_out.at[(t < slab).astype(jnp.int32)],
            slab_in.at[source],
            slab_send.at[t],
            slab_recv.at[source],
            (2 * t + c, s),
            MESH,
        )

    def send_slab(d, _):
        slab_copy(lax.rem(slab + d, GROUP), slab).start()
        return 0

    lax.fori_loop(1, GROUP, send_slab, 0)
    slab_in[slab] = slab_out[0]

    lax.fori_loop(0, 5, within, 0)

    def wait_slab_logs(d, _):
        t = lax.rem(slab + d, GROUP)
        slab_log_copy(t, t).wait_recv()
        return 0

    lax.fori_loop(1, GROUP, wait_slab_logs, 0)
    table = jnp.concatenate([log_slabs[t][0:1, :] for t in range(GROUP)], axis=0)
    coef_t[...] = dot(split(jnp.exp2(table), 3), expand[...])

    def wait_slab(d, _):
        t = lax.rem(slab + d, GROUP)
        slab_copy(t, t).wait_recv()
        return 0

    lax.fori_loop(1, GROUP, wait_slab, 0)
    forward = jnp.zeros((16, HALF), F32)
    backward = jnp.zeros((16, HALF), F32)
    for k in range(GROUP):
        r = GROUP - 1 - k
        forward = jnp.where(
            k < slab, coef_t[k : k + 1, :HALF] * forward + slab_in[k].astype(F32), forward
        )
        backward = jnp.where(
            r > slab, coef_t[r : r + 1, HALF:] * backward + slab_in[r].astype(F32), backward
        )
    come = jnp.concatenate([forward, backward], axis=1)

    def ent_copy(k, source):
        return pltpu.make_async_remote_copy(
            ent_out.at[k], ent_in.at[source], ent_send.at[k], ent_recv.at[source], (tm, k), MESH
        )

    def entering(k):
        return (local[k] + coef[pl.ds(GROUP + k, 1), :] * come).astype(BF16)

    def send_ent(d, _):
        k = lax.rem(s + d, GROUP)
        ent_out[k] = entering(k)
        ent_copy(k, s).start()
        return 0

    lax.fori_loop(1, GROUP, send_ent, 0)
    ent_in[s] = entering(s)

    lax.fori_loop(5, 12, within, 0)

    def wait_ent(d, _):
        k = lax.rem(s + d, GROUP)
        ent_copy(k, k).wait_recv()
        return 0

    lax.fori_loop(1, GROUP, wait_ent, 0)
    for k in range(GROUP):
        rows = slice(16 * k, 16 * k + 16)
        first, last = ent_in[k, :, :HALF], ent_in[k, :, HALF:]
        ent[0, 0, rows, :] = first
        ent[1, 1, rows, :] = last
        ent[1, 0, rows, :] = (d0[:, :HALF] * first.astype(F32) + st[0, 0, rows, :]).astype(BF16)
        ent[0, 1, rows, :] = (d1[:, HALF:] * last.astype(F32) + st[1, 1, rows, :]).astype(BF16)
    ent_pair = pltpu.make_async_remote_copy(
        ent.at[1 - c], ent.at[2], epair_send, epair_recv, (2 * slab + 1 - c, s), MESH
    )
    ent_pair.start()

    def finish(i, squares):
        t = lax.rem(c * 3 + i, 6)

        @pl.when(i == 3)
        def _():
            ent_pair.wait_recv()

        span = pl.ds(pl.multiple_of(t * CHUNK, CHUNK), CHUNK)
        slot = jnp.where(t // 3 == c, c, 2)
        place = pl.ds(pl.multiple_of((t % 3) * CHUNK, CHUNK), CHUNK)
        total = y[:, span]
        for e, conv in ((0, conv_f), (1, conv_b)):
            total = total + grow[e, :, span] * dot(conv[:, INNER + STATE :], ent[slot, e, :, place])
        gated = total * gate[:, span]
        y[:, span] = gated
        return squares + jnp.sum(gated * gated, axis=1, keepdims=True)

    squares = lax.fori_loop(0, 6, finish, jnp.zeros((PATCH, 1), F32))
    scale = lax.rsqrt(squares * (1.0 / INNER) + 1e-05)
    gains = norm_gain[...].reshape(1, INNER)
    loads[3].wait()

    core_home = s // 4
    slot_home = u - 8 * core_home

    def send_out(b, action):
        mine = jnp.logical_and(b == s, core_home == c)
        src, dst = mix.at[pl.ds(pl.multiple_of(32 * b, 32), 32)], out.at[slot_home]

        @pl.when(jnp.logical_not(mine))
        def _():
            action(
                pltpu.make_async_remote_copy(
                    src, dst, out_send.at[b], out_sem, (2 * slab + core_home, b), MESH
                )
            )

        if action is started:

            @pl.when(mine)
            def _():
                pltpu.make_async_copy(src, dst, out_sem).start()

    for turn in range(2):
        half = turn
        rows = slice(128 * half, 128 * half + 128)
        near_scale = scale[rows]
        normed = (y[rows, :] * near_scale * gains).astype(BF16)
        mix[rows, :] = dot(normed, w_out[...]).astype(BF16)
        for i in range(4):
            send_out(4 * half + i, started)

    all_tokens(left)
    pair_copy().wait_send()
    ent_pair.wait_send()

    log_copy().wait_send()

    def wait_sent_group(d, _):
        k = lax.rem(s + d, GROUP)
        part_copy(k, s).wait_send()
        ent_copy(k, s).wait_send()
        chip_log_copy(k, s).wait_send()
        t = lax.rem(slab + d, GROUP)
        slab_log_copy(t, slab).wait_send()
        slab_copy(t, slab).wait_send()
        return 0

    lax.fori_loop(1, GROUP, wait_sent_group, 0)
    for b in range(8):
        send_out(b, left)
    pltpu.make_async_copy(out, out, out_sem).wait()


def body(*args):
    args = args[:4] + (args[4].T,) + args[5:]
    hbm = pl.BlockSpec(memory_space=pl.ANY)
    dma = pltpu.SemaphoreType.DMA
    scratch = [
        pltpu.VMEM((HEADS, D), BF16),
        pltpu.VMEM((2, 4, WIDE), F32),
        pltpu.VMEM((2, WIDE), F32),
        pltpu.VMEM((2, HEADS), F32),
        pltpu.VMEM((2, HEADS), F32),
        pltpu.VMEM((2, HEADS), F32),
        pltpu.VMEM((INNER,), F32),
        pltpu.VMEM((D, WIDE), BF16),
        pltpu.VMEM((D, INNER), BF16),
        pltpu.VMEM((INNER, D), BF16),
        pltpu.VMEM((PATCH + 2 * EDGE, D), BF16),
        pltpu.VMEM((PATCH + 2 * EDGE, CHUNK), F32),
        pltpu.VMEM((PATCH, WIDE), BF16),
        pltpu.VMEM((PATCH, WIDE), BF16),
        pltpu.VMEM((2, STATE, PATCH), BF16),
        pltpu.VMEM((PATCH, INNER), F32),
        pltpu.VMEM((PATCH, INNER), F32),
        pltpu.VMEM((2, PATCH, PATCH), F32),
        pltpu.VMEM((PATCH, 384), BF16),
        pltpu.VMEM((128, PATCH), F32),
        pltpu.VMEM((PATCH, 256), BF16),
        pltpu.VMEM((PATCH, 256), BF16),
        pltpu.VMEM((8, INNER), F32),
        pltpu.VMEM((384, INNER), BF16),
        pltpu.VMEM((2, 384, INNER), BF16),
        pltpu.VMEM((2, PATCH, INNER), F32),
        pltpu.VMEM((3, 2, STATE, HALF), F32),
        pltpu.VMEM((GROUP, 16, INNER), BF16),
        pltpu.VMEM((GROUP, 16, INNER), BF16),
        pltpu.VMEM((GROUP, 16, INNER), F32),
        pltpu.VMEM((24, INNER), F32),
        pltpu.VMEM((GROUP, INNER), F32),
        pltpu.VMEM((2, 16, HALF), BF16),
        pltpu.VMEM((GROUP, 16, HALF), BF16),
        pltpu.VMEM((GROUP, 16, INNER), BF16),
        pltpu.VMEM((GROUP, 16, INNER), BF16),
        pltpu.VMEM((3, 2, STATE, HALF), BF16),
        pltpu.VMEM((8, 128), F32),
        pltpu.VMEM((2, 8, 128), F32),
        pltpu.VMEM((8, 128), F32),
        pltpu.VMEM((GROUP, 8, 128), F32),
        pltpu.VMEM((8, 128), F32),
        pltpu.VMEM((GROUP, 8, 128), F32),
        pltpu.VMEM((PATCH, D), BF16),
        dma((11,)),
        dma,
        dma((8,)),
        dma((2, 8)),
        dma,
        dma,
        dma((GROUP,)),
        dma((GROUP,)),
        dma((GROUP,)),
        dma((GROUP,)),
        dma,
        dma,
        dma((GROUP,)),
        dma((GROUP,)),
        dma((GROUP,)),
        dma((GROUP,)),
        dma((GROUP,)),
        dma((GROUP,)),
        dma,
        dma,
        dma((8,)),
        dma,
    ]
    return pl.pallas_call(
        kernel,
        out_shape=jax.ShapeDtypeStruct((8, 32, D), BF16),
        in_specs=[hbm] * 12,
        out_specs=hbm,
        scratch_shapes=scratch,
        compiler_params=pltpu.CompilerParams(
            collective_id=0, has_side_effects=True, vmem_limit_bytes=60 * 1024 * 1024
        ),
    )(*args)


def solution(mesh):
    return jax.shard_map(
        body,
        mesh=mesh,
        in_specs=(P("tm", "space", None),) + (P(),) * 11,
        out_specs=P("tm", "space", None),
        check_vma=False,
    )
```

```python
import jax
import jax.numpy as jnp
from jax import lax
from jax.experimental import pallas as pl
from jax.experimental.pallas import tpu as pltpu
from jax.sharding import PartitionSpec as P

HEADS = 24
STATE = 128
PATCH = 256
D = 768
INNER = 1536
WIDE = INNER + 2 * STATE
HALF = INNER // 2
GROUP = 8
EDGE = 16
CHUNK = 256
LOG2E = 1.4426950408889634
F32, BF16 = jnp.float32, jnp.bfloat16
MESH = pl.DeviceIdType.MESH


def iota(shape, dim):
    return lax.broadcasted_iota(jnp.int32, shape, dim)


def split(a, parts):
    pieces = []
    for _ in range(parts):
        piece = a.astype(BF16)
        pieces.append(piece)
        a = a - piece.astype(F32)
    return jnp.concatenate(pieces, axis=1)


def dot(a, b):
    return jnp.dot(a, b, preferred_element_type=F32)


def silu(a):
    half = 0.5 * a
    return half + half * jnp.tanh(half)


def spread(parts, width, target):
    rows = iota((parts * 128, width), 0) & 127
    return (rows == target(iota((parts * 128, width), 1))).astype(F32).astype(BF16)


def pad_lanes(first, second):
    rows = first.shape[0]
    return jnp.concatenate([first, second, jnp.zeros((rows, 128 - 2 * HEADS), F32)], axis=1)


def kernel(
    tokens,
    x_weight,
    z_weight,
    bc_weight,
    dt_weight_hbm,
    conv_weight_hbm,
    conv_bias_hbm,
    dt_bias_hbm,
    decay_rate_hbm,
    skip_gain_hbm,
    norm_gain_hbm,
    out_weight,
    out,
    dt_weight,
    conv_weight,
    conv_bias,
    dt_bias,
    decay_rate,
    skip_gain,
    norm_gain,
    w_in,
    w_z,
    w_out,
    tok,
    xbc,
    conv_f,
    conv_b,
    b_turned,
    gate,
    y,
    scores,
    columns,
    q_rows,
    fac,
    ep,
    skip_rows,
    expand,
    heads,
    grow,
    st,
    part_out,
    part_in,
    local,
    coef,
    coef_t,
    slab_out,
    slab_in,
    ent_out,
    ent_in,
    ent,
    log_mine,
    log_in,
    log_chip,
    log_chips,
    log_slab,
    log_slabs,
    mix,
    w_sem,
    tok_sem,
    tok_send,
    edge_send,
    log_send,
    log_recv,
    logc_send,
    logc_recv,
    logt_send,
    logt_recv,
    pair_send,
    pair_recv,
    part_send,
    part_recv,
    slab_send,
    slab_recv,
    ent_send,
    ent_recv,
    epair_send,
    epair_recv,
    out_send,
    out_sem,
):
    tm = lax.axis_index("tm")
    s = lax.axis_index("space")
    slab = tm // 2
    c = tm % 2
    u = 2 * s + c
    far, at = 1 - s // 4, s % 4

    def peer(d):
        half = jnp.where(d <= 4, far, 1 - far)
        return 4 * half + lax.rem(at + jnp.where(d <= 4, d - 1, d - 4), 4)

    corner_hi = jnp.logical_and(s == GROUP - 1, c == 1)
    corner_lo = jnp.logical_and(s == 0, c == 0)

    loads = [
        pltpu.make_async_copy(bc_weight, w_in.at[:, pl.ds(INNER, 2 * STATE)], w_sem.at[0]),
        pltpu.make_async_copy(x_weight, w_in.at[:, pl.ds(0, INNER)], w_sem.at[1]),
        pltpu.make_async_copy(z_weight, w_z, w_sem.at[2]),
        pltpu.make_async_copy(out_weight, w_out, w_sem.at[3]),
    ]
    small = [
        pltpu.make_async_copy(source, target, w_sem.at[4 + at])
        for at, (source, target) in enumerate(
            (
                (skip_gain_hbm, skip_gain),
                (dt_weight_hbm, dt_weight),
                (dt_bias_hbm, dt_bias),
                (decay_rate_hbm, decay_rate),
                (conv_weight_hbm, conv_weight),
                (conv_bias_hbm, conv_bias),
                (norm_gain_hbm, norm_gain),
            )
        )
    ]
    for load in small + loads:
        load.start()

    barrier = pltpu.get_barrier_semaphore()

    def greet(d, _):
        v = lax.rem(u + d, 16)
        pl.semaphore_signal(barrier, inc=1, device_id=(2 * slab + v % 2, v // 2), device_id_type=MESH)
        return 0

    lax.fori_loop(1, 16, greet, 0)

    def greet_slab(d, _):
        t = lax.rem(slab + d, GROUP)
        pl.semaphore_signal(barrier, inc=1, device_id=(2 * t + c, s), device_id_type=MESH)
        return 0

    lax.fori_loop(1, GROUP, greet_slab, 0)
    above = lax.rem(slab + 1, GROUP)
    below = lax.rem(slab + GROUP - 1, GROUP)

    @pl.when(corner_hi)
    def _():
        pl.semaphore_signal(barrier, inc=1, device_id=(2 * above, 0), device_id_type=MESH)

    @pl.when(corner_lo)
    def _():
        pl.semaphore_signal(
            barrier, inc=1, device_id=(2 * below + 1, GROUP - 1), device_id_type=MESH
        )

    half_target = lambda l: (l >> 6) + jnp.where(l < HALF, 12 * c, HEADS - 12 + 12 * c)
    expand[...] = spread(3, INNER, half_target)
    for e in range(2):
        heads[e] = spread(3, INNER, lambda l: HEADS * e + (l >> 6))
    pl.semaphore_wait(barrier, 22 + jnp.logical_or(corner_hi, corner_lo).astype(jnp.int32))

    def send_tokens(j, action):
        ds, dc = 4 * c + j // 2, j % 2
        mine = jnp.logical_and(ds == s, dc == c)
        src, dst = tokens.at[j], tok.at[pl.ds(pl.multiple_of(EDGE + 32 * s, 16), 32)]

        @pl.when(jnp.logical_not(mine))
        def _():
            action(
                pltpu.make_async_remote_copy(
                    src, dst, tok_send.at[j], tok_sem, (2 * slab + dc, ds), MESH
                )
            )

        if action is started:

            @pl.when(mine)
            def _():
                pltpu.make_async_copy(src, dst, tok_sem).start()

    def send_edge(j, action, side):
        g = 8 * c + j + (1 if side == 0 else -1)
        ds, dc = lax.rem(g + 16, 16) // 2, lax.rem(g + 16, 16) % 2
        dt = lax.rem(slab + lax.div(g + 16, 16) - 1 + GROUP, GROUP)
        mine = jnp.logical_and(jnp.logical_and(ds == s, dc == c), dt == slab)
        src = tokens.at[j, pl.ds(16 if side == 0 else 0, EDGE)]
        dst = tok.at[pl.ds(0 if side == 0 else EDGE + PATCH, EDGE)]

        @pl.when(jnp.logical_not(mine))
        def _():
            action(
                pltpu.make_async_remote_copy(
                    src, dst, edge_send.at[side, j], tok_sem, (2 * dt + dc, ds), MESH
                )
            )

        if action is started:

            @pl.when(mine)
            def _():
                pltpu.make_async_copy(src, dst, tok_sem).start()

    def started(copy):
        copy.start()

    def left(copy):
        copy.wait_send()

    def all_tokens(action):
        def one(i, _):
            send_tokens(lax.rem(s + i, 8), action)
            return 0

        lax.fori_loop(0, 8, one, 0)

        @pl.when(s == GROUP - 1)
        def _():
            def one(j, _):
                send_edge(j, action, 0)
                return 0

            lax.fori_loop(0, 8, one, 0)

        @pl.when(s == 0)
        def _():
            def one(j, _):
                send_edge(j, action, 1)
                return 0

            lax.fori_loop(0, 8, one, 0)

    all_tokens(started)

    for load in small:
        load.wait()
    skips = pad_lanes(skip_gain[0:1, :], skip_gain[1:2, :])
    for e in range(2):
        skip_rows[e : e + 1, :] = dot(split(jnp.broadcast_to(skips, (8, 128)), 3), heads[e])[0:1, :]

    pltpu.make_async_copy(tok, tok, tok_sem).wait()

    @pl.when(jnp.logical_and(corner_lo, slab == 0))
    def _():
        tok[0:EDGE, :] = jnp.zeros((EDGE, D), BF16)

    @pl.when(jnp.logical_and(corner_hi, slab == GROUP - 1))
    def _():
        tok[EDGE + PATCH :, :] = jnp.zeros((EDGE, D), BF16)

    dt_raw = lax.dot_general(
        tok[EDGE : EDGE + PATCH, :],
        dt_weight[...],
        (((1,), (1,)), ((), ())),
        preferred_element_type=F32,
    )
    step = jax.nn.softplus(
        pad_lanes(dt_raw, dt_raw) + pad_lanes(dt_bias[0:1, :], dt_bias[1:2, :])
    )
    rates = pad_lanes(decay_rate[0:1, :], decay_rate[1:2, :])
    rate_step = split(step * (rates * -LOG2E), 3)
    row, col = iota((PATCH, PATCH), 0), iota((PATCH, PATCH), 1)
    down = dot((row >= col).astype(F32).astype(BF16), rate_step)
    up = dot((row <= col).astype(F32).astype(BF16), rate_step)
    down = down[:, 0:128] + (down[:, 128:256] + down[:, 256:384])
    up = up[:, 0:128] + (up[:, 128:256] + up[:, 256:384])
    lane = iota((PATCH, 128), 1)
    prefix = jnp.where(lane < HEADS, down, up)
    total = jnp.where(lane[0:1] < HEADS, down[PATCH - 1 :, :], up[0:1, :])
    log_mine[...] = jnp.broadcast_to(total, (8, 128))
    log_in[c] = log_mine[...]

    def log_copy():
        return pltpu.make_async_remote_copy(
            log_mine, log_in.at[c], log_send, log_recv, (2 * slab + 1 - c, s), MESH
        )

    log_copy().start()

    columns[...] = split(prefix, 3)
    fac[...] = split(jnp.exp2(total - prefix) * step, 2)
    ep[...] = split(jnp.exp2(prefix), 2)
    q_rows[...] = (prefix - LOG2E * jnp.log(step)).T

    def convolved(offset, turn):
        span = pl.ds(offset, CHUNK)
        xbc[turn] = dot(tok[...], w_in[:, span]).astype(BF16).astype(F32)
        forward = conv_bias[0:1, span]
        backward = conv_bias[1:2, span]
        for k in range(4):
            forward = forward + conv_weight[0, k : k + 1, span] * xbc[turn, pl.ds(EDGE - 3 + k, PATCH), :]
            backward = (
                backward + conv_weight[1, k : k + 1, span] * xbc[turn, pl.ds(EDGE + 3 - k, PATCH), :]
            )
        forward, backward = silu(forward).astype(BF16), silu(backward).astype(BF16)
        conv_f[:, span] = forward
        conv_b[:, span] = backward
        return forward, backward

    loads[0].wait()
    both = convolved(INNER, 6)
    for e in range(2):
        b_turned[e] = both[e][:, 0:STATE].astype(F32).T.astype(BF16)
    loads[1].wait()

    def pair_copy():
        return pltpu.make_async_remote_copy(
            st.at[2], st.at[c], pair_send, pair_recv, (2 * slab + 1 - c, s), MESH
        )

    def project(i):
        t = lax.rem((1 - c) * 3 + i, 6)
        x_f, x_b = convolved(pl.multiple_of(t * CHUNK, CHUNK), i)
        slot = jnp.where(t // 3 == c, c, 2)
        place = pl.ds(pl.multiple_of((t % 3) * CHUNK, CHUNK), CHUNK)
        for e, x in ((0, x_f), (1, x_b)):
            factor = dot(fac[...], heads[e, 0:256, pl.ds(pl.multiple_of(t * CHUNK, CHUNK), CHUNK)])
            scaled = (x.astype(F32) * factor).astype(BF16)
            st[slot, e, :, place] = dot(b_turned[e], scaled)

    for i in range(3):
        project(i)
    pair_copy().start()
    for i in range(3, 6):
        project(i)

    log_copy().wait_recv()
    pair_logs = [log_in[0][0:1, :], log_in[1][0:1, :]]
    chip_log = pair_logs[0] + pair_logs[1]
    log_chip[...] = jnp.broadcast_to(chip_log, (8, 128))
    log_chips[s] = log_chip[...]

    def chip_log_copy(k, source):
        return pltpu.make_async_remote_copy(
            log_chip, log_chips.at[source], logc_send.at[k], logc_recv.at[source], (tm, k), MESH
        )

    def send_chip_logs(d, _):
        chip_log_copy(lax.rem(s + d, GROUP), s).start()
        return 0

    lax.fori_loop(1, GROUP, send_chip_logs, 0)
    coef[16:24, :] = dot(
        split(jnp.exp2(jnp.concatenate(pair_logs + [jnp.zeros((6, 128), F32)], axis=0)), 3),
        expand[...],
    )

    pair_copy().wait_recv()
    d0, d1 = coef[16:17, :], coef[17:18, :]

    def part_copy(k, source):
        return pltpu.make_async_remote_copy(
            part_out.at[k],
            part_in.at[source],
            part_send.at[k],
            part_recv.at[source],
            (tm, k),
            MESH,
        )

    def combined(k):
        rows = pl.ds(pl.multiple_of(k * 16, 16), 16)
        return jnp.concatenate(
            [
                d1[:, :HALF] * st[0, 0, rows, :] + st[1, 0, rows, :],
                d0[:, HALF:] * st[1, 1, rows, :] + st[0, 1, rows, :],
            ],
            axis=1,
        ).astype(BF16)

    def send_part(d, _):
        k = peer(d)
        part_out[k] = combined(k)
        part_copy(k, s).start()
        return 0

    lax.fori_loop(1, GROUP, send_part, 0)

    part_in[s] = combined(s)

    for e, conv in ((0, conv_f), (1, conv_b)):
        scores[e] = lax.dot_general(
            conv[:, INNER + STATE :],
            conv[:, INNER : INNER + STATE],
            (((1,), (1,)), ((), ())),
            preferred_element_type=F32,
        )
    lower = iota((128, 128), 0) >= iota((128, 128), 1)
    upper = iota((128, 128), 0) <= iota((128, 128), 1)
    near = [
        (iota((1, 128), 1) < 64).astype(F32).astype(BF16),
        (iota((1, 128), 1) >= 64).astype(F32).astype(BF16),
    ]

    def weigh(e, i, j, column, line, mask):
        gap = column[128 * i : 128 * i + 128, :] - line[:, 128 * j : 128 * j + 128]
        if mask is not None:
            gap = jnp.where(mask, gap, -jnp.inf)
        return (
            scores[e, 128 * i : 128 * i + 128, 128 * j : 128 * j + 128] * jnp.exp2(gap)
        ).astype(BF16)

    def within(t, _):
        span = pl.ds(pl.multiple_of(t * 128, 128), 128)
        x_f, x_b = conv_f[:, span], conv_b[:, span]
        wide = dot(
            columns[...],
            spread(3, 512, lambda l: 2 * t + ((l >> 7) & 1) + jnp.where(l < 256, 0, HEADS)),
        )
        tops, bottoms, top_x, bottom_x = [], [], [], []
        for h in range(2):
            pf, pb = wide[:, 128 * h : 128 * h + 128], wide[:, 256 + 128 * h : 384 + 128 * h]
            qf, qb = q_rows[pl.ds(2 * t + h, 1), :], q_rows[pl.ds(HEADS + 2 * t + h, 1), :]
            tops += [
                weigh(0, 0, 0, pf, qf, lower),
                weigh(1, 0, 0, pb, qb, upper),
                weigh(1, 0, 1, pb, qb, None),
            ]
            bottoms += [
                weigh(0, 1, 0, pf, qf, None),
                weigh(0, 1, 1, pf, qf, lower),
                weigh(1, 1, 1, pb, qb, upper),
            ]
            xf, xb = x_f * near[h], x_b * near[h]
            top_x += [xf[0:128], xb]
            bottom_x += [xf, xb[128:256]]
        skip = skip_rows[0:1, span] * x_f.astype(F32) + skip_rows[1:2, span] * x_b.astype(F32)
        y[0:128, span] = skip[0:128] + dot(jnp.concatenate(tops, axis=1), jnp.concatenate(top_x, axis=0))
        y[128:256, span] = skip[128:256] + dot(jnp.concatenate(bottoms, axis=1), jnp.concatenate(bottom_x, axis=0))
        return 0

    def gate_columns(t, _):
        span = pl.ds(pl.multiple_of(t * CHUNK, CHUNK), CHUNK)
        gate[:, span] = silu(dot(tok[EDGE : EDGE + PATCH, :], w_z[:, span]))
        for e in range(2):
            grow[e, :, span] = dot(ep[...], heads[e, 0:256, span])
        return 0

    loads[2].wait()
    lax.fori_loop(0, 3, gate_columns, 0)

    def wait_chip_logs(d, _):
        k = lax.rem(s + d, GROUP)
        chip_log_copy(k, k).wait_recv()
        return 0

    lax.fori_loop(1, GROUP, wait_chip_logs, 0)
    chips = [log_chips[k][0:1, :] for k in range(GROUP)]
    zero = jnp.zeros((1, 128), F32)
    before, after = [zero], [zero]
    for k in range(GROUP):
        before.append(before[-1] + chips[k])
        after.append(after[-1] + chips[GROUP - 1 - k])
    narrow = iota((1, 128), 1) < HEADS
    outside = [jnp.where(narrow, before[k], after[GROUP - 1 - k]) for k in range(GROUP)]
    log_slab[...] = jnp.broadcast_to(before[GROUP], (8, 128))
    log_slabs[slab] = log_slab[...]

    def slab_log_copy(t, source):
        return pltpu.make_async_remote_copy(
            log_slab,
            log_slabs.at[source],
            logt_send.at[t],
            logt_recv.at[source],
            (2 * t + c, s),
            MESH,
        )

    def send_slab_logs(d, _):
        slab_log_copy(lax.rem(slab + d, GROUP), slab).start()
        return 0

    lax.fori_loop(1, GROUP, send_slab_logs, 0)
    lax.fori_loop(3, 6, gate_columns, 0)
    coef[0:16, :] = dot(
        split(jnp.exp2(jnp.concatenate(chips + outside, axis=0)), 3), expand[...]
    )

    def wait_part(d, _):
        k = lax.rem(s + d, GROUP)
        part_copy(k, k).wait_recv()
        return 0

    lax.fori_loop(1, GROUP, wait_part, 0)
    forward = jnp.zeros((16, HALF), F32)
    backward = jnp.zeros((16, HALF), F32)
    for k in range(GROUP):
        r = GROUP - 1 - k
        local[k, :, :HALF] = forward
        local[r, :, HALF:] = backward
        forward = coef[k : k + 1, :HALF] * forward + part_in[k, :, :HALF].astype(F32)
        backward = coef[r : r + 1, HALF:] * backward + part_in[r, :, HALF:].astype(F32)
    slab_out[0] = forward.astype(BF16)
    slab_out[1] = backward.astype(BF16)

    def slab_copy(t, source):
        return pltpu.make_async_remote_copy(
            slab_out.at[(t < slab).astype(jnp.int32)],
            slab_in.at[source],
            slab_send.at[t],
            slab_recv.at[source],
            (2 * t + c, s),
            MESH,
        )

    def send_slab(d, _):
        slab_copy(lax.rem(slab + d, GROUP), slab).start()
        return 0

    lax.fori_loop(1, GROUP, send_slab, 0)
    slab_in[slab] = slab_out[0]

    lax.fori_loop(0, 5, within, 0)

    def wait_slab_logs(d, _):
        t = lax.rem(slab + d, GROUP)
        slab_log_copy(t, t).wait_recv()
        return 0

    lax.fori_loop(1, GROUP, wait_slab_logs, 0)
    table = jnp.concatenate([log_slabs[t][0:1, :] for t in range(GROUP)], axis=0)
    coef_t[...] = dot(split(jnp.exp2(table), 3), expand[...])

    def wait_slab(d, _):
        t = lax.rem(slab + d, GROUP)
        slab_copy(t, t).wait_recv()
        return 0

    lax.fori_loop(1, GROUP, wait_slab, 0)
    forward = jnp.zeros((16, HALF), F32)
    backward = jnp.zeros((16, HALF), F32)
    for k in range(GROUP):
        r = GROUP - 1 - k
        forward = jnp.where(
            k < slab, coef_t[k : k + 1, :HALF] * forward + slab_in[k].astype(F32), forward
        )
        backward = jnp.where(
            r > slab, coef_t[r : r + 1, HALF:] * backward + slab_in[r].astype(F32), backward
        )
    come = jnp.concatenate([forward, backward], axis=1)

    def ent_copy(k, source):
        return pltpu.make_async_remote_copy(
            ent_out.at[k], ent_in.at[source], ent_send.at[k], ent_recv.at[source], (tm, k), MESH
        )

    def entering(k):
        return (local[k] + coef[pl.ds(GROUP + k, 1), :] * come).astype(BF16)

    def send_ent(d, _):
        k = peer(d)
        ent_out[k] = entering(k)
        ent_copy(k, s).start()
        return 0

    lax.fori_loop(1, GROUP, send_ent, 0)
    ent_in[s] = entering(s)

    lax.fori_loop(5, 12, within, 0)

    def wait_ent(d, _):
        k = lax.rem(s + d, GROUP)
        ent_copy(k, k).wait_recv()
        return 0

    lax.fori_loop(1, GROUP, wait_ent, 0)
    for k in range(GROUP):
        rows = slice(16 * k, 16 * k + 16)
        first, last = ent_in[k, :, :HALF], ent_in[k, :, HALF:]
        ent[0, 0, rows, :] = first
        ent[1, 1, rows, :] = last
        ent[1, 0, rows, :] = (d0[:, :HALF] * first.astype(F32) + st[0, 0, rows, :]).astype(BF16)
        ent[0, 1, rows, :] = (d1[:, HALF:] * last.astype(F32) + st[1, 1, rows, :]).astype(BF16)
    ent_pair = pltpu.make_async_remote_copy(
        ent.at[1 - c], ent.at[2], epair_send, epair_recv, (2 * slab + 1 - c, s), MESH
    )
    ent_pair.start()

    core_home = s // 4
    slot_home = u - 8 * core_home

    def send_out(b, action):
        mine = jnp.logical_and(b == s, core_home == c)
        src, dst = mix.at[pl.ds(pl.multiple_of(32 * b, 32), 32)], out.at[slot_home]

        @pl.when(jnp.logical_not(mine))
        def _():
            action(
                pltpu.make_async_remote_copy(
                    src, dst, out_send.at[b], out_sem, (2 * slab + core_home, b), MESH
                )
            )

        if action is started:

            @pl.when(mine)
            def _():
                pltpu.make_async_copy(src, dst, out_sem).start()

    def finish(i, rows, squares):
        t = lax.rem(c * 3 + i, 6)
        span = pl.ds(pl.multiple_of(t * CHUNK, CHUNK), CHUNK)
        slot = jnp.where(t // 3 == c, c, 2)
        place = pl.ds(pl.multiple_of((t % 3) * CHUNK, CHUNK), CHUNK)
        total = y[rows, span]
        for e, conv in ((0, conv_f), (1, conv_b)):
            total = total + grow[e, rows, span] * dot(
                conv[rows, INNER + STATE :], ent[slot, e, :, place]
            )
        gated = total * gate[rows, span]
        y[rows, span] = gated
        return squares + jnp.sum(gated * gated, axis=1, keepdims=True)

    gains = norm_gain[...].reshape(1, INNER)
    for turn in range(2):
        half = far if turn == 0 else 1 - far
        rows = pl.ds(pl.multiple_of(128 * half, 128), 128)
        squares = jnp.zeros((128, 1), F32)
        for i in range(3):
            squares = finish(i, rows, squares)
        if turn == 0:
            ent_pair.wait_recv()
        for i in range(3, 6):
            squares = finish(i, rows, squares)
        scale = lax.rsqrt(squares * (1.0 / INNER) + 1e-05)
        if turn == 0:
            loads[3].wait()
        normed = (y[rows, :] * scale * gains).astype(BF16)
        mix[rows, :] = dot(normed, w_out[...]).astype(BF16)
        for i in range(4):
            send_out(4 * half + lax.rem(s + i, 4), started)

    all_tokens(left)
    pair_copy().wait_send()
    ent_pair.wait_send()

    log_copy().wait_send()

    def wait_sent_group(d, _):
        k = lax.rem(s + d, GROUP)
        part_copy(k, s).wait_send()
        ent_copy(k, s).wait_send()
        chip_log_copy(k, s).wait_send()
        t = lax.rem(slab + d, GROUP)
        slab_log_copy(t, slab).wait_send()
        slab_copy(t, slab).wait_send()
        return 0

    lax.fori_loop(1, GROUP, wait_sent_group, 0)
    for b in range(8):
        send_out(b, left)
    pltpu.make_async_copy(out, out, out_sem).wait()


def body(*args):
    args = args[:4] + (args[4].T,) + args[5:]
    hbm = pl.BlockSpec(memory_space=pl.ANY)
    dma = pltpu.SemaphoreType.DMA
    scratch = [
        pltpu.VMEM((HEADS, D), BF16),
        pltpu.VMEM((2, 4, WIDE), F32),
        pltpu.VMEM((2, WIDE), F32),
        pltpu.VMEM((2, HEADS), F32),
        pltpu.VMEM((2, HEADS), F32),
        pltpu.VMEM((2, HEADS), F32),
        pltpu.VMEM((INNER,), F32),
        pltpu.VMEM((D, WIDE), BF16),
        pltpu.VMEM((D, INNER), BF16),
        pltpu.VMEM((INNER, D), BF16),
        pltpu.VMEM((PATCH + 2 * EDGE, D), BF16),
        pltpu.VMEM((7, PATCH + 2 * EDGE, CHUNK), F32),
        pltpu.VMEM((PATCH, WIDE), BF16),
        pltpu.VMEM((PATCH, WIDE), BF16),
        pltpu.VMEM((2, STATE, PATCH), BF16),
        pltpu.VMEM((PATCH, INNER), F32),
        pltpu.VMEM((PATCH, INNER), F32),
        pltpu.VMEM((2, PATCH, PATCH), F32),
        pltpu.VMEM((PATCH, 384), BF16),
        pltpu.VMEM((128, PATCH), F32),
        pltpu.VMEM((PATCH, 256), BF16),
        pltpu.VMEM((PATCH, 256), BF16),
        pltpu.VMEM((8, INNER), F32),
        pltpu.VMEM((384, INNER), BF16),
        pltpu.VMEM((2, 384, INNER), BF16),
        pltpu.VMEM((2, PATCH, INNER), F32),
        pltpu.VMEM((3, 2, STATE, HALF), F32),
        pltpu.VMEM((GROUP, 16, INNER), BF16),
        pltpu.VMEM((GROUP, 16, INNER), BF16),
        pltpu.VMEM((GROUP, 16, INNER), F32),
        pltpu.VMEM((24, INNER), F32),
        pltpu.VMEM((GROUP, INNER), F32),
        pltpu.VMEM((2, 16, HALF), BF16),
        pltpu.VMEM((GROUP, 16, HALF), BF16),
        pltpu.VMEM((GROUP, 16, INNER), BF16),
        pltpu.VMEM((GROUP, 16, INNER), BF16),
        pltpu.VMEM((3, 2, STATE, HALF), BF16),
        pltpu.VMEM((8, 128), F32),
        pltpu.VMEM((2, 8, 128), F32),
        pltpu.VMEM((8, 128), F32),
        pltpu.VMEM((GROUP, 8, 128), F32),
        pltpu.VMEM((8, 128), F32),
        pltpu.VMEM((GROUP, 8, 128), F32),
        pltpu.VMEM((PATCH, D), BF16),
        dma((11,)),
        dma,
        dma((8,)),
        dma((2, 8)),
        dma,
        dma,
        dma((GROUP,)),
        dma((GROUP,)),
        dma((GROUP,)),
        dma((GROUP,)),
        dma,
        dma,
        dma((GROUP,)),
        dma((GROUP,)),
        dma((GROUP,)),
        dma((GROUP,)),
        dma((GROUP,)),
        dma((GROUP,)),
        dma,
        dma,
        dma((8,)),
        dma,
    ]
    return pl.pallas_call(
        kernel,
        out_shape=jax.ShapeDtypeStruct((8, 32, D), BF16),
        in_specs=[hbm] * 12,
        out_specs=hbm,
        scratch_shapes=scratch,
        compiler_params=pltpu.CompilerParams(
            collective_id=0, has_side_effects=True, vmem_limit_bytes=60 * 1024 * 1024
        ),
    )(*args)


def solution(mesh):
    return jax.shard_map(
        body,
        mesh=mesh,
        in_specs=(P("tm", "space", None),) + (P(),) * 11,
        out_specs=P("tm", "space", None),
        check_vma=False,
    )
```

```python
import jax
import jax.numpy as jnp
from jax import lax
from jax.experimental import pallas as pl
from jax.experimental.pallas import tpu as pltpu
from jax.sharding import PartitionSpec as P

HEADS = 24
STATE = 128
PATCH = 256
D = 768
INNER = 1536
WIDE = INNER + 2 * STATE
HALF = INNER // 2
GROUP = 8
EDGE = 16
CHUNK = 256
LOG2E = 1.4426950408889634
F32, BF16 = jnp.float32, jnp.bfloat16
MESH = pl.DeviceIdType.MESH


def iota(shape, dim):
    return lax.broadcasted_iota(jnp.int32, shape, dim)


def split(a, parts):
    pieces = []
    for _ in range(parts):
        piece = a.astype(BF16)
        pieces.append(piece)
        a = a - piece.astype(F32)
    return jnp.concatenate(pieces, axis=1)


def dot(a, b):
    return jnp.dot(a, b, preferred_element_type=F32)


def silu(a):
    half = 0.5 * a
    return half + half * jnp.tanh(half)


def spread(parts, width, target):
    rows = iota((parts * 128, width), 0) & 127
    return (rows == target(iota((parts * 128, width), 1))).astype(F32).astype(BF16)


def pad_lanes(first, second):
    rows = first.shape[0]
    return jnp.concatenate([first, second, jnp.zeros((rows, 128 - 2 * HEADS), F32)], axis=1)


def kernel(
    tokens_hbm,
    x_weight,
    z_weight,
    bc_weight,
    dt_weight_hbm,
    conv_weight_hbm,
    conv_bias_hbm,
    dt_bias_hbm,
    decay_rate_hbm,
    skip_gain_hbm,
    norm_gain_hbm,
    out_weight,
    out,
    tokens,
    dt_weight,
    conv_weight,
    conv_bias,
    dt_bias,
    decay_rate,
    skip_gain,
    norm_gain,
    w_in,
    w_z,
    w_out,
    tok,
    xbc,
    conv_f,
    conv_b,
    b_turned,
    gate,
    y,
    scores,
    columns,
    q_rows,
    fac,
    ep,
    skip_rows,
    expand,
    heads,
    grow,
    st,
    part_out,
    part_in,
    local,
    coef,
    coef_t,
    slab_out,
    slab_in,
    ent_out,
    ent_in,
    ent,
    log_mine,
    log_in,
    log_chip,
    log_chips,
    log_slab,
    log_slabs,
    mix,
    w_sem,
    tok_sem,
    tok_send,
    edge_send,
    log_send,
    log_recv,
    logc_send,
    logc_recv,
    logt_send,
    logt_recv,
    pair_send,
    pair_recv,
    part_send,
    part_recv,
    slab_send,
    slab_recv,
    ent_send,
    ent_recv,
    epair_send,
    epair_recv,
    out_send,
    out_sem,
):
    tm = lax.axis_index("tm")
    s = lax.axis_index("space")
    slab = tm // 2
    c = tm % 2
    u = 2 * s + c
    far, at = 1 - s // 4, s % 4

    def peer(d):
        half = jnp.where(d <= 4, far, 1 - far)
        return 4 * half + lax.rem(at + jnp.where(d <= 4, d - 1, d - 4), 4)

    corner_hi = jnp.logical_and(s == GROUP - 1, c == 1)
    corner_lo = jnp.logical_and(s == 0, c == 0)

    fetch = pltpu.make_async_copy(tokens_hbm, tokens, w_sem.at[11])
    fetch.start()
    loads = [
        pltpu.make_async_copy(bc_weight, w_in.at[:, pl.ds(INNER, 2 * STATE)], w_sem.at[0]),
        pltpu.make_async_copy(x_weight, w_in.at[:, pl.ds(0, INNER)], w_sem.at[1]),
        pltpu.make_async_copy(z_weight, w_z, w_sem.at[2]),
        pltpu.make_async_copy(out_weight, w_out, w_sem.at[3]),
    ]
    small = [
        pltpu.make_async_copy(source, target, w_sem.at[4 + at])
        for at, (source, target) in enumerate(
            (
                (skip_gain_hbm, skip_gain),
                (dt_weight_hbm, dt_weight),
                (dt_bias_hbm, dt_bias),
                (decay_rate_hbm, decay_rate),
                (conv_weight_hbm, conv_weight),
                (conv_bias_hbm, conv_bias),
                (norm_gain_hbm, norm_gain),
            )
        )
    ]
    for load in small + loads:
        load.start()

    barrier = pltpu.get_barrier_semaphore()

    def greet(d, _):
        v = lax.rem(u + d, 16)
        pl.semaphore_signal(barrier, inc=1, device_id=(2 * slab + v % 2, v // 2), device_id_type=MESH)
        return 0

    lax.fori_loop(1, 16, greet, 0)

    def greet_slab(d, _):
        t = lax.rem(slab + d, GROUP)
        pl.semaphore_signal(barrier, inc=1, device_id=(2 * t + c, s), device_id_type=MESH)
        return 0

    lax.fori_loop(1, GROUP, greet_slab, 0)
    above = lax.rem(slab + 1, GROUP)
    below = lax.rem(slab + GROUP - 1, GROUP)

    @pl.when(corner_hi)
    def _():
        pl.semaphore_signal(barrier, inc=1, device_id=(2 * above, 0), device_id_type=MESH)

    @pl.when(corner_lo)
    def _():
        pl.semaphore_signal(
            barrier, inc=1, device_id=(2 * below + 1, GROUP - 1), device_id_type=MESH
        )

    half_target = lambda l: (l >> 6) + jnp.where(l < HALF, 12 * c, HEADS - 12 + 12 * c)
    expand[...] = spread(3, INNER, half_target)
    for e in range(2):
        heads[e] = spread(3, INNER, lambda l: HEADS * e + (l >> 6))
    fetch.wait()
    pl.semaphore_wait(barrier, 22 + jnp.logical_or(corner_hi, corner_lo).astype(jnp.int32))

    def send_tokens(j, action):
        ds, dc = 4 * c + j // 2, j % 2
        mine = jnp.logical_and(ds == s, dc == c)
        src, dst = tokens.at[j], tok.at[pl.ds(pl.multiple_of(EDGE + 32 * s, 16), 32)]

        @pl.when(jnp.logical_not(mine))
        def _():
            action(
                pltpu.make_async_remote_copy(
                    src, dst, tok_send.at[j], tok_sem, (2 * slab + dc, ds), MESH
                )
            )

        if action is started:

            @pl.when(mine)
            def _():
                pltpu.make_async_copy(src, dst, tok_sem).start()

    def send_edge(j, action, side):
        g = 8 * c + j + (1 if side == 0 else -1)
        ds, dc = lax.rem(g + 16, 16) // 2, lax.rem(g + 16, 16) % 2
        dt = lax.rem(slab + lax.div(g + 16, 16) - 1 + GROUP, GROUP)
        mine = jnp.logical_and(jnp.logical_and(ds == s, dc == c), dt == slab)
        src = tokens.at[j, pl.ds(16 if side == 0 else 0, EDGE)]
        dst = tok.at[pl.ds(0 if side == 0 else EDGE + PATCH, EDGE)]

        @pl.when(jnp.logical_not(mine))
        def _():
            action(
                pltpu.make_async_remote_copy(
                    src, dst, edge_send.at[side, j], tok_sem, (2 * dt + dc, ds), MESH
                )
            )

        if action is started:

            @pl.when(mine)
            def _():
                pltpu.make_async_copy(src, dst, tok_sem).start()

    def started(copy):
        copy.start()

    def left(copy):
        copy.wait_send()

    def all_tokens(action):
        def one(i, _):
            send_tokens(lax.rem(s + i, 8), action)
            return 0

        lax.fori_loop(0, 8, one, 0)

        @pl.when(s == GROUP - 1)
        def _():
            def one(j, _):
                send_edge(j, action, 0)
                return 0

            lax.fori_loop(0, 8, one, 0)

        @pl.when(s == 0)
        def _():
            def one(j, _):
                send_edge(j, action, 1)
                return 0

            lax.fori_loop(0, 8, one, 0)

    all_tokens(started)

    for load in small:
        load.wait()
    skips = pad_lanes(skip_gain[0:1, :], skip_gain[1:2, :])
    for e in range(2):
        skip_rows[e : e + 1, :] = dot(split(jnp.broadcast_to(skips, (8, 128)), 3), heads[e])[0:1, :]

    loads[0].wait()
    loads[1].wait()
    pltpu.make_async_copy(tok, tok, tok_sem).wait()

    @pl.when(jnp.logical_and(corner_lo, slab == 0))
    def _():
        tok[0:EDGE, :] = jnp.zeros((EDGE, D), BF16)

    @pl.when(jnp.logical_and(corner_hi, slab == GROUP - 1))
    def _():
        tok[EDGE + PATCH :, :] = jnp.zeros((EDGE, D), BF16)

    def convolved(offset, turn):
        span = pl.ds(offset, CHUNK)
        xbc[turn] = dot(tok[...], w_in[:, span]).astype(BF16).astype(F32)
        forward = conv_bias[0:1, span]
        backward = conv_bias[1:2, span]
        for k in range(4):
            forward = forward + conv_weight[0, k : k + 1, span] * xbc[turn, pl.ds(EDGE - 3 + k, PATCH), :]
            backward = (
                backward + conv_weight[1, k : k + 1, span] * xbc[turn, pl.ds(EDGE + 3 - k, PATCH), :]
            )
        forward, backward = silu(forward).astype(BF16), silu(backward).astype(BF16)
        conv_f[:, span] = forward
        conv_b[:, span] = backward
        return forward, backward

    both = convolved(INNER, 6)
    for e in range(2):
        b_turned[e] = both[e][:, 0:STATE].astype(F32).T.astype(BF16)
    dt_raw = lax.dot_general(
        tok[EDGE : EDGE + PATCH, :],
        dt_weight[...],
        (((1,), (1,)), ((), ())),
        preferred_element_type=F32,
    )
    step = jax.nn.softplus(
        pad_lanes(dt_raw, dt_raw) + pad_lanes(dt_bias[0:1, :], dt_bias[1:2, :])
    )
    rates = pad_lanes(decay_rate[0:1, :], decay_rate[1:2, :])
    rate_step = split(step * (rates * -LOG2E), 3)
    row, col = iota((PATCH, PATCH), 0), iota((PATCH, PATCH), 1)
    down = dot((row >= col).astype(F32).astype(BF16), rate_step)
    up = dot((row <= col).astype(F32).astype(BF16), rate_step)
    down = down[:, 0:128] + (down[:, 128:256] + down[:, 256:384])
    up = up[:, 0:128] + (up[:, 128:256] + up[:, 256:384])
    lane = iota((PATCH, 128), 1)
    prefix = jnp.where(lane < HEADS, down, up)
    total = jnp.where(lane[0:1] < HEADS, down[PATCH - 1 :, :], up[0:1, :])
    log_mine[...] = jnp.broadcast_to(total, (8, 128))
    log_in[c] = log_mine[...]

    def log_copy():
        return pltpu.make_async_remote_copy(
            log_mine, log_in.at[c], log_send, log_recv, (2 * slab + 1 - c, s), MESH
        )

    log_copy().start()

    columns[...] = split(prefix, 3)
    fac[...] = split(jnp.exp2(total - prefix) * step, 2)
    ep[...] = split(jnp.exp2(prefix), 2)
    q_rows[...] = (prefix - LOG2E * jnp.log(step)).T

    def pair_copy():
        return pltpu.make_async_remote_copy(
            st.at[2], st.at[c], pair_send, pair_recv, (2 * slab + 1 - c, s), MESH
        )

    def project(i):
        t = lax.rem((1 - c) * 3 + i, 6)
        x_f, x_b = convolved(pl.multiple_of(t * CHUNK, CHUNK), i)
        slot = jnp.where(t // 3 == c, c, 2)
        place = pl.ds(pl.multiple_of((t % 3) * CHUNK, CHUNK), CHUNK)
        for e, x in ((0, x_f), (1, x_b)):
            factor = dot(fac[...], heads[e, 0:256, pl.ds(pl.multiple_of(t * CHUNK, CHUNK), CHUNK)])
            scaled = (x.astype(F32) * factor).astype(BF16)
            st[slot, e, :, place] = dot(b_turned[e], scaled)

    for i in range(3):
        project(i)
    pair_copy().start()
    for i in range(3, 6):
        project(i)

    log_copy().wait_recv()
    pair_logs = [log_in[0][0:1, :], log_in[1][0:1, :]]
    chip_log = pair_logs[0] + pair_logs[1]
    log_chip[...] = jnp.broadcast_to(chip_log, (8, 128))
    log_chips[s] = log_chip[...]

    def chip_log_copy(k, source):
        return pltpu.make_async_remote_copy(
            log_chip, log_chips.at[source], logc_send.at[k], logc_recv.at[source], (tm, k), MESH
        )

    def send_chip_logs(d, _):
        chip_log_copy(lax.rem(s + d, GROUP), s).start()
        return 0

    lax.fori_loop(1, GROUP, send_chip_logs, 0)
    coef[16:24, :] = dot(
        split(jnp.exp2(jnp.concatenate(pair_logs + [jnp.zeros((6, 128), F32)], axis=0)), 3),
        expand[...],
    )

    pair_copy().wait_recv()
    d0, d1 = coef[16:17, :], coef[17:18, :]

    def part_copy(k, source):
        return pltpu.make_async_remote_copy(
            part_out.at[k],
            part_in.at[source],
            part_send.at[k],
            part_recv.at[source],
            (tm, k),
            MESH,
        )

    def combined(k):
        rows = pl.ds(pl.multiple_of(k * 16, 16), 16)
        return jnp.concatenate(
            [
                d1[:, :HALF] * st[0, 0, rows, :] + st[1, 0, rows, :],
                d0[:, HALF:] * st[1, 1, rows, :] + st[0, 1, rows, :],
            ],
            axis=1,
        ).astype(BF16)

    def send_part(d, _):
        k = peer(d)
        part_out[k] = combined(k)
        part_copy(k, s).start()
        return 0

    lax.fori_loop(1, GROUP, send_part, 0)

    part_in[s] = combined(s)

    for e, conv in ((0, conv_f), (1, conv_b)):
        scores[e] = lax.dot_general(
            conv[:, INNER + STATE :],
            conv[:, INNER : INNER + STATE],
            (((1,), (1,)), ((), ())),
            preferred_element_type=F32,
        )
    lower = iota((128, 128), 0) >= iota((128, 128), 1)
    upper = iota((128, 128), 0) <= iota((128, 128), 1)
    near = [
        (iota((1, 128), 1) < 64).astype(F32).astype(BF16),
        (iota((1, 128), 1) >= 64).astype(F32).astype(BF16),
    ]

    def weigh(e, i, j, column, line, mask):
        gap = column[128 * i : 128 * i + 128, :] - line[:, 128 * j : 128 * j + 128]
        if mask is not None:
            gap = jnp.where(mask, gap, -jnp.inf)
        return (
            scores[e, 128 * i : 128 * i + 128, 128 * j : 128 * j + 128] * jnp.exp2(gap)
        ).astype(BF16)

    def within(t, _):
        span = pl.ds(pl.multiple_of(t * 128, 128), 128)
        x_f, x_b = conv_f[:, span], conv_b[:, span]
        wide = dot(
            columns[...],
            spread(3, 512, lambda l: 2 * t + ((l >> 7) & 1) + jnp.where(l < 256, 0, HEADS)),
        )
        tops, bottoms, top_x, bottom_x = [], [], [], []
        for h in range(2):
            pf, pb = wide[:, 128 * h : 128 * h + 128], wide[:, 256 + 128 * h : 384 + 128 * h]
            qf, qb = q_rows[pl.ds(2 * t + h, 1), :], q_rows[pl.ds(HEADS + 2 * t + h, 1), :]
            tops += [
                weigh(0, 0, 0, pf, qf, lower),
                weigh(1, 0, 0, pb, qb, upper),
                weigh(1, 0, 1, pb, qb, None),
            ]
            bottoms += [
                weigh(0, 1, 0, pf, qf, None),
                weigh(0, 1, 1, pf, qf, lower),
                weigh(1, 1, 1, pb, qb, upper),
            ]
            xf, xb = x_f * near[h], x_b * near[h]
            top_x += [xf[0:128], xb]
            bottom_x += [xf, xb[128:256]]
        skip = skip_rows[0:1, span] * x_f.astype(F32) + skip_rows[1:2, span] * x_b.astype(F32)
        y[0:128, span] = skip[0:128] + dot(jnp.concatenate(tops, axis=1), jnp.concatenate(top_x, axis=0))
        y[128:256, span] = skip[128:256] + dot(jnp.concatenate(bottoms, axis=1), jnp.concatenate(bottom_x, axis=0))
        return 0

    def gate_columns(t, _):
        span = pl.ds(pl.multiple_of(t * CHUNK, CHUNK), CHUNK)
        gate[:, span] = silu(dot(tok[EDGE : EDGE + PATCH, :], w_z[:, span]))
        for e in range(2):
            grow[e, :, span] = dot(ep[...], heads[e, 0:256, span])
        return 0

    loads[2].wait()
    lax.fori_loop(0, 3, gate_columns, 0)

    def wait_chip_logs(d, _):
        k = lax.rem(s + d, GROUP)
        chip_log_copy(k, k).wait_recv()
        return 0

    lax.fori_loop(1, GROUP, wait_chip_logs, 0)
    chips = [log_chips[k][0:1, :] for k in range(GROUP)]
    zero = jnp.zeros((1, 128), F32)
    before, after = [zero], [zero]
    for k in range(GROUP):
        before.append(before[-1] + chips[k])
        after.append(after[-1] + chips[GROUP - 1 - k])
    narrow = iota((1, 128), 1) < HEADS
    outside = [jnp.where(narrow, before[k], after[GROUP - 1 - k]) for k in range(GROUP)]
    log_slab[...] = jnp.broadcast_to(before[GROUP], (8, 128))
    log_slabs[slab] = log_slab[...]

    def slab_log_copy(t, source):
        return pltpu.make_async_remote_copy(
            log_slab,
            log_slabs.at[source],
            logt_send.at[t],
            logt_recv.at[source],
            (2 * t + c, s),
            MESH,
        )

    def send_slab_logs(d, _):
        slab_log_copy(lax.rem(slab + d, GROUP), slab).start()
        return 0

    lax.fori_loop(1, GROUP, send_slab_logs, 0)
    lax.fori_loop(3, 6, gate_columns, 0)
    coef[0:16, :] = dot(
        split(jnp.exp2(jnp.concatenate(chips + outside, axis=0)), 3), expand[...]
    )

    def wait_part(d, _):
        k = lax.rem(s + d, GROUP)
        part_copy(k, k).wait_recv()
        return 0

    lax.fori_loop(1, GROUP, wait_part, 0)
    forward = jnp.zeros((16, HALF), F32)
    backward = jnp.zeros((16, HALF), F32)
    for k in range(GROUP):
        r = GROUP - 1 - k
        local[k, :, :HALF] = forward
        local[r, :, HALF:] = backward
        forward = coef[k : k + 1, :HALF] * forward + part_in[k, :, :HALF].astype(F32)
        backward = coef[r : r + 1, HALF:] * backward + part_in[r, :, HALF:].astype(F32)
    slab_out[0] = forward.astype(BF16)
    slab_out[1] = backward.astype(BF16)

    def slab_copy(t, source):
        return pltpu.make_async_remote_copy(
            slab_out.at[(t < slab).astype(jnp.int32)],
            slab_in.at[source],
            slab_send.at[t],
            slab_recv.at[source],
            (2 * t + c, s),
            MESH,
        )

    def send_slab(d, _):
        slab_copy(lax.rem(slab + d, GROUP), slab).start()
        return 0

    lax.fori_loop(1, GROUP, send_slab, 0)
    slab_in[slab] = slab_out[0]

    lax.fori_loop(0, 5, within, 0)

    def wait_slab_logs(d, _):
        t = lax.rem(slab + d, GROUP)
        slab_log_copy(t, t).wait_recv()
        return 0

    lax.fori_loop(1, GROUP, wait_slab_logs, 0)
    table = jnp.concatenate([log_slabs[t][0:1, :] for t in range(GROUP)], axis=0)
    coef_t[...] = dot(split(jnp.exp2(table), 3), expand[...])

    def wait_slab(d, _):
        t = lax.rem(slab + d, GROUP)
        slab_copy(t, t).wait_recv()
        return 0

    lax.fori_loop(1, GROUP, wait_slab, 0)
    forward = jnp.zeros((16, HALF), F32)
    backward = jnp.zeros((16, HALF), F32)
    for k in range(GROUP):
        r = GROUP - 1 - k
        forward = jnp.where(
            k < slab, coef_t[k : k + 1, :HALF] * forward + slab_in[k].astype(F32), forward
        )
        backward = jnp.where(
            r > slab, coef_t[r : r + 1, HALF:] * backward + slab_in[r].astype(F32), backward
        )
    come = jnp.concatenate([forward, backward], axis=1)

    def ent_copy(k, source):
        return pltpu.make_async_remote_copy(
            ent_out.at[k], ent_in.at[source], ent_send.at[k], ent_recv.at[source], (tm, k), MESH
        )

    def entering(k):
        return (local[k] + coef[pl.ds(GROUP + k, 1), :] * come).astype(BF16)

    def send_ent(d, _):
        k = peer(d)
        ent_out[k] = entering(k)
        ent_copy(k, s).start()
        return 0

    lax.fori_loop(1, GROUP, send_ent, 0)
    ent_in[s] = entering(s)

    lax.fori_loop(5, 12, within, 0)

    def wait_ent(d, _):
        k = lax.rem(s + d, GROUP)
        ent_copy(k, k).wait_recv()
        return 0

    lax.fori_loop(1, GROUP, wait_ent, 0)
    for k in range(GROUP):
        rows = slice(16 * k, 16 * k + 16)
        first, last = ent_in[k, :, :HALF], ent_in[k, :, HALF:]
        ent[0, 0, rows, :] = first
        ent[1, 1, rows, :] = last
        ent[1, 0, rows, :] = (d0[:, :HALF] * first.astype(F32) + st[0, 0, rows, :]).astype(BF16)
        ent[0, 1, rows, :] = (d1[:, HALF:] * last.astype(F32) + st[1, 1, rows, :]).astype(BF16)
    ent_pair = pltpu.make_async_remote_copy(
        ent.at[1 - c], ent.at[2], epair_send, epair_recv, (2 * slab + 1 - c, s), MESH
    )
    ent_pair.start()

    core_home = s // 4
    slot_home = u - 8 * core_home

    def send_out(b, action):
        mine = jnp.logical_and(b == s, core_home == c)
        src, dst = mix.at[pl.ds(pl.multiple_of(32 * b, 32), 32)], out.at[slot_home]

        @pl.when(jnp.logical_not(mine))
        def _():
            action(
                pltpu.make_async_remote_copy(
                    src, dst, out_send.at[b], out_sem, (2 * slab + core_home, b), MESH
                )
            )

        if action is started:

            @pl.when(mine)
            def _():
                pltpu.make_async_copy(src, dst, out_sem).start()

    def finish(i, rows, squares):
        t = lax.rem(c * 3 + i, 6)
        span = pl.ds(pl.multiple_of(t * CHUNK, CHUNK), CHUNK)
        slot = jnp.where(t // 3 == c, c, 2)
        place = pl.ds(pl.multiple_of((t % 3) * CHUNK, CHUNK), CHUNK)
        total = y[rows, span]
        for e, conv in ((0, conv_f), (1, conv_b)):
            total = total + grow[e, rows, span] * dot(
                conv[rows, INNER + STATE :], ent[slot, e, :, place]
            )
        gated = total * gate[rows, span]
        y[rows, span] = gated
        return squares + jnp.sum(gated * gated, axis=1, keepdims=True)

    gains = norm_gain[...].reshape(1, INNER)
    for turn in range(2):
        half = far if turn == 0 else 1 - far
        rows = pl.ds(pl.multiple_of(128 * half, 128), 128)
        squares = jnp.zeros((128, 1), F32)
        for i in range(3):
            squares = finish(i, rows, squares)
        if turn == 0:
            ent_pair.wait_recv()
        for i in range(3, 6):
            squares = finish(i, rows, squares)
        scale = lax.rsqrt(squares * (1.0 / INNER) + 1e-05)
        if turn == 0:
            loads[3].wait()
        normed = (y[rows, :] * scale * gains).astype(BF16)
        mix[rows, :] = dot(normed, w_out[...]).astype(BF16)
        for i in range(4):
            send_out(4 * half + lax.rem(s + i, 4), started)

    all_tokens(left)
    pair_copy().wait_send()
    ent_pair.wait_send()

    log_copy().wait_send()

    def wait_sent_group(d, _):
        k = lax.rem(s + d, GROUP)
        part_copy(k, s).wait_send()
        ent_copy(k, s).wait_send()
        chip_log_copy(k, s).wait_send()
        t = lax.rem(slab + d, GROUP)
        slab_log_copy(t, slab).wait_send()
        slab_copy(t, slab).wait_send()
        return 0

    lax.fori_loop(1, GROUP, wait_sent_group, 0)
    for b in range(8):
        send_out(b, left)
    pltpu.make_async_copy(out, out, out_sem).wait()


def body(*args):
    args = args[:4] + (args[4].T,) + args[5:]
    hbm = pl.BlockSpec(memory_space=pl.ANY)
    dma = pltpu.SemaphoreType.DMA
    scratch = [
        pltpu.VMEM((8, 32, D), BF16),
        pltpu.VMEM((HEADS, D), BF16),
        pltpu.VMEM((2, 4, WIDE), F32),
        pltpu.VMEM((2, WIDE), F32),
        pltpu.VMEM((2, HEADS), F32),
        pltpu.VMEM((2, HEADS), F32),
        pltpu.VMEM((2, HEADS), F32),
        pltpu.VMEM((INNER,), F32),
        pltpu.VMEM((D, WIDE), BF16),
        pltpu.VMEM((D, INNER), BF16),
        pltpu.VMEM((INNER, D), BF16),
        pltpu.VMEM((PATCH + 2 * EDGE, D), BF16),
        pltpu.VMEM((7, PATCH + 2 * EDGE, CHUNK), F32),
        pltpu.VMEM((PATCH, WIDE), BF16),
        pltpu.VMEM((PATCH, WIDE), BF16),
        pltpu.VMEM((2, STATE, PATCH), BF16),
        pltpu.VMEM((PATCH, INNER), F32),
        pltpu.VMEM((PATCH, INNER), F32),
        pltpu.VMEM((2, PATCH, PATCH), F32),
        pltpu.VMEM((PATCH, 384), BF16),
        pltpu.VMEM((128, PATCH), F32),
        pltpu.VMEM((PATCH, 256), BF16),
        pltpu.VMEM((PATCH, 256), BF16),
        pltpu.VMEM((8, INNER), F32),
        pltpu.VMEM((384, INNER), BF16),
        pltpu.VMEM((2, 384, INNER), BF16),
        pltpu.VMEM((2, PATCH, INNER), F32),
        pltpu.VMEM((3, 2, STATE, HALF), F32),
        pltpu.VMEM((GROUP, 16, INNER), BF16),
        pltpu.VMEM((GROUP, 16, INNER), BF16),
        pltpu.VMEM((GROUP, 16, INNER), F32),
        pltpu.VMEM((24, INNER), F32),
        pltpu.VMEM((GROUP, INNER), F32),
        pltpu.VMEM((2, 16, HALF), BF16),
        pltpu.VMEM((GROUP, 16, HALF), BF16),
        pltpu.VMEM((GROUP, 16, INNER), BF16),
        pltpu.VMEM((GROUP, 16, INNER), BF16),
        pltpu.VMEM((3, 2, STATE, HALF), BF16),
        pltpu.VMEM((8, 128), F32),
        pltpu.VMEM((2, 8, 128), F32),
        pltpu.VMEM((8, 128), F32),
        pltpu.VMEM((GROUP, 8, 128), F32),
        pltpu.VMEM((8, 128), F32),
        pltpu.VMEM((GROUP, 8, 128), F32),
        pltpu.VMEM((PATCH, D), BF16),
        dma((12,)),
        dma,
        dma((8,)),
        dma((2, 8)),
        dma,
        dma,
        dma((GROUP,)),
        dma((GROUP,)),
        dma((GROUP,)),
        dma((GROUP,)),
        dma,
        dma,
        dma((GROUP,)),
        dma((GROUP,)),
        dma((GROUP,)),
        dma((GROUP,)),
        dma((GROUP,)),
        dma((GROUP,)),
        dma,
        dma,
        dma((8,)),
        dma,
    ]
    return pl.pallas_call(
        kernel,
        out_shape=jax.ShapeDtypeStruct((8, 32, D), BF16),
        in_specs=[hbm] * 12,
        out_specs=hbm,
        scratch_shapes=scratch,
        compiler_params=pltpu.CompilerParams(
            collective_id=0, has_side_effects=True, vmem_limit_bytes=60 * 1024 * 1024
        ),
    )(*args)


def solution(mesh):
    return jax.shard_map(
        body,
        mesh=mesh,
        in_specs=(P("tm", "space", None),) + (P(),) * 11,
        out_specs=P("tm", "space", None),
        check_vma=False,
    )
```

```python
import jax
import jax.numpy as jnp
from jax import lax
from jax.experimental import pallas as pl
from jax.experimental.pallas import tpu as pltpu
from jax.sharding import PartitionSpec as P

HEADS = 24
STATE = 128
PATCH = 256
D = 768
INNER = 1536
WIDE = INNER + 2 * STATE
HALF = INNER // 2
GROUP = 8
EDGE = 16
CHUNK = 256
LOG2E = 1.4426950408889634
F32, BF16 = jnp.float32, jnp.bfloat16
MESH = pl.DeviceIdType.MESH


def iota(shape, dim):
    return lax.broadcasted_iota(jnp.int32, shape, dim)


def split(a, parts):
    pieces = []
    for _ in range(parts):
        piece = a.astype(BF16)
        pieces.append(piece)
        a = a - piece.astype(F32)
    return jnp.concatenate(pieces, axis=1)


def dot(a, b):
    return jnp.dot(a, b, preferred_element_type=F32)


def silu_of_half(half):
    return half + half * jnp.tanh(half)


def silu(a):
    return silu_of_half(0.5 * a)


def spread(parts, width, target):
    rows = iota((parts * 128, width), 0) & 127
    return (rows == target(iota((parts * 128, width), 1))).astype(F32).astype(BF16)


def pad_lanes(first, second):
    rows = first.shape[0]
    return jnp.concatenate([first, second, jnp.zeros((rows, 128 - 2 * HEADS), F32)], axis=1)


def kernel(
    tokens_hbm,
    x_weight,
    z_weight,
    bc_weight,
    dt_weight_hbm,
    conv_weight_hbm,
    conv_bias_hbm,
    dt_bias_hbm,
    decay_rate_hbm,
    skip_gain_hbm,
    norm_gain_hbm,
    out_weight,
    out,
    tokens,
    dt_weight,
    conv_weight,
    conv_bias,
    dt_bias,
    decay_rate,
    skip_gain,
    norm_gain,
    w_in,
    w_z,
    w_out,
    tok,
    conv_f,
    conv_b,
    b_turned,
    gate,
    y,
    scores,
    columns,
    q_rows,
    fac,
    ep,
    skip_rows,
    expand,
    heads,
    grow,
    st,
    part_out,
    part_in,
    local,
    coef,
    coef_t,
    slab_out,
    slab_in,
    ent_out,
    ent_in,
    ent,
    log_mine,
    log_in,
    log_chip,
    log_chips,
    log_slab,
    log_slabs,
    mix,
    w_sem,
    tok_sem,
    tok_send,
    edge_send,
    log_send,
    log_recv,
    logc_send,
    logc_recv,
    logt_send,
    logt_recv,
    pair_send,
    pair_recv,
    part_send,
    part_recv,
    slab_send,
    slab_recv,
    ent_send,
    ent_recv,
    epair_send,
    epair_recv,
    out_send,
    out_sem,
):
    tm = lax.axis_index("tm")
    s = lax.axis_index("space")
    slab = tm // 2
    c = tm % 2
    u = 2 * s + c
    far, at = 1 - s // 4, s % 4

    def peer(d):
        half = jnp.where(d <= 4, far, 1 - far)
        return 4 * half + lax.rem(at + jnp.where(d <= 4, d - 1, d - 4), 4)

    corner_hi = jnp.logical_and(s == GROUP - 1, c == 1)
    corner_lo = jnp.logical_and(s == 0, c == 0)

    fetch = pltpu.make_async_copy(tokens_hbm, tokens, w_sem.at[11])
    fetch.start()
    loads = [
        pltpu.make_async_copy(bc_weight, w_in.at[:, pl.ds(INNER, 2 * STATE)], w_sem.at[0]),
        pltpu.make_async_copy(x_weight, w_in.at[:, pl.ds(0, INNER)], w_sem.at[1]),
        pltpu.make_async_copy(z_weight, w_z, w_sem.at[2]),
        pltpu.make_async_copy(out_weight, w_out, w_sem.at[3]),
    ]
    small = [
        pltpu.make_async_copy(source, target, w_sem.at[4 + at])
        for at, (source, target) in enumerate(
            (
                (skip_gain_hbm, skip_gain),
                (dt_weight_hbm, dt_weight),
                (dt_bias_hbm, dt_bias),
                (decay_rate_hbm, decay_rate),
                (conv_weight_hbm, conv_weight),
                (conv_bias_hbm, conv_bias),
                (norm_gain_hbm, norm_gain),
            )
        )
    ]
    for load in small + loads:
        load.start()

    barrier = pltpu.get_barrier_semaphore()

    def greet(d, _):
        v = lax.rem(u + d, 16)
        pl.semaphore_signal(barrier, inc=1, device_id=(2 * slab + v % 2, v // 2), device_id_type=MESH)
        return 0

    lax.fori_loop(1, 16, greet, 0)

    def greet_slab(d, _):
        t = lax.rem(slab + d, GROUP)
        pl.semaphore_signal(barrier, inc=1, device_id=(2 * t + c, s), device_id_type=MESH)
        return 0

    lax.fori_loop(1, GROUP, greet_slab, 0)
    above = lax.rem(slab + 1, GROUP)
    below = lax.rem(slab + GROUP - 1, GROUP)

    @pl.when(corner_hi)
    def _():
        pl.semaphore_signal(barrier, inc=1, device_id=(2 * above, 0), device_id_type=MESH)

    @pl.when(corner_lo)
    def _():
        pl.semaphore_signal(
            barrier, inc=1, device_id=(2 * below + 1, GROUP - 1), device_id_type=MESH
        )

    half_target = lambda l: (l >> 6) + jnp.where(l < HALF, 12 * c, HEADS - 12 + 12 * c)
    expand[...] = spread(3, INNER, half_target)
    for e in range(2):
        heads[e] = spread(3, INNER, lambda l: HEADS * e + (l >> 6))
    fetch.wait()
    pl.semaphore_wait(barrier, 22 + jnp.logical_or(corner_hi, corner_lo).astype(jnp.int32))

    def send_tokens(j, action):
        ds, dc = 4 * c + j // 2, j % 2
        mine = jnp.logical_and(ds == s, dc == c)
        src, dst = tokens.at[j], tok.at[pl.ds(pl.multiple_of(EDGE + 32 * s, 16), 32)]

        @pl.when(jnp.logical_not(mine))
        def _():
            action(
                pltpu.make_async_remote_copy(
                    src, dst, tok_send.at[j], tok_sem, (2 * slab + dc, ds), MESH
                )
            )

        if action is started:

            @pl.when(mine)
            def _():
                pltpu.make_async_copy(src, dst, tok_sem).start()

    def send_edge(j, action, side):
        g = 8 * c + j + (1 if side == 0 else -1)
        ds, dc = lax.rem(g + 16, 16) // 2, lax.rem(g + 16, 16) % 2
        dt = lax.rem(slab + lax.div(g + 16, 16) - 1 + GROUP, GROUP)
        mine = jnp.logical_and(jnp.logical_and(ds == s, dc == c), dt == slab)
        src = tokens.at[j, pl.ds(16 if side == 0 else 0, EDGE)]
        dst = tok.at[pl.ds(0 if side == 0 else EDGE + PATCH, EDGE)]

        @pl.when(jnp.logical_not(mine))
        def _():
            action(
                pltpu.make_async_remote_copy(
                    src, dst, edge_send.at[side, j], tok_sem, (2 * dt + dc, ds), MESH
                )
            )

        if action is started:

            @pl.when(mine)
            def _():
                pltpu.make_async_copy(src, dst, tok_sem).start()

    def started(copy):
        copy.start()

    def left(copy):
        copy.wait_send()

    def all_tokens(action):
        def one(i, _):
            send_tokens(lax.rem(s + i, 8), action)
            return 0

        lax.fori_loop(0, 8, one, 0)

        @pl.when(s == GROUP - 1)
        def _():
            def one(j, _):
                send_edge(j, action, 0)
                return 0

            lax.fori_loop(0, 8, one, 0)

        @pl.when(s == 0)
        def _():
            def one(j, _):
                send_edge(j, action, 1)
                return 0

            lax.fori_loop(0, 8, one, 0)

    all_tokens(started)

    for load in small:
        load.wait()
    skips = pad_lanes(skip_gain[0:1, :], skip_gain[1:2, :])
    for e in range(2):
        skip_rows[e : e + 1, :] = dot(split(jnp.broadcast_to(skips, (8, 128)), 3), heads[e])[0:1, :]

    loads[0].wait()
    loads[1].wait()
    pltpu.make_async_copy(tok, tok, tok_sem).wait()

    @pl.when(jnp.logical_and(corner_lo, slab == 0))
    def _():
        tok[0:EDGE, :] = jnp.zeros((EDGE, D), BF16)

    @pl.when(jnp.logical_and(corner_hi, slab == GROUP - 1))
    def _():
        tok[EDGE + PATCH :, :] = jnp.zeros((EDGE, D), BF16)

    def convolved(offset):
        span = pl.ds(offset, CHUNK)
        wide = dot(tok[...], w_in[:, span]).astype(BF16).astype(F32)
        forward = 0.5 * conv_bias[0:1, span]
        backward = 0.5 * conv_bias[1:2, span]
        taps = 0.5 * conv_weight[:, :, span]
        for k in range(4):
            forward = forward + taps[0, k : k + 1] * pltpu.roll(wide, 3 - k, 0)[EDGE : EDGE + PATCH]
            backward = (
                backward + taps[1, k : k + 1] * pltpu.roll(wide, (PATCH + 2 * EDGE - 3 + k) % (PATCH + 2 * EDGE), 0)[EDGE : EDGE + PATCH]
            )
        forward, backward = silu_of_half(forward).astype(BF16), silu_of_half(backward).astype(BF16)
        conv_f[:, span] = forward
        conv_b[:, span] = backward
        return forward, backward

    both = convolved(INNER)
    for e in range(2):
        b_turned[e] = both[e][:, 0:STATE].astype(F32).T.astype(BF16)
    dt_raw = lax.dot_general(
        tok[EDGE : EDGE + PATCH, :],
        dt_weight[...],
        (((1,), (1,)), ((), ())),
        preferred_element_type=F32,
    )
    step = jax.nn.softplus(
        pad_lanes(dt_raw, dt_raw) + pad_lanes(dt_bias[0:1, :], dt_bias[1:2, :])
    )
    rates = pad_lanes(decay_rate[0:1, :], decay_rate[1:2, :])
    rate_step = split(step * (rates * -LOG2E), 3)
    row, col = iota((PATCH, PATCH), 0), iota((PATCH, PATCH), 1)
    down = dot((row >= col).astype(F32).astype(BF16), rate_step)
    up = dot((row <= col).astype(F32).astype(BF16), rate_step)
    down = down[:, 0:128] + (down[:, 128:256] + down[:, 256:384])
    up = up[:, 0:128] + (up[:, 128:256] + up[:, 256:384])
    lane = iota((PATCH, 128), 1)
    prefix = jnp.where(lane < HEADS, down, up)
    total = jnp.where(lane[0:1] < HEADS, down[PATCH - 1 :, :], up[0:1, :])
    log_mine[...] = jnp.broadcast_to(total, (8, 128))
    log_in[c] = log_mine[...]

    def log_copy():
        return pltpu.make_async_remote_copy(
            log_mine, log_in.at[c], log_send, log_recv, (2 * slab + 1 - c, s), MESH
        )

    log_copy().start()

    columns[...] = split(prefix, 3)
    fac[...] = split(jnp.exp2(total - prefix) * step, 2)
    ep[...] = split(jnp.exp2(prefix), 2)
    q_rows[...] = (prefix - LOG2E * jnp.log(step)).T

    def pair_copy():
        return pltpu.make_async_remote_copy(
            st.at[2], st.at[c], pair_send, pair_recv, (2 * slab + 1 - c, s), MESH
        )

    def project(i):
        t = lax.rem((1 - c) * 3 + i, 6)
        x_f, x_b = convolved(pl.multiple_of(t * CHUNK, CHUNK))
        slot = jnp.where(t // 3 == c, c, 2)
        place = pl.ds(pl.multiple_of((t % 3) * CHUNK, CHUNK), CHUNK)
        for e, x in ((0, x_f), (1, x_b)):
            factor = dot(fac[...], heads[e, 0:256, pl.ds(pl.multiple_of(t * CHUNK, CHUNK), CHUNK)])
            scaled = (x.astype(F32) * factor).astype(BF16)
            st[slot, e, :, place] = dot(b_turned[e], scaled)

    for i in range(3):
        project(i)
    pair_copy().start()
    for i in range(3, 6):
        project(i)

    log_copy().wait_recv()
    pair_logs = [log_in[0][0:1, :], log_in[1][0:1, :]]
    chip_log = pair_logs[0] + pair_logs[1]
    log_chip[...] = jnp.broadcast_to(chip_log, (8, 128))
    log_chips[s] = log_chip[...]

    def chip_log_copy(k, source):
        return pltpu.make_async_remote_copy(
            log_chip, log_chips.at[source], logc_send.at[k], logc_recv.at[source], (tm, k), MESH
        )

    def send_chip_logs(d, _):
        chip_log_copy(lax.rem(s + d, GROUP), s).start()
        return 0

    lax.fori_loop(1, GROUP, send_chip_logs, 0)
    coef[16:24, :] = dot(
        split(jnp.exp2(jnp.concatenate(pair_logs + [jnp.zeros((6, 128), F32)], axis=0)), 3),
        expand[...],
    )

    pair_copy().wait_recv()
    d0, d1 = coef[16:17, :], coef[17:18, :]

    def part_copy(k, source):
        return pltpu.make_async_remote_copy(
            part_out.at[k],
            part_in.at[source],
            part_send.at[k],
            part_recv.at[source],
            (tm, k),
            MESH,
        )

    def combined(k):
        rows = pl.ds(pl.multiple_of(k * 16, 16), 16)
        return jnp.concatenate(
            [
                d1[:, :HALF] * st[0, 0, rows, :] + st[1, 0, rows, :],
                d0[:, HALF:] * st[1, 1, rows, :] + st[0, 1, rows, :],
            ],
            axis=1,
        ).astype(BF16)

    def send_part(d, _):
        k = peer(d)
        part_out[k] = combined(k)
        part_copy(k, s).start()
        return 0

    lax.fori_loop(1, GROUP, send_part, 0)

    part_in[s] = combined(s)

    for e, conv in ((0, conv_f), (1, conv_b)):
        scores[e] = lax.dot_general(
            conv[:, INNER + STATE :],
            conv[:, INNER : INNER + STATE],
            (((1,), (1,)), ((), ())),
            preferred_element_type=F32,
        )
    lower = iota((128, 128), 0) >= iota((128, 128), 1)
    upper = iota((128, 128), 0) <= iota((128, 128), 1)
    near = [
        (iota((1, 128), 1) < 64).astype(F32).astype(BF16),
        (iota((1, 128), 1) >= 64).astype(F32).astype(BF16),
    ]

    def weigh(e, i, j, column, line, mask):
        gap = column[128 * i : 128 * i + 128, :] - line[:, 128 * j : 128 * j + 128]
        if mask is not None:
            gap = jnp.where(mask, gap, -jnp.inf)
        return (
            scores[e, 128 * i : 128 * i + 128, 128 * j : 128 * j + 128] * jnp.exp2(gap)
        ).astype(BF16)

    def within(t, _):
        span = pl.ds(pl.multiple_of(t * 128, 128), 128)
        x_f, x_b = conv_f[:, span], conv_b[:, span]
        wide = dot(
            columns[...],
            spread(3, 512, lambda l: 2 * t + ((l >> 7) & 1) + jnp.where(l < 256, 0, HEADS)),
        )
        tops, bottoms, top_x, bottom_x = [], [], [], []
        for h in range(2):
            pf, pb = wide[:, 128 * h : 128 * h + 128], wide[:, 256 + 128 * h : 384 + 128 * h]
            qf, qb = q_rows[pl.ds(2 * t + h, 1), :], q_rows[pl.ds(HEADS + 2 * t + h, 1), :]
            tops += [
                weigh(0, 0, 0, pf, qf, lower),
                weigh(1, 0, 0, pb, qb, upper),
                weigh(1, 0, 1, pb, qb, None),
            ]
            bottoms += [
                weigh(0, 1, 0, pf, qf, None),
                weigh(0, 1, 1, pf, qf, lower),
                weigh(1, 1, 1, pb, qb, upper),
            ]
            xf, xb = x_f * near[h], x_b * near[h]
            top_x += [xf[0:128], xb]
            bottom_x += [xf, xb[128:256]]
        skip = skip_rows[0:1, span] * x_f.astype(F32) + skip_rows[1:2, span] * x_b.astype(F32)
        y[0:128, span] = skip[0:128] + dot(jnp.concatenate(tops, axis=1), jnp.concatenate(top_x, axis=0))
        y[128:256, span] = skip[128:256] + dot(jnp.concatenate(bottoms, axis=1), jnp.concatenate(bottom_x, axis=0))
        return 0

    def gate_columns(t, _):
        span = pl.ds(pl.multiple_of(t * CHUNK, CHUNK), CHUNK)
        gate[:, span] = silu(dot(tok[EDGE : EDGE + PATCH, :], w_z[:, span]))
        for e in range(2):
            grow[e, :, span] = dot(ep[...], heads[e, 0:256, span])
        return 0

    loads[2].wait()
    lax.fori_loop(0, 3, gate_columns, 0)

    def wait_chip_logs(d, _):
        k = lax.rem(s + d, GROUP)
        chip_log_copy(k, k).wait_recv()
        return 0

    lax.fori_loop(1, GROUP, wait_chip_logs, 0)
    chips = [log_chips[k][0:1, :] for k in range(GROUP)]
    zero = jnp.zeros((1, 128), F32)
    before, after = [zero], [zero]
    for k in range(GROUP):
        before.append(before[-1] + chips[k])
        after.append(after[-1] + chips[GROUP - 1 - k])
    narrow = iota((1, 128), 1) < HEADS
    outside = [jnp.where(narrow, before[k], after[GROUP - 1 - k]) for k in range(GROUP)]
    log_slab[...] = jnp.broadcast_to(before[GROUP], (8, 128))
    log_slabs[slab] = log_slab[...]

    def slab_log_copy(t, source):
        return pltpu.make_async_remote_copy(
            log_slab,
            log_slabs.at[source],
            logt_send.at[t],
            logt_recv.at[source],
            (2 * t + c, s),
            MESH,
        )

    def send_slab_logs(d, _):
        slab_log_copy(lax.rem(slab + d, GROUP), slab).start()
        return 0

    lax.fori_loop(1, GROUP, send_slab_logs, 0)
    lax.fori_loop(3, 6, gate_columns, 0)
    coef[0:16, :] = dot(
        split(jnp.exp2(jnp.concatenate(chips + outside, axis=0)), 3), expand[...]
    )

    def wait_part(d, _):
        k = lax.rem(s + d, GROUP)
        part_copy(k, k).wait_recv()
        return 0

    lax.fori_loop(1, GROUP, wait_part, 0)
    forward = jnp.zeros((16, HALF), F32)
    backward = jnp.zeros((16, HALF), F32)
    for k in range(GROUP):
        r = GROUP - 1 - k
        local[k, :, :HALF] = forward
        local[r, :, HALF:] = backward
        forward = coef[k : k + 1, :HALF] * forward + part_in[k, :, :HALF].astype(F32)
        backward = coef[r : r + 1, HALF:] * backward + part_in[r, :, HALF:].astype(F32)
    slab_out[0] = forward.astype(BF16)
    slab_out[1] = backward.astype(BF16)

    def slab_copy(t, source):
        return pltpu.make_async_remote_copy(
            slab_out.at[(t < slab).astype(jnp.int32)],
            slab_in.at[source],
            slab_send.at[t],
            slab_recv.at[source],
            (2 * t + c, s),
            MESH,
        )

    def send_slab(d, _):
        slab_copy(lax.rem(slab + d, GROUP), slab).start()
        return 0

    lax.fori_loop(1, GROUP, send_slab, 0)
    slab_in[slab] = slab_out[0]

    lax.fori_loop(0, 5, within, 0)

    def wait_slab_logs(d, _):
        t = lax.rem(slab + d, GROUP)
        slab_log_copy(t, t).wait_recv()
        return 0

    lax.fori_loop(1, GROUP, wait_slab_logs, 0)
    table = jnp.concatenate([log_slabs[t][0:1, :] for t in range(GROUP)], axis=0)
    coef_t[...] = dot(split(jnp.exp2(table), 3), expand[...])

    def wait_slab(d, _):
        t = lax.rem(slab + d, GROUP)
        slab_copy(t, t).wait_recv()
        return 0

    lax.fori_loop(1, GROUP, wait_slab, 0)
    forward = jnp.zeros((16, HALF), F32)
    backward = jnp.zeros((16, HALF), F32)
    for k in range(GROUP):
        r = GROUP - 1 - k
        forward = jnp.where(
            k < slab, coef_t[k : k + 1, :HALF] * forward + slab_in[k].astype(F32), forward
        )
        backward = jnp.where(
            r > slab, coef_t[r : r + 1, HALF:] * backward + slab_in[r].astype(F32), backward
        )
    come = jnp.concatenate([forward, backward], axis=1)

    def ent_copy(k, source):
        return pltpu.make_async_remote_copy(
            ent_out.at[k], ent_in.at[source], ent_send.at[k], ent_recv.at[source], (tm, k), MESH
        )

    def entering(k):
        return (local[k] + coef[pl.ds(GROUP + k, 1), :] * come).astype(BF16)

    def send_ent(d, _):
        k = peer(d)
        ent_out[k] = entering(k)
        ent_copy(k, s).start()
        return 0

    lax.fori_loop(1, GROUP, send_ent, 0)
    ent_in[s] = entering(s)

    lax.fori_loop(5, 12, within, 0)

    def wait_ent(d, _):
        k = lax.rem(s + d, GROUP)
        ent_copy(k, k).wait_recv()
        return 0

    lax.fori_loop(1, GROUP, wait_ent, 0)
    for k in range(GROUP):
        rows = slice(16 * k, 16 * k + 16)
        first, last = ent_in[k, :, :HALF], ent_in[k, :, HALF:]
        ent[0, 0, rows, :] = first
        ent[1, 1, rows, :] = last
        ent[1, 0, rows, :] = (d0[:, :HALF] * first.astype(F32) + st[0, 0, rows, :]).astype(BF16)
        ent[0, 1, rows, :] = (d1[:, HALF:] * last.astype(F32) + st[1, 1, rows, :]).astype(BF16)
    ent_pair = pltpu.make_async_remote_copy(
        ent.at[1 - c], ent.at[2], epair_send, epair_recv, (2 * slab + 1 - c, s), MESH
    )
    ent_pair.start()

    core_home = s // 4
    slot_home = u - 8 * core_home

    def send_out(b, action):
        mine = jnp.logical_and(b == s, core_home == c)
        src, dst = mix.at[pl.ds(pl.multiple_of(32 * b, 32), 32)], out.at[slot_home]

        @pl.when(jnp.logical_not(mine))
        def _():
            action(
                pltpu.make_async_remote_copy(
                    src, dst, out_send.at[b], out_sem, (2 * slab + core_home, b), MESH
                )
            )

        if action is started:

            @pl.when(mine)
            def _():
                pltpu.make_async_copy(src, dst, out_sem).start()

    def finish(i, rows, squares):
        t = lax.rem(c * 3 + i, 6)
        span = pl.ds(pl.multiple_of(t * CHUNK, CHUNK), CHUNK)
        slot = jnp.where(t // 3 == c, c, 2)
        place = pl.ds(pl.multiple_of((t % 3) * CHUNK, CHUNK), CHUNK)
        total = y[rows, span]
        for e, conv in ((0, conv_f), (1, conv_b)):
            total = total + grow[e, rows, span] * dot(
                conv[rows, INNER + STATE :], ent[slot, e, :, place]
            )
        gated = total * gate[rows, span]
        y[rows, span] = gated
        return squares + jnp.sum(gated * gated, axis=1, keepdims=True)

    gains = norm_gain[...].reshape(1, INNER)
    for turn in range(2):
        half = far if turn == 0 else 1 - far
        rows = pl.ds(pl.multiple_of(128 * half, 128), 128)
        squares = jnp.zeros((128, 1), F32)
        for i in range(3):
            squares = finish(i, rows, squares)
        if turn == 0:
            ent_pair.wait_recv()
        for i in range(3, 6):
            squares = finish(i, rows, squares)
        scale = lax.rsqrt(squares * (1.0 / INNER) + 1e-05)
        if turn == 0:
            loads[3].wait()
        normed = (y[rows, :] * scale * gains).astype(BF16)
        mix[rows, :] = dot(normed, w_out[...]).astype(BF16)
        for i in range(4):
            send_out(4 * half + lax.rem(s + i, 4), started)

    all_tokens(left)
    pair_copy().wait_send()
    ent_pair.wait_send()

    log_copy().wait_send()

    def wait_sent_group(d, _):
        k = lax.rem(s + d, GROUP)
        part_copy(k, s).wait_send()
        ent_copy(k, s).wait_send()
        chip_log_copy(k, s).wait_send()
        t = lax.rem(slab + d, GROUP)
        slab_log_copy(t, slab).wait_send()
        slab_copy(t, slab).wait_send()
        return 0

    lax.fori_loop(1, GROUP, wait_sent_group, 0)
    for b in range(8):
        send_out(b, left)
    pltpu.make_async_copy(out, out, out_sem).wait()


def body(*args):
    args = args[:4] + (args[4].T,) + args[5:]
    hbm = pl.BlockSpec(memory_space=pl.ANY)
    dma = pltpu.SemaphoreType.DMA
    scratch = [
        pltpu.VMEM((8, 32, D), BF16),
        pltpu.VMEM((HEADS, D), BF16),
        pltpu.VMEM((2, 4, WIDE), F32),
        pltpu.VMEM((2, WIDE), F32),
        pltpu.VMEM((2, HEADS), F32),
        pltpu.VMEM((2, HEADS), F32),
        pltpu.VMEM((2, HEADS), F32),
        pltpu.VMEM((INNER,), F32),
        pltpu.VMEM((D, WIDE), BF16),
        pltpu.VMEM((D, INNER), BF16),
        pltpu.VMEM((INNER, D), BF16),
        pltpu.VMEM((PATCH + 2 * EDGE, D), BF16),
        pltpu.VMEM((PATCH, WIDE), BF16),
        pltpu.VMEM((PATCH, WIDE), BF16),
        pltpu.VMEM((2, STATE, PATCH), BF16),
        pltpu.VMEM((PATCH, INNER), F32),
        pltpu.VMEM((PATCH, INNER), F32),
        pltpu.VMEM((2, PATCH, PATCH), F32),
        pltpu.VMEM((PATCH, 384), BF16),
        pltpu.VMEM((128, PATCH), F32),
        pltpu.VMEM((PATCH, 256), BF16),
        pltpu.VMEM((PATCH, 256), BF16),
        pltpu.VMEM((8, INNER), F32),
        pltpu.VMEM((384, INNER), BF16),
        pltpu.VMEM((2, 384, INNER), BF16),
        pltpu.VMEM((2, PATCH, INNER), F32),
        pltpu.VMEM((3, 2, STATE, HALF), F32),
        pltpu.VMEM((GROUP, 16, INNER), BF16),
        pltpu.VMEM((GROUP, 16, INNER), BF16),
        pltpu.VMEM((GROUP, 16, INNER), F32),
        pltpu.VMEM((24, INNER), F32),
        pltpu.VMEM((GROUP, INNER), F32),
        pltpu.VMEM((2, 16, HALF), BF16),
        pltpu.VMEM((GROUP, 16, HALF), BF16),
        pltpu.VMEM((GROUP, 16, INNER), BF16),
        pltpu.VMEM((GROUP, 16, INNER), BF16),
        pltpu.VMEM((3, 2, STATE, HALF), BF16),
        pltpu.VMEM((8, 128), F32),
        pltpu.VMEM((2, 8, 128), F32),
        pltpu.VMEM((8, 128), F32),
        pltpu.VMEM((GROUP, 8, 128), F32),
        pltpu.VMEM((8, 128), F32),
        pltpu.VMEM((GROUP, 8, 128), F32),
        pltpu.VMEM((PATCH, D), BF16),
        dma((12,)),
        dma,
        dma((8,)),
        dma((2, 8)),
        dma,
        dma,
        dma((GROUP,)),
        dma((GROUP,)),
        dma((GROUP,)),
        dma((GROUP,)),
        dma,
        dma,
        dma((GROUP,)),
        dma((GROUP,)),
        dma((GROUP,)),
        dma((GROUP,)),
        dma((GROUP,)),
        dma((GROUP,)),
        dma,
        dma,
        dma((8,)),
        dma,
    ]
    return pl.pallas_call(
        kernel,
        out_shape=jax.ShapeDtypeStruct((8, 32, D), BF16),
        in_specs=[hbm] * 12,
        out_specs=hbm,
        scratch_shapes=scratch,
        compiler_params=pltpu.CompilerParams(
            collective_id=0, has_side_effects=True, vmem_limit_bytes=60 * 1024 * 1024
        ),
    )(*args)


def solution(mesh):
    return jax.shard_map(
        body,
        mesh=mesh,
        in_specs=(P("tm", "space", None),) + (P(),) * 11,
        out_specs=P("tm", "space", None),
        check_vma=False,
    )
```

```python
import jax
import jax.numpy as jnp
from jax import lax
from jax.experimental import pallas as pl
from jax.experimental.pallas import tpu as pltpu
from jax.sharding import PartitionSpec as P

HEADS = 24
STATE = 128
PATCH = 256
D = 768
INNER = 1536
WIDE = INNER + 2 * STATE
HALF = INNER // 2
GROUP = 8
EDGE = 16
CHUNK = 256
LOG2E = 1.4426950408889634
F32, BF16 = jnp.float32, jnp.bfloat16
MESH = pl.DeviceIdType.MESH


def iota(shape, dim):
    return lax.broadcasted_iota(jnp.int32, shape, dim)


def split(a, parts):
    pieces = []
    for _ in range(parts):
        piece = a.astype(BF16)
        pieces.append(piece)
        a = a - piece.astype(F32)
    return jnp.concatenate(pieces, axis=1)


def dot(a, b):
    return jnp.dot(a, b, preferred_element_type=F32)


def silu_of_half(half):
    return half + half * jnp.tanh(half)


def silu(a):
    return silu_of_half(0.5 * a)


def spread(parts, width, target):
    rows = iota((parts * 128, width), 0) & 127
    return (rows == target(iota((parts * 128, width), 1))).astype(F32).astype(BF16)


def pad_lanes(first, second):
    rows = first.shape[0]
    return jnp.concatenate([first, second, jnp.zeros((rows, 128 - 2 * HEADS), F32)], axis=1)


def kernel(
    tokens_hbm,
    x_weight,
    z_weight,
    bc_weight,
    dt_weight_hbm,
    conv_weight_hbm,
    conv_bias_hbm,
    dt_bias_hbm,
    decay_rate_hbm,
    skip_gain_hbm,
    norm_gain_hbm,
    out_weight,
    out,
    tokens,
    dt_weight,
    conv_weight,
    conv_bias,
    dt_bias,
    decay_rate,
    skip_gain,
    norm_gain,
    w_in,
    w_z,
    w_out,
    tok,
    conv_f,
    conv_b,
    b_turned,
    gate,
    y,
    scores,
    columns,
    q_rows,
    fac,
    ep,
    skip_rows,
    expand,
    heads,
    grow,
    st,
    part_out,
    part_in,
    local,
    coef,
    coef_t,
    slab_out,
    slab_in,
    ent_out,
    ent_in,
    ent,
    log_mine,
    log_in,
    log_chip,
    log_chips,
    log_slab,
    log_slabs,
    mix,
    w_sem,
    tok_sem,
    tok_send,
    edge_send,
    log_send,
    log_recv,
    logc_send,
    logc_recv,
    logt_send,
    logt_recv,
    pair_send,
    pair_recv,
    part_send,
    part_recv,
    slab_send,
    slab_recv,
    ent_send,
    ent_recv,
    epair_send,
    epair_recv,
    out_send,
    out_sem,
):
    tm = lax.axis_index("tm")
    s = lax.axis_index("space")
    slab = tm // 2
    c = tm % 2
    u = 2 * s + c
    far, at = 1 - s // 4, s % 4

    def peer(d):
        half = jnp.where(d <= 4, far, 1 - far)
        return 4 * half + lax.rem(at + jnp.where(d <= 4, d - 1, d - 4), 4)

    corner_hi = jnp.logical_and(s == GROUP - 1, c == 1)
    corner_lo = jnp.logical_and(s == 0, c == 0)

    fetch = pltpu.make_async_copy(tokens_hbm, tokens, w_sem.at[11])
    fetch.start()
    loads = [
        pltpu.make_async_copy(bc_weight, w_in.at[:, pl.ds(INNER, 2 * STATE)], w_sem.at[0]),
        pltpu.make_async_copy(x_weight, w_in.at[:, pl.ds(0, INNER)], w_sem.at[1]),
        pltpu.make_async_copy(z_weight, w_z, w_sem.at[2]),
        pltpu.make_async_copy(out_weight, w_out, w_sem.at[3]),
    ]
    small = [
        pltpu.make_async_copy(source, target, w_sem.at[4 + at])
        for at, (source, target) in enumerate(
            (
                (skip_gain_hbm, skip_gain),
                (dt_weight_hbm, dt_weight),
                (dt_bias_hbm, dt_bias),
                (decay_rate_hbm, decay_rate),
                (conv_weight_hbm, conv_weight),
                (conv_bias_hbm, conv_bias),
                (norm_gain_hbm, norm_gain),
            )
        )
    ]
    for load in small + loads:
        load.start()

    barrier = pltpu.get_barrier_semaphore()

    def greet(d, _):
        v = lax.rem(u + d, 16)
        pl.semaphore_signal(barrier, inc=1, device_id=(2 * slab + v % 2, v // 2), device_id_type=MESH)
        return 0

    lax.fori_loop(1, 16, greet, 0)

    def greet_slab(d, _):
        t = lax.rem(slab + d, GROUP)
        pl.semaphore_signal(barrier, inc=1, device_id=(2 * t + c, s), device_id_type=MESH)
        return 0

    lax.fori_loop(1, GROUP, greet_slab, 0)
    above = lax.rem(slab + 1, GROUP)
    below = lax.rem(slab + GROUP - 1, GROUP)

    @pl.when(corner_hi)
    def _():
        pl.semaphore_signal(barrier, inc=1, device_id=(2 * above, 0), device_id_type=MESH)

    @pl.when(corner_lo)
    def _():
        pl.semaphore_signal(
            barrier, inc=1, device_id=(2 * below + 1, GROUP - 1), device_id_type=MESH
        )

    half_target = lambda l: (l >> 6) + jnp.where(l < HALF, 12 * c, HEADS - 12 + 12 * c)
    expand[...] = spread(3, INNER, half_target)
    for e in range(2):
        heads[e] = spread(3, INNER, lambda l: HEADS * e + (l >> 6))
    fetch.wait()
    pl.semaphore_wait(barrier, 22 + jnp.logical_or(corner_hi, corner_lo).astype(jnp.int32))

    def send_tokens(j, action):
        ds, dc = 4 * c + j // 2, j % 2
        mine = jnp.logical_and(ds == s, dc == c)
        src, dst = tokens.at[j], tok.at[pl.ds(pl.multiple_of(EDGE + 32 * s, 16), 32)]

        @pl.when(jnp.logical_not(mine))
        def _():
            action(
                pltpu.make_async_remote_copy(
                    src, dst, tok_send.at[j], tok_sem, (2 * slab + dc, ds), MESH
                )
            )

        if action is started:

            @pl.when(mine)
            def _():
                pltpu.make_async_copy(src, dst, tok_sem).start()

    def send_edge(j, action, side):
        g = 8 * c + j + (1 if side == 0 else -1)
        ds, dc = lax.rem(g + 16, 16) // 2, lax.rem(g + 16, 16) % 2
        dt = lax.rem(slab + lax.div(g + 16, 16) - 1 + GROUP, GROUP)
        mine = jnp.logical_and(jnp.logical_and(ds == s, dc == c), dt == slab)
        src = tokens.at[j, pl.ds(16 if side == 0 else 0, EDGE)]
        dst = tok.at[pl.ds(0 if side == 0 else EDGE + PATCH, EDGE)]

        @pl.when(jnp.logical_not(mine))
        def _():
            action(
                pltpu.make_async_remote_copy(
                    src, dst, edge_send.at[side, j], tok_sem, (2 * dt + dc, ds), MESH
                )
            )

        if action is started:

            @pl.when(mine)
            def _():
                pltpu.make_async_copy(src, dst, tok_sem).start()

    def started(copy):
        copy.start()

    def left(copy):
        copy.wait_send()

    def all_tokens(action):
        def one(i, _):
            send_tokens(lax.rem(s + i, 8), action)
            return 0

        lax.fori_loop(0, 8, one, 0)

        @pl.when(s == GROUP - 1)
        def _():
            def one(j, _):
                send_edge(j, action, 0)
                return 0

            lax.fori_loop(0, 8, one, 0)

        @pl.when(s == 0)
        def _():
            def one(j, _):
                send_edge(j, action, 1)
                return 0

            lax.fori_loop(0, 8, one, 0)

    all_tokens(started)

    for load in small:
        load.wait()
    skips = pad_lanes(skip_gain[0:1, :], skip_gain[1:2, :])
    for e in range(2):
        skip_rows[e : e + 1, :] = dot(split(jnp.broadcast_to(skips, (8, 128)), 3), heads[e])[0:1, :]

    loads[0].wait()
    loads[1].wait()
    pltpu.make_async_copy(tok, tok, tok_sem).wait()

    @pl.when(jnp.logical_and(corner_lo, slab == 0))
    def _():
        tok[0:EDGE, :] = jnp.zeros((EDGE, D), BF16)

    @pl.when(jnp.logical_and(corner_hi, slab == GROUP - 1))
    def _():
        tok[EDGE + PATCH :, :] = jnp.zeros((EDGE, D), BF16)

    def convolved(offset):
        span = pl.ds(offset, CHUNK)
        wide = dot(tok[...], w_in[:, span]).astype(BF16).astype(F32)
        forward = 0.5 * conv_bias[0:1, span]
        backward = 0.5 * conv_bias[1:2, span]
        taps = 0.5 * conv_weight[:, :, span]
        for k in range(4):
            forward = forward + taps[0, k : k + 1] * pltpu.roll(wide, 3 - k, 0)[EDGE : EDGE + PATCH]
            backward = (
                backward + taps[1, k : k + 1] * pltpu.roll(wide, (PATCH + 2 * EDGE - 3 + k) % (PATCH + 2 * EDGE), 0)[EDGE : EDGE + PATCH]
            )
        forward, backward = silu_of_half(forward).astype(BF16), silu_of_half(backward).astype(BF16)
        conv_f[:, span] = forward
        conv_b[:, span] = backward
        return forward, backward

    both = convolved(INNER)
    for e in range(2):
        b_turned[e] = both[e][:, 0:STATE].astype(F32).T.astype(BF16)
    dt_raw = lax.dot_general(
        tok[EDGE : EDGE + PATCH, :],
        dt_weight[...],
        (((1,), (1,)), ((), ())),
        preferred_element_type=F32,
    )
    step = jax.nn.softplus(
        pad_lanes(dt_raw, dt_raw) + pad_lanes(dt_bias[0:1, :], dt_bias[1:2, :])
    )
    rates = pad_lanes(decay_rate[0:1, :], decay_rate[1:2, :])
    rate_step = split(step * (rates * -LOG2E), 3)
    row, col = iota((PATCH, PATCH), 0), iota((PATCH, PATCH), 1)
    down = dot((row >= col).astype(F32).astype(BF16), rate_step)
    up = dot((row <= col).astype(F32).astype(BF16), rate_step)
    down = down[:, 0:128] + (down[:, 128:256] + down[:, 256:384])
    up = up[:, 0:128] + (up[:, 128:256] + up[:, 256:384])
    lane = iota((PATCH, 128), 1)
    prefix = jnp.where(lane < HEADS, down, up)
    total = jnp.where(lane[0:1] < HEADS, down[PATCH - 1 :, :], up[0:1, :])
    log_mine[...] = jnp.broadcast_to(total, (8, 128))
    log_in[c] = log_mine[...]

    def log_copy():
        return pltpu.make_async_remote_copy(
            log_mine, log_in.at[c], log_send, log_recv, (2 * slab + 1 - c, s), MESH
        )

    log_copy().start()

    columns[...] = split(prefix, 3)
    fac[...] = split(jnp.exp2(total - prefix) * step, 2)
    ep[...] = split(jnp.exp2(prefix), 2)
    q_rows[...] = (prefix - LOG2E * jnp.log(step)).T

    def pair_copy():
        return pltpu.make_async_remote_copy(
            st.at[2], st.at[c], pair_send, pair_recv, (2 * slab + 1 - c, s), MESH
        )

    def project(i):
        t = lax.rem((1 - c) * 3 + i, 6)
        x_f, x_b = convolved(pl.multiple_of(t * CHUNK, CHUNK))
        slot = jnp.where(t // 3 == c, c, 2)
        place = pl.ds(pl.multiple_of((t % 3) * CHUNK, CHUNK), CHUNK)
        for e, x in ((0, x_f), (1, x_b)):
            factor = dot(fac[...], heads[e, 0:256, pl.ds(pl.multiple_of(t * CHUNK, CHUNK), CHUNK)])
            scaled = (x.astype(F32) * factor).astype(BF16)
            st[slot, e, :, place] = dot(b_turned[e], scaled)

    for i in range(3):
        project(i)
    pair_copy().start()
    for i in range(3, 6):
        project(i)

    log_copy().wait_recv()
    pair_logs = [log_in[0][0:1, :], log_in[1][0:1, :]]
    chip_log = pair_logs[0] + pair_logs[1]
    log_chip[...] = jnp.broadcast_to(chip_log, (8, 128))
    log_chips[s] = log_chip[...]

    def chip_log_copy(k, source):
        return pltpu.make_async_remote_copy(
            log_chip, log_chips.at[source], logc_send.at[k], logc_recv.at[source], (tm, k), MESH
        )

    def send_chip_logs(d, _):
        chip_log_copy(lax.rem(s + d, GROUP), s).start()
        return 0

    lax.fori_loop(1, GROUP, send_chip_logs, 0)
    coef[16:24, :] = dot(
        split(jnp.exp2(jnp.concatenate(pair_logs + [jnp.zeros((6, 128), F32)], axis=0)), 3),
        expand[...],
    )

    pair_copy().wait_recv()
    d0, d1 = coef[16:17, :], coef[17:18, :]

    def part_copy(k, source):
        return pltpu.make_async_remote_copy(
            part_out.at[k],
            part_in.at[source],
            part_send.at[k],
            part_recv.at[source],
            (tm, k),
            MESH,
        )

    def combined(k):
        rows = pl.ds(pl.multiple_of(k * 16, 16), 16)
        return jnp.concatenate(
            [
                d1[:, :HALF] * st[0, 0, rows, :] + st[1, 0, rows, :],
                d0[:, HALF:] * st[1, 1, rows, :] + st[0, 1, rows, :],
            ],
            axis=1,
        ).astype(BF16)

    def send_part(d, _):
        k = peer(d)
        part_out[k] = combined(k)
        part_copy(k, s).start()
        return 0

    lax.fori_loop(1, GROUP, send_part, 0)

    part_in[s] = combined(s)

    for e, conv in ((0, conv_f), (1, conv_b)):
        scores[e] = lax.dot_general(
            conv[:, INNER + STATE :],
            conv[:, INNER : INNER + STATE],
            (((1,), (1,)), ((), ())),
            preferred_element_type=F32,
        )
    lower = iota((128, 128), 0) >= iota((128, 128), 1)
    upper = iota((128, 128), 0) <= iota((128, 128), 1)
    near = [
        (iota((1, 128), 1) < 64).astype(F32).astype(BF16),
        (iota((1, 128), 1) >= 64).astype(F32).astype(BF16),
    ]

    def weigh(e, i, j, column, line, mask):
        gap = column[128 * i : 128 * i + 128, :] - line[:, 128 * j : 128 * j + 128]
        if mask is not None:
            gap = jnp.where(mask, gap, -jnp.inf)
        return (
            scores[e, 128 * i : 128 * i + 128, 128 * j : 128 * j + 128] * jnp.exp2(gap)
        ).astype(BF16)

    def within(t, _):
        span = pl.ds(pl.multiple_of(t * 128, 128), 128)
        x_f, x_b = conv_f[:, span], conv_b[:, span]
        wide = dot(
            columns[...],
            spread(3, 512, lambda l: 2 * t + ((l >> 7) & 1) + jnp.where(l < 256, 0, HEADS)),
        )
        tops, bottoms, top_x, bottom_x = [], [], [], []
        for h in range(2):
            pf, pb = wide[:, 128 * h : 128 * h + 128], wide[:, 256 + 128 * h : 384 + 128 * h]
            qf, qb = q_rows[pl.ds(2 * t + h, 1), :], q_rows[pl.ds(HEADS + 2 * t + h, 1), :]
            tops += [
                weigh(0, 0, 0, pf, qf, lower),
                weigh(1, 0, 0, pb, qb, upper),
                weigh(1, 0, 1, pb, qb, None),
            ]
            bottoms += [
                weigh(0, 1, 0, pf, qf, None),
                weigh(0, 1, 1, pf, qf, lower),
                weigh(1, 1, 1, pb, qb, upper),
            ]
            xf, xb = x_f * near[h], x_b * near[h]
            top_x += [xf[0:128], xb]
            bottom_x += [xf, xb[128:256]]
        skip = skip_rows[0:1, span] * x_f.astype(F32) + skip_rows[1:2, span] * x_b.astype(F32)
        y[0:128, span] = skip[0:128] + dot(jnp.concatenate(tops, axis=1), jnp.concatenate(top_x, axis=0))
        y[128:256, span] = skip[128:256] + dot(jnp.concatenate(bottoms, axis=1), jnp.concatenate(bottom_x, axis=0))
        return 0

    def gate_columns(t, _):
        span = pl.ds(pl.multiple_of(t * CHUNK, CHUNK), CHUNK)
        gate[:, span] = silu(dot(tok[EDGE : EDGE + PATCH, :], w_z[:, span]))
        for e in range(2):
            grow[e, :, span] = dot(ep[...], heads[e, 0:256, span])
        return 0

    loads[2].wait()
    lax.fori_loop(0, 3, gate_columns, 0)

    def wait_chip_logs(d, _):
        k = lax.rem(s + d, GROUP)
        chip_log_copy(k, k).wait_recv()
        return 0

    lax.fori_loop(1, GROUP, wait_chip_logs, 0)
    chips = [log_chips[k][0:1, :] for k in range(GROUP)]
    zero = jnp.zeros((1, 128), F32)
    before, after = [zero], [zero]
    for k in range(GROUP):
        before.append(before[-1] + chips[k])
        after.append(after[-1] + chips[GROUP - 1 - k])
    narrow = iota((1, 128), 1) < HEADS
    outside = [jnp.where(narrow, before[k], after[GROUP - 1 - k]) for k in range(GROUP)]
    log_slab[...] = jnp.broadcast_to(before[GROUP], (8, 128))
    log_slabs[slab] = log_slab[...]

    def slab_log_copy(t, source):
        return pltpu.make_async_remote_copy(
            log_slab,
            log_slabs.at[source],
            logt_send.at[t],
            logt_recv.at[source],
            (2 * t + c, s),
            MESH,
        )

    def send_slab_logs(d, _):
        slab_log_copy(lax.rem(slab + d, GROUP), slab).start()
        return 0

    lax.fori_loop(1, GROUP, send_slab_logs, 0)
    lax.fori_loop(3, 6, gate_columns, 0)
    coef[0:16, :] = dot(
        split(jnp.exp2(jnp.concatenate(chips + outside, axis=0)), 3), expand[...]
    )

    def wait_part(d, _):
        k = lax.rem(s + d, GROUP)
        part_copy(k, k).wait_recv()
        return 0

    lax.fori_loop(1, GROUP, wait_part, 0)
    forward = jnp.zeros((16, HALF), F32)
    backward = jnp.zeros((16, HALF), F32)
    for k in range(GROUP):
        r = GROUP - 1 - k
        local[k, :, :HALF] = forward
        local[r, :, HALF:] = backward
        forward = coef[k : k + 1, :HALF] * forward + part_in[k, :, :HALF].astype(F32)
        backward = coef[r : r + 1, HALF:] * backward + part_in[r, :, HALF:].astype(F32)
    slab_out[0] = forward.astype(BF16)
    slab_out[1] = backward.astype(BF16)

    def slab_copy(t, source):
        return pltpu.make_async_remote_copy(
            slab_out.at[(t < slab).astype(jnp.int32)],
            slab_in.at[source],
            slab_send.at[t],
            slab_recv.at[source],
            (2 * t + c, s),
            MESH,
        )

    def send_slab(d, _):
        slab_copy(lax.rem(slab + d, GROUP), slab).start()
        return 0

    lax.fori_loop(1, GROUP, send_slab, 0)
    slab_in[slab] = slab_out[0]

    lax.fori_loop(0, 5, within, 0)

    def wait_slab_logs(d, _):
        t = lax.rem(slab + d, GROUP)
        slab_log_copy(t, t).wait_recv()
        return 0

    lax.fori_loop(1, GROUP, wait_slab_logs, 0)
    table = jnp.concatenate([log_slabs[t][0:1, :] for t in range(GROUP)], axis=0)
    coef_t[...] = dot(split(jnp.exp2(table), 3), expand[...])

    def wait_slab(d, _):
        t = lax.rem(slab + d, GROUP)
        slab_copy(t, t).wait_recv()
        return 0

    lax.fori_loop(1, GROUP, wait_slab, 0)
    forward = jnp.zeros((16, HALF), F32)
    backward = jnp.zeros((16, HALF), F32)
    for k in range(GROUP):
        r = GROUP - 1 - k
        forward = jnp.where(
            k < slab, coef_t[k : k + 1, :HALF] * forward + slab_in[k].astype(F32), forward
        )
        backward = jnp.where(
            r > slab, coef_t[r : r + 1, HALF:] * backward + slab_in[r].astype(F32), backward
        )
    come = jnp.concatenate([forward, backward], axis=1)

    def ent_copy(k, source):
        return pltpu.make_async_remote_copy(
            ent_out.at[k], ent_in.at[source], ent_send.at[k], ent_recv.at[source], (tm, k), MESH
        )

    def entering(k):
        return (local[k] + coef[pl.ds(GROUP + k, 1), :] * come).astype(BF16)

    def send_ent(d, _):
        k = peer(d)
        ent_out[k] = entering(k)
        ent_copy(k, s).start()
        return 0

    lax.fori_loop(1, GROUP, send_ent, 0)
    ent_in[s] = entering(s)

    lax.fori_loop(5, 12, within, 0)

    def wait_ent(d, _):
        k = lax.rem(s + d, GROUP)
        ent_copy(k, k).wait_recv()
        return 0

    lax.fori_loop(1, GROUP, wait_ent, 0)
    for k in range(GROUP):
        rows = slice(16 * k, 16 * k + 16)
        first, last = ent_in[k, :, :HALF], ent_in[k, :, HALF:]
        ent[0, 0, rows, :] = first
        ent[1, 1, rows, :] = last
        ent[1, 0, rows, :] = (d0[:, :HALF] * first.astype(F32) + st[0, 0, rows, :]).astype(BF16)
        ent[0, 1, rows, :] = (d1[:, HALF:] * last.astype(F32) + st[1, 1, rows, :]).astype(BF16)
    ent_pair = pltpu.make_async_remote_copy(
        ent.at[1 - c], ent.at[2], epair_send, epair_recv, (2 * slab + 1 - c, s), MESH
    )
    ent_pair.start()

    core_home = s // 4
    slot_home = u - 8 * core_home

    def send_out(b, action):
        mine = jnp.logical_and(b == s, core_home == c)
        src, dst = mix.at[pl.ds(pl.multiple_of(32 * b, 32), 32)], out.at[slot_home]

        @pl.when(jnp.logical_not(mine))
        def _():
            action(
                pltpu.make_async_remote_copy(
                    src, dst, out_send.at[b], out_sem, (2 * slab + core_home, b), MESH
                )
            )

        if action is started:

            @pl.when(mine)
            def _():
                pltpu.make_async_copy(src, dst, out_sem).start()

    def finish(i, rows, squares):
        t = lax.rem(c * 3 + i, 6)
        span = pl.ds(pl.multiple_of(t * CHUNK, CHUNK), CHUNK)
        slot = jnp.where(t // 3 == c, c, 2)
        place = pl.ds(pl.multiple_of((t % 3) * CHUNK, CHUNK), CHUNK)
        total = y[rows, span]
        for e, conv in ((0, conv_f), (1, conv_b)):
            total = total + grow[e, rows, span] * dot(
                conv[rows, INNER + STATE :], ent[slot, e, :, place]
            )
        gated = total * gate[rows, span]
        y[rows, span] = gated
        return squares + jnp.sum(gated * gated, axis=1, keepdims=True)

    gains = norm_gain[...].reshape(1, INNER)
    for turn in range(2):
        half = far if turn == 0 else 1 - far
        rows = pl.ds(pl.multiple_of(128 * half, 128), 128)
        squares = jnp.zeros((128, 1), F32)
        for i in range(3):
            squares = finish(i, rows, squares)
        if turn == 0:
            ent_pair.wait_recv()
        for i in range(3, 6):
            squares = finish(i, rows, squares)
        scale = lax.rsqrt(squares * (1.0 / INNER) + 1e-05)
        if turn == 0:
            loads[3].wait()
        for q in range(2):
            piece = pl.ds(pl.multiple_of(128 * half + 64 * q, 64), 64)
            normed = (y[piece, :] * scale[64 * q : 64 * q + 64] * gains).astype(BF16)
            mix[piece, :] = dot(normed, w_out[...]).astype(BF16)
            for i in range(2):
                send_out(4 * half + 2 * q + i, started)

    all_tokens(left)
    pair_copy().wait_send()
    ent_pair.wait_send()

    log_copy().wait_send()

    def wait_sent_group(d, _):
        k = lax.rem(s + d, GROUP)
        part_copy(k, s).wait_send()
        ent_copy(k, s).wait_send()
        chip_log_copy(k, s).wait_send()
        t = lax.rem(slab + d, GROUP)
        slab_log_copy(t, slab).wait_send()
        slab_copy(t, slab).wait_send()
        return 0

    lax.fori_loop(1, GROUP, wait_sent_group, 0)
    for b in range(8):
        send_out(b, left)
    pltpu.make_async_copy(out, out, out_sem).wait()


def body(*args):
    args = args[:4] + (args[4].T,) + args[5:]
    hbm = pl.BlockSpec(memory_space=pl.ANY)
    dma = pltpu.SemaphoreType.DMA
    scratch = [
        pltpu.VMEM((8, 32, D), BF16),
        pltpu.VMEM((HEADS, D), BF16),
        pltpu.VMEM((2, 4, WIDE), F32),
        pltpu.VMEM((2, WIDE), F32),
        pltpu.VMEM((2, HEADS), F32),
        pltpu.VMEM((2, HEADS), F32),
        pltpu.VMEM((2, HEADS), F32),
        pltpu.VMEM((INNER,), F32),
        pltpu.VMEM((D, WIDE), BF16),
        pltpu.VMEM((D, INNER), BF16),
        pltpu.VMEM((INNER, D), BF16),
        pltpu.VMEM((PATCH + 2 * EDGE, D), BF16),
        pltpu.VMEM((PATCH, WIDE), BF16),
        pltpu.VMEM((PATCH, WIDE), BF16),
        pltpu.VMEM((2, STATE, PATCH), BF16),
        pltpu.VMEM((PATCH, INNER), F32),
        pltpu.VMEM((PATCH, INNER), F32),
        pltpu.VMEM((2, PATCH, PATCH), F32),
        pltpu.VMEM((PATCH, 384), BF16),
        pltpu.VMEM((128, PATCH), F32),
        pltpu.VMEM((PATCH, 256), BF16),
        pltpu.VMEM((PATCH, 256), BF16),
        pltpu.VMEM((8, INNER), F32),
        pltpu.VMEM((384, INNER), BF16),
        pltpu.VMEM((2, 384, INNER), BF16),
        pltpu.VMEM((2, PATCH, INNER), F32),
        pltpu.VMEM((3, 2, STATE, HALF), F32),
        pltpu.VMEM((GROUP, 16, INNER), BF16),
        pltpu.VMEM((GROUP, 16, INNER), BF16),
        pltpu.VMEM((GROUP, 16, INNER), F32),
        pltpu.VMEM((24, INNER), F32),
        pltpu.VMEM((GROUP, INNER), F32),
        pltpu.VMEM((2, 16, HALF), BF16),
        pltpu.VMEM((GROUP, 16, HALF), BF16),
        pltpu.VMEM((GROUP, 16, INNER), BF16),
        pltpu.VMEM((GROUP, 16, INNER), BF16),
        pltpu.VMEM((3, 2, STATE, HALF), BF16),
        pltpu.VMEM((8, 128), F32),
        pltpu.VMEM((2, 8, 128), F32),
        pltpu.VMEM((8, 128), F32),
        pltpu.VMEM((GROUP, 8, 128), F32),
        pltpu.VMEM((8, 128), F32),
        pltpu.VMEM((GROUP, 8, 128), F32),
        pltpu.VMEM((PATCH, D), BF16),
        dma((12,)),
        dma,
        dma((8,)),
        dma((2, 8)),
        dma,
        dma,
        dma((GROUP,)),
        dma((GROUP,)),
        dma((GROUP,)),
        dma((GROUP,)),
        dma,
        dma,
        dma((GROUP,)),
        dma((GROUP,)),
        dma((GROUP,)),
        dma((GROUP,)),
        dma((GROUP,)),
        dma((GROUP,)),
        dma,
        dma,
        dma((8,)),
        dma,
    ]
    return pl.pallas_call(
        kernel,
        out_shape=jax.ShapeDtypeStruct((8, 32, D), BF16),
        in_specs=[hbm] * 12,
        out_specs=hbm,
        scratch_shapes=scratch,
        compiler_params=pltpu.CompilerParams(
            collective_id=0, has_side_effects=True, vmem_limit_bytes=60 * 1024 * 1024
        ),
    )(*args)


def solution(mesh):
    return jax.shard_map(
        body,
        mesh=mesh,
        in_specs=(P("tm", "space", None),) + (P(),) * 11,
        out_specs=P("tm", "space", None),
        check_vma=False,
    )
```
